32 devices in a mesh: dp: 16 (over z, y, x), tensor: 2 (over core).
Axes of the slice: x: 2, y: 2, z: 4, core: 2. Of those that a mesh axis runs over, the one named last changes fastest.
Arguments:
- tokens: bfloat16 [32, 580, 1024], P('dp', 'tensor'), may hold values from -6 to 6
- lengths: int32 [32], P('dp'), may hold values from 290 to 580, as said below
- ln1_gain: bfloat16 [1024], P('dp'), may hold values from 0.5 to 1.5
- ln1_bias: bfloat16 [1024], P('dp'), may hold values from -3 to 3
- qkv_weight: bfloat16 [1024, 3072], P('dp', 'tensor'), may hold values from -0.1875 to 0.1875
- qv_bias: bfloat16 [16, 128], P('tensor', 'dp'), may hold values from -3 to 3
- out_weight: bfloat16 [1024, 1024], P('dp', 'tensor'), may hold values from -1.5 to 1.5
- out_bias: bfloat16 [1024], P('dp'), may hold values from -3 to 3
- ln2_gain: bfloat16 [1024], P('dp'), may hold values from 0.5 to 1.5
- ln2_bias: bfloat16 [1024], P('dp'), may hold values from -3 to 3
- fc1_weight: bfloat16 [1024, 4096], P('dp', 'tensor'), may hold values from -0.1875 to 0.1875
- fc1_bias: bfloat16 [32, 128], P('tensor', 'dp'), may hold values from -3 to 3
- fc2_weight: bfloat16 [1024, 4096], P('dp', 'tensor'), may hold values from -0.09375 to 0.09375
- fc2_bias: bfloat16 [1024], P('dp'), may hold values from -3 to 3
- cotangent: bfloat16 [32, 580, 1024], P('dp', 'tensor'), may hold values from -6 to 6
Outputs:
- result: bfloat16 [32, 580, 1024], P('dp', 'tensor')
- tokens_grad: bfloat16 [32, 580, 1024], P('dp', 'tensor')
- ln1_gain_grad: float32 [1024], P('dp')
- ln1_bias_grad: float32 [1024], P('dp')
- qkv_weight_grad: float32 [1024, 3072], P('dp', 'tensor')
- qv_bias_grad: float32 [16, 128], P('tensor', 'dp')
- out_weight_grad: float32 [1024, 1024], P('dp', 'tensor')
- out_bias_grad: float32 [1024], P('dp')
- ln2_gain_grad: float32 [1024], P('dp')
- ln2_bias_grad: float32 [1024], P('dp')
- fc1_weight_grad: float32 [1024, 4096], P('dp', 'tensor')
- fc1_bias_grad: float32 [32, 128], P('tensor', 'dp')
- fc2_weight_grad: float32 [1024, 4096], P('dp', 'tensor')
- fc2_bias_grad: float32 [1024], P('dp')
The draws below stay inside these ranges and needn't reach their ends.
Inputs may be any that keep to these rules, and one draw needn't show every extreme that they name: `lengths`: keys at positions of an image's length or beyond are masked; some image has all 580 token slots valid in every draw.
All inputs are finite; a program needn't handle non-finite values.
Results may differ from the reference program's by a relative error of at most 0.015.
Values may be sent and summed in bfloat16 or wider, within the bound.
A program may use at most 256 MiB of HBM per device.

```python
import jax
import jax.numpy as jnp
from jax import lax

D = 1024
H = 16
HD = 64
FF = 4096
SEQ = 580
IMG_DEV = 2
IMAGES = 32


def draw_lengths(key, part):
    drawn = jax.random.randint(key, (IMAGES,), SEQ // 2, SEQ + 1).astype(jnp.int32)
    return drawn.at[0].set(SEQ)


def raised(values, rng, source, target, parts, factor):
    owner, partner = [(jnp.arange(values.shape[axis_at]) // (values.shape[axis_at] // parts)).reshape([-1 if axis == axis_at else 1 for axis in range(values.ndim)]) for axis_at in (source, target)]
    chosen = jax.random.permutation(rng, parts)[partner]
    strong = (owner == chosen) | (owner == (partner + parts // 2) % parts)
    return jnp.where(strong, factor * values, values)


def levels(own_key, dims, pieces, least, largest):
    def one(axis_at, parts):
        steps = jax.random.uniform(jax.random.fold_in(jax.random.fold_in(own_key, 6), axis_at), (parts,), jnp.float32, least / len(pieces), largest / len(pieces))
        return jnp.repeat(jnp.exp(steps), dims[axis_at] // parts).reshape((-1,) + (1,) * (len(dims) - axis_at - 1))

    level = one(*pieces[0])
    for cut in pieces[1:]:
        level = level * one(*cut)
    return level


def centred(stream_key, dims, scale, limit, split=(), kind=jnp.bfloat16):
    values = jax.random.normal(stream_key, dims, jnp.float32) * scale
    if len(split) > 0:
        values = levels(stream_key, dims, split, -0.22, 0.18) * values
    return jnp.clip(values, min=-limit, max=limit).astype(kind)


def heavy_noise(own_key, shape, scale, most, cuts, heavy, held_as=jnp.bfloat16):
    array = scale * jax.random.normal(own_key, shape, jnp.float32)
    if cuts:
        array = array * levels(own_key, shape, cuts, -0.22, 0.18)
    return jnp.clip(raised(array, jax.random.fold_in(own_key, 3), *heavy), -most, most).astype(held_as)


def setup_inputs(seed: int = 0) -> dict:
    splits = jax.random.split(jax.random.key(seed), 16)
    return {
        "tokens": centred(splits[0], (IMAGES, SEQ, D), 1.0, 6.0, ((0, 16), (1, 2))),
        "lengths": draw_lengths(jax.random.fold_in(splits[15], 71), 0),
        "ln1_gain": jnp.clip(1.0 + 0.1 * jax.random.normal(splits[2], (D,), jnp.float32), 0.5, 1.5).astype(jnp.bfloat16),
        "ln1_bias": centred(splits[3], (D,), 0.5, 3.0, ((0, 16),)),
        "qkv_weight": centred(splits[4], (D, 3 * D), D ** -0.5, 0.1875, ((0, 16), (1, 2))),
        "qv_bias": centred(splits[5], (H, 2 * HD), 0.5, 3.0, ((0, 2), (1, 16))),
        "out_weight": centred(splits[6], (D, D), (D // 64) ** -0.5, 1.5, ((0, 16), (1, 2))),
        "out_bias": centred(splits[7], (D,), 0.5, 3.0, ((0, 16),)),
        "ln2_gain": jnp.clip(1.0 + 0.1 * jax.random.normal(splits[8], (D,), jnp.float32), 0.5, 1.5).astype(jnp.bfloat16),
        "ln2_bias": centred(splits[9], (D,), 0.5, 3.0, ((0, 16),)),
        "fc1_weight": centred(splits[10], (D, FF), D ** -0.5, 0.1875, ((0, 16), (1, 2))),
        "fc1_bias": centred(splits[11], (FF // 128, 128), 0.5, 3.0, ((0, 2), (1, 16))),
        "fc2_weight": centred(splits[12], (D, FF), FF ** -0.5, 0.09375, ((0, 16), (1, 2))),
        "fc2_bias": centred(splits[13], (D,), 0.5, 3.0, ((0, 16),)),
        "cotangent": heavy_noise(splits[14], (IMAGES, SEQ, D), 1.0, 6.0, ((0, 16), (1, 2)), (0, 2, 16, 2.0)),
    }


@jax.custom_vjp
def low(v):
    return lax.optimization_barrier(v.astype(jnp.bfloat16)).astype(jnp.float32)

@jax.custom_vjp
def low_back(v):
    return v

def low_keep(v):
    return (low(v), None)

def low_pass(kept, grad):
    return (grad,)

def back_keep(v):
    return (v, None)

def back_low(kept, grad):
    return (low(grad),)
low.defvjp(low_keep, low_pass)
low_back.defvjp(back_keep, back_low)

def layer_norm(values, gain, shift):
    center = values - lax.optimization_barrier(jnp.mean(values, -1, keepdims=True))
    spread = lax.optimization_barrier(jnp.mean(center * center, -1, keepdims=True))
    return center * lax.rsqrt(spread + 1e-05) * gain + shift

def matmul(left, right):
    return jnp.einsum('gsd,de->gse', left, right, precision=lax.Precision.HIGHEST)

def block_forward(params, token_rows, image_lengths):
    gain_one, shift_one, qkv_full, qv_full, out_full, out_shift, gain_two, shift_two, fc1_full, fc1_shift, fc2_full, fc2_shift = params
    groups = token_rows.shape[0]
    hidden_one = low(layer_norm(token_rows, gain_one, shift_one))
    no_key_bias = jnp.zeros((H, HD), jnp.float32)
    qkv_shift = jnp.concatenate([qv_full[:, :HD], no_key_bias, qv_full[:, HD:]], axis=1).reshape(3 * D)
    packed = low(low_back(matmul(hidden_one, qkv_full)) + qkv_shift).reshape(groups, SEQ, H, 3, HD)
    query_matrix = packed[:, :, :, 0]
    key_matrix_rows = packed[:, :, :, 1]
    value_rows = packed[:, :, :, 2]
    scores = jnp.einsum('gqhd,gkhd->ghqk', query_matrix, key_matrix_rows, precision=lax.Precision.HIGHEST) * HD ** (-0.5)
    key_mask = jnp.arange(SEQ, dtype=jnp.int32)[None, :] < image_lengths[:, None]
    scores = low_back(jnp.where(key_mask[:, None, None, :], scores, -1e+30))
    row_peak = lax.optimization_barrier(jnp.max(scores, -1, keepdims=True))
    row_exp = jnp.exp(scores - row_peak)
    attn_probs = low(row_exp / lax.optimization_barrier(jnp.sum(row_exp, -1, keepdims=True)))
    context = jnp.einsum('ghqk,gkhd->gqhd', attn_probs, value_rows, precision=lax.Precision.HIGHEST)
    context = low(low_back(context.reshape(groups, SEQ, D)))
    projected = jnp.einsum('gsi,oi->gso', context, out_full, precision=lax.Precision.HIGHEST)
    middle = token_rows + low_back(projected) + out_shift
    hidden_two = low(layer_norm(middle, gain_two, shift_two))
    pre_act = low_back(matmul(hidden_two, fc1_full)) + fc1_shift.reshape(FF)
    active = low(pre_act * jax.nn.sigmoid(1.702 * pre_act))
    mlp_out = jnp.einsum('gsf,df->gsd', active, fc2_full, precision=lax.Precision.HIGHEST)
    return middle + mlp_out + fc2_shift

def reference(tokens, lengths, ln1_gain, ln1_bias, qkv_weight, qv_bias, out_weight, out_bias, ln2_gain, ln2_bias, fc1_weight, fc1_bias, fc2_weight, fc2_bias, cotangent):
    params = tuple((weight.astype(jnp.float32) for weight in (ln1_gain, ln1_bias, qkv_weight, qv_bias, out_weight, out_bias, ln2_gain, ln2_bias, fc1_weight, fc1_bias, fc2_weight, fc2_bias)))
    groups = IMAGES // IMG_DEV
    tok_blocks = tokens.astype(jnp.float32).reshape(groups, IMG_DEV, SEQ, D)
    len_blocks = lengths.reshape(groups, IMG_DEV)
    cot_blocks = cotangent.astype(jnp.float32).reshape(groups, IMG_DEV, SEQ, D)

    def visit(totals, inputs):
        tok_block, len_block, cot_block = inputs

        def apply_block(weights, block):
            return block_forward(weights, block, len_block)
        result, pullback = jax.vjp(apply_block, params, tok_block)
        grads, tok_grad = pullback(cot_block)
        totals = jax.tree.map(lambda left, right: left + right, totals, grads)
        return (totals, (result.astype(jnp.bfloat16), tok_grad.astype(jnp.bfloat16)))
    start = jax.tree.map(jnp.zeros_like, params)
    totals, (outputs, tok_grads) = lax.scan(visit, start, (tok_blocks, len_blocks, cot_blocks))
    return (outputs.reshape(IMAGES, SEQ, D), tok_grads.reshape(IMAGES, SEQ, D), totals[0], totals[1], totals[2], totals[3], totals[4], totals[5], totals[6], totals[7], totals[8], totals[9], totals[10], totals[11])
```

```python
import functools

import jax
import jax.numpy as jnp
from jax import lax
from jax.experimental import pallas as pl
from jax.experimental.pallas import tpu as pltpu
from jax.sharding import PartitionSpec as P

HD = 64
UNIT = 256
SLAB = 128
RING = 4
BLOCKS = (4, 2, 2)
VEC_ROWS = 48
GVEC_ROWS = 40
F32 = jnp.float32
BF16 = jnp.bfloat16
MESH = pl.DeviceIdType.MESH


def mm(left, right, left_dim, right_dim):
    return lax.dot_general(
        left, right, (((left_dim,), (right_dim,)), ((), ())), preferred_element_type=F32
    )


def when(condition, action):
    if isinstance(condition, bool):
        if condition:
            action()
    else:
        pl.when(condition)(action)


def stats(values):
    center = values - jnp.mean(values, -1, keepdims=True)
    inverse = lax.rsqrt(jnp.mean(center * center, -1, keepdims=True) + 1e-05)
    return center * inverse, inverse


def stats_back(scaled, normed, inverse):
    return inverse * (
        scaled
        - jnp.mean(scaled, -1, keepdims=True)
        - normed * jnp.mean(scaled * normed, -1, keepdims=True)
    )


def three_terms(values):
    first = values.astype(BF16).astype(F32)
    second = (values - first).astype(BF16).astype(F32)
    return first, second, values - first - second


def layer_kernel(
    images,
    half,
    rows_half,
    linked,
    lengths,
    tok,
    cot_in,
    vec_in,
    wq_in,
    wo_in,
    w1_in,
    w2_in,
    result,
    tok_grad,
    gq,
    go,
    g1,
    g2,
    gvec,
    buf,
    h1,
    qkv,
    ctx,
    h2,
    act,
    gp,
    cot,
    mid,
    own,
    snd,
    rcv,
    lse,
    vec,
    acc,
    r1,
    r2,
    r3,
    vb,
    vbr,
    vs,
    vr,
    local_sem,
    cot_sem,
    gs,
    gr,
    hs,
    hr,
    xs,
    xr,
    ts,
    tr,
    vgs,
    vgr,
    vss,
    vsr,
):
    R = rows_half
    T = images * 2 * R
    D = tok.shape[-1]
    d_idx = lax.axis_index("dp")
    t_idx = lax.axis_index("tensor")
    core = {"dp": d_idx, "tensor": 1 - t_idx}
    if linked:
        x = lax.rem(d_idx, 2)
        y = lax.rem(lax.div(d_idx, 2), 2)
        z = lax.div(d_idx, 4)

        def chip(zz, yy, xx):
            return {"dp": (zz * 2 + yy) * 2 + xx, "tensor": t_idx}

        xdev = chip(z, y, 1 - x)
        ydev = chip(z, 1 - y, x)
        zdev = [chip(lax.rem(z + k, 4), y, x) for k in (1, 2, 3)]
    else:
        x = y = z = 0
        xdev = ydev = None
        zdev = []

    def remote(src, dst, send, recv, device):
        return pltpu.make_async_remote_copy(
            src_ref=src,
            dst_ref=dst,
            send_sem=send,
            recv_sem=recv,
            device_id=device,
            device_id_type=MESH,
        )

    def start(copies):
        for copy in copies:
            copy.start()

    def wait(copies):
        for copy in copies:
            copy.wait()

    barrier = pltpu.get_barrier_semaphore()
    peers = [core] + ([xdev, ydev] + zdev if linked else [])
    for peer in peers:
        pl.semaphore_signal(barrier, inc=1, device_id=peer, device_id_type=MESH)

    def unit_source(s):
        ref, u = (
            (wq_in, s)
            if s < 6
            else (wo_in, s - 6)
            if s < 8
            else (w1_in, s - 8)
            if s < 16
            else (w2_in, s - 16)
        )
        cols = pl.ds(u * UNIT, UNIT)
        return ref.at[:, cols] if linked else ref.at[:, :, :, :, cols]

    def place(s):
        return s + 16 - 16 * (s // 8)

    def place_dyn(s):
        return s + 16 - 16 * lax.div(s, 8)

    weight_copies = []
    for s in range(24):
        target = buf.at[place(s), z, y, x] if linked else buf.at[place(s)]
        weight_copies.append(pltpu.make_async_copy(unit_source(s), target, local_sem.at[s]))
    start(weight_copies)
    cot_copies = [
        pltpu.make_async_copy(cot_in.at[i], cot.at[pl.ds(i * 2 * R, R)], cot_sem.at[i])
        for i in range(images)
    ]
    start(cot_copies)
    pl.semaphore_wait(barrier, len(peers))

    def spread1(s):
        u, slot = place_dyn(s), lax.rem(s, RING)
        block = buf.at[u, z, y, x]
        return [
            remote(block, block, gs.at[slot, k], gr.at[slot, k], zdev[k]) for k in range(3)
        ]

    def spread2(s):
        u, slot = place_dyn(s), lax.rem(s, RING)
        a = buf.at[u, :, y, x, pl.ds(0, 32)]
        b = buf.at[u, :, y, x, pl.ds(32, 32)]
        return [
            remote(a, a, gs.at[slot, 3], gr.at[slot, 3], xdev),
            remote(b, b, gs.at[slot, 4], gr.at[slot, 4], ydev),
        ]

    def spread3(s):
        u, slot = place_dyn(s), lax.rem(s, RING)
        a = buf.at[u, :, y, :, pl.ds(0, 32)]
        b = buf.at[u, :, :, x, pl.ds(32, 32)]
        return [
            remote(a, a, gs.at[slot, 5], gr.at[slot, 5], ydev),
            remote(b, b, gs.at[slot, 6], gr.at[slot, 6], xdev),
        ]

    def gather_tick(s):
        if not linked:
            return
        s = jnp.int32(s)

        def begin():
            start(spread1(s))

        def second():
            wait(spread1(s - 1))
            start(spread2(s - 1))

        def third():
            wait(spread2(s - 2))
            start(spread3(s - 2))

        def end():
            wait(spread3(s - 3))

        when(s < 24, begin)
        when((s >= 1) & (s < 25), second)
        when((s >= 2) & (s < 26), third)
        when((s >= 3) & (s < 27), end)

    def grad_place(r):
        return lax.rem(r + 24, 32)

    def first(r):
        g, slot = grad_place(r), lax.rem(r, RING)
        return [
            remote(
                buf.at[g, :, 1 - y, :, pl.ds(0, 32)],
                r1.at[slot, 0],
                hs.at[slot, 0],
                hr.at[slot, 0],
                ydev,
            ),
            remote(
                buf.at[g, :, :, 1 - x, pl.ds(32, 32)],
                r1.at[slot, 1],
                hs.at[slot, 1],
                hr.at[slot, 1],
                xdev,
            ),
        ]

    def second_step(r):
        g, slot = grad_place(r), lax.rem(r, RING)
        return [
            remote(
                buf.at[g, :, y, 1 - x, pl.ds(0, 32)],
                r2.at[slot, 0],
                hs.at[slot, 2],
                hr.at[slot, 2],
                xdev,
            ),
            remote(
                buf.at[g, :, 1 - y, x, pl.ds(32, 32)],
                r2.at[slot, 1],
                hs.at[slot, 3],
                hr.at[slot, 3],
                ydev,
            ),
        ]

    def third_step(r):
        g, slot = grad_place(r), lax.rem(r, RING)
        return [
            remote(
                buf.at[g, lax.rem(z + k + 1, 4), y, x],
                r3.at[slot, k],
                hs.at[slot, 4 + k],
                hr.at[slot, 4 + k],
                zdev[k],
            )
            for k in range(3)
        ]

    def add1(r):
        g, slot = grad_place(r), lax.rem(r, RING)
        top = buf[g, :, y, :, pl.ds(0, 32)].astype(F32) + r1[slot, 0].astype(F32)
        buf[g, :, y, :, pl.ds(0, 32)] = top.astype(BF16)
        low = buf[g, :, :, x, pl.ds(32, 32)].astype(F32) + r1[slot, 1].astype(F32)
        buf[g, :, :, x, pl.ds(32, 32)] = low.astype(BF16)

    def add2(r):
        g, slot = grad_place(r), lax.rem(r, RING)
        top = buf[g, :, y, x, pl.ds(0, 32)].astype(F32) + r2[slot, 0].astype(F32)
        buf[g, :, y, x, pl.ds(0, 32)] = top.astype(BF16)
        low = buf[g, :, y, x, pl.ds(32, 32)].astype(F32) + r2[slot, 1].astype(F32)
        buf[g, :, y, x, pl.ds(32, 32)] = low.astype(BF16)

    def add3(r):
        g, slot = grad_place(r), lax.rem(r, RING)
        total = buf[g, z, y, x].astype(F32)
        for k in range(3):
            total = total + r3[slot, k].astype(F32)

        def put(ref, base):
            def store():
                ref[:, pl.ds(pl.multiple_of((r - base) * UNIT, UNIT), UNIT)] = total

            return store

        when(r < 8, put(g2, 0))
        when((r >= 8) & (r < 16), put(g1, 8))
        when((r >= 16) & (r < 18), put(go, 16))
        when(r >= 18, put(gq, 18))

    def scatter_tick(s):
        if not linked:
            return
        s = jnp.int32(s)

        def begin():
            start(first(s))

        def second():
            wait(first(s - 1))
            add1(s - 1)
            start(second_step(s - 1))

        def third():
            wait(second_step(s - 2))
            add2(s - 2)
            start(third_step(s - 2))

        def end():
            wait(third_step(s - 3))
            add3(s - 3)

        when((s >= 0) & (s < 24), begin)
        when((s >= 1) & (s < 25), second)
        when((s >= 2) & (s < 26), third)
        when((s >= 3) & (s < 27), end)

    def put_grad(r, value):
        buf[grad_place(r)] = value.astype(BF16).reshape(BLOCKS + (D // 16, UNIT))
        if not linked:

            def put(ref, base):
                def store():
                    cols = pl.ds(pl.multiple_of((r - base) * UNIT, UNIT), UNIT)
                    copy = pltpu.make_async_copy(
                        buf.at[grad_place(r)], ref.at[:, :, :, :, cols], local_sem.at[0]
                    )
                    copy.start()
                    copy.wait()

                return store

            when(r < 8, put(g2, 0))
            when((r >= 8) & (r < 16), put(g1, 8))
            when((r >= 16) & (r < 18), put(go, 16))
            when(r >= 18, put(gq, 18))

    def weight(place_idx):
        return buf[place_idx].reshape(D, UNIT)

    def pair(ref, n):
        return jnp.concatenate([ref[2 * n], ref[2 * n + 1]], axis=1)

    def put_pair(ref, n, value):
        ref[2 * n] = value[:, :SLAB]
        ref[2 * n + 1] = value[:, SLAB:]

    def token_exchange(which, ref, i):
        return remote(
            ref.at[pl.ds(i * 2 * R, R)],
            ref.at[pl.ds((i * 2 + 1) * R, R)],
            ts.at[which, i],
            tr.at[which, i],
            core,
        )

    def partial_exchange(which, side, j):
        return remote(snd.at[j], rcv.at[side, j], xs.at[which, j], xr.at[which, j], core)

    def project(which, side, slabs, places, tick=None):
        groups = len(places)

        def one(j, carry):
            left = jnp.concatenate([ref[n] for ref, n in slabs], axis=1)
            right = jnp.concatenate(
                [buf[u, j].reshape(UNIT, UNIT) for u in places], axis=1
            )
            total = mm(left, right, 1, 1)
            for i in range(images):
                own[j, pl.ds(i * R, R)] = total[i * 2 * R : (i * 2 + 1) * R]
                snd[j, pl.ds(i * R, R)] = total[(i * 2 + 1) * R : (i * 2 + 2) * R].astype(BF16)
            partial_exchange(which, side, j).start()
            if tick is not None:
                tick(j)
            return carry

        del groups
        lax.fori_loop(0, D // UNIT, one, 0)

    def partial_wait(which, side):
        for j in range(D // UNIT):
            partial_exchange(which, side, j).wait()

    def summed(side, rows):
        return jnp.concatenate(
            [own[j, rows] + rcv[side, j, rows].astype(F32) for j in range(D // UNIT)], axis=1
        )

    CHUNK = 16

    def token_loop(i, body):
        def step(c, carry):
            r = pl.multiple_of(i * R + c * CHUNK, CHUNK)
            full = pl.multiple_of(i * 2 * R + c * CHUNK, CHUNK)
            body(pl.ds(r, CHUNK), pl.ds(full, CHUNK))
            return carry

        lax.fori_loop(0, R // CHUNK, step, 0, unroll=1)

    def tokens_of(i, rows):
        return tok[rows].astype(F32)

    if linked:
        vb[0] = vec_in[...]

        def vec_copy(k, stage, device):
            return remote(vb.at[stage], vbr.at[k], vgs.at[k], vgr.at[k], device)

        vx = vec_copy(0, 0, xdev)
        vx.start()
        wait(weight_copies[:6])
        gather_tick(0)
        vx.wait()
        vb[1] = vb[0] + vbr[0]
        vy = vec_copy(1, 1, ydev)
        vy.start()
        gather_tick(1)
        vy.wait()
        vb[2] = vb[1] + vbr[1]
        vz = [vec_copy(2 + k, 2, zdev[k]) for k in range(3)]
        start(vz)
        gather_tick(2)
        wait(vz)
        vec[...] = (
            vb[2].astype(F32) + vbr[2].astype(F32) + vbr[3].astype(F32) + vbr[4].astype(F32)
        )
    else:
        wait(weight_copies[:6])
        vec[...] = vec_in[...].astype(F32)

    def vector(n):
        return jnp.concatenate([vec[4 * n + k : 4 * n + k + 1] for k in range(4)], axis=1)

    gain1, shift1, out_bias, gain2, shift2, fc2_bias = [vector(n) for n in range(6)]
    gvec[...] = jnp.zeros_like(gvec)
    acc[...] = jnp.zeros_like(acc)
    lse[...] = jnp.zeros_like(lse)

    for i in range(images):

        def norm_one(rows, full):
            normed, _ = stats(tok[rows].astype(F32))
            h1[full] = (normed * gain1 + shift1).astype(BF16)

        token_loop(i, norm_one)
        token_exchange(0, h1, i).start()
    wait(weight_copies[6:])
    wait(cot_copies)
    for i in range(images):
        token_exchange(1, cot, i).start()
    for s in (3, 4, 5):
        gather_tick(s)
    for i in range(images):
        token_exchange(0, h1, i).wait()
        token_exchange(1, cot, i).wait()

    lane = lax.broadcasted_iota(jnp.int32, (2 * R, SLAB), 1)
    row = lax.broadcasted_iota(jnp.int32, (2 * R, SLAB), 0)
    second_half = row >= R
    inside = jnp.where(second_half, row - R, row)
    position = inside + jnp.where(second_half, (1 - t_idx) * half, t_idx * half)
    low_lanes = lane[:R] < HD

    def head_lanes(e, lanes):
        return lanes < HD if e == 0 else lanes >= HD

    def extra(e):
        return HD * (1 - e)

    def key_bias(i):
        valid = (inside < half) & (position < lengths[i])
        return jnp.where(valid, 0.0, -1e30)

    def project_heads(c):
        def one(j, carry):
            u = 3 * c + j
            value = mm(h1[...], weight(16 + u), 1, 0) + vec[pl.ds(24 + u, 1)]
            put_pair(qkv, u, value.astype(BF16))
            return carry

        lax.fori_loop(0, 3, one, 0)

    def attend(i, c, p):
        rows = pl.ds(pl.multiple_of(i * 2 * R, 16), 2 * R)
        q = qkv[c * 6 + p, rows].astype(F32) * HD**-0.5
        k = qkv[c * 6 + 2 + p, rows].astype(F32)
        v = qkv[c * 6 + 4 + p, rows]
        bias = key_bias(i)
        heads = []
        for e in range(2):
            inhead = head_lanes(e, lane)
            first_extra = lane == extra(e)
            qm = jnp.where(inhead, q, jnp.where(first_extra, 1.0, 0.0)).astype(BF16)
            km = jnp.where(inhead, k, jnp.where(first_extra, bias, 0.0)).astype(BF16)
            heads.append((qm, km))
        for m in range(2):
            outs, sums = [], []
            for e in range(2):
                qm, km = heads[e]
                scores = mm(qm[m * R : (m + 1) * R], km, 1, 1)
                peak = jnp.max(scores, -1, keepdims=True)
                exps = jnp.exp(scores - peak)
                total = jnp.sum(exps, -1, keepdims=True)
                outs.append(mm(exps.astype(BF16), v, 1, 0) * (1.0 / total))
                sums.append(peak + jnp.log(total))
            tile = pl.ds(pl.multiple_of(i * 2 * R + m * R, 16), R)
            ctx[2 * c + p, tile] = jnp.where(low_lanes, outs[0], outs[1]).astype(BF16)
            column = lane[:R]
            head = (2 * c + p) * 2
            lse[tile] = jnp.where(
                column == head, sums[0], jnp.where(column == head + 1, sums[1], lse[tile])
            )

    for c in range(2):
        project_heads(c)

        def attend_step(n, carry):
            gather_tick(6 + 4 * c + n)
            attend(lax.div(n, 2), c, lax.rem(n, 2))
            return carry

        lax.fori_loop(0, images * 2, attend_step, 0)

    project(0, 0, [(ctx, n) for n in range(4)], [22, 23])
    gather_tick(14)
    partial_wait(0, 0)
    for i in range(images):

        def norm_two(rows, full):
            middle = tok[rows].astype(F32) + summed(0, rows) + out_bias
            mid[rows] = middle
            normed, _ = stats(middle)
            h2[full] = (normed * gain2 + shift2).astype(BF16)

        token_loop(i, norm_two)
        token_exchange(2, h2, i).start()
        if i == 0:
            gather_tick(15)
    for i in range(images):
        token_exchange(2, h2, i).wait()

    def hidden(u, carry):
        if linked:
            pl.when(lax.rem(u, 2) == 0)(lambda: gather_tick(16 + lax.div(u, 2)))
        pre = mm(h2[...], weight(8 + u), 1, 0) + vec[pl.ds(30 + u, 1)]
        sig = 0.5 * jnp.tanh(0.851 * pre) + 0.5
        active = pre * sig
        slope = sig + 1.702 * active * (1.0 - sig)
        put_pair(act, u, active.astype(BF16))
        put_pair(gp, u, slope.astype(BF16))
        return carry

    lax.fori_loop(0, 8, hidden, 0)

    def hidden_back(u, carry):
        put_grad(u, mm(cot[...], pair(act, u), 0, 0))
        gather_tick(20 + u)
        pre_grad = mm(cot[...], weight(u), 1, 0) * pair(gp, u).astype(F32)
        gvec[pl.ds(28 + u, 1)] = jnp.sum(pre_grad, 0, keepdims=True)
        put_pair(gp, u, pre_grad.astype(BF16))
        scatter_tick(u - 2)
        return carry

    lax.fori_loop(0, 8, hidden_back, 0)

    def odd_tick(base):
        if not linked:
            return None

        def tick(j):
            pl.when(lax.rem(j, 2) == 1)(lambda: scatter_tick(base + lax.div(j, 2)))

        return tick

    project(1, 1, [(act, n) for n in range(16)], list(range(8)), odd_tick(6))

    def first_grad(u, carry):
        put_grad(8 + u, mm(h2[...], pair(gp, u), 0, 0))
        if linked:
            pl.when(lax.rem(u, 3) == 2)(lambda: scatter_tick(8 + lax.div(u, 3)))
        return carry

    lax.fori_loop(0, 8, first_grad, 0)
    scatter_tick(10)
    partial_wait(1, 1)
    for i in range(images):

        def finish(rows, full):
            total = mid[rows] + summed(1, rows) + fc2_bias
            result[rows] = total.astype(BF16)

        token_loop(i, finish)
    project(2, 0, [(gp, n) for n in range(16)], list(range(8, 16)), odd_tick(11))
    partial_wait(2, 0)

    def add_rows(n, value):
        acc[n] += value[:8] + value[8:]

    for i in range(images):

        def norm_two_back(rows, full):
            grad = summed(0, rows)
            normed, inverse = stats(mid[rows])
            cots = cot[full].astype(F32)
            middle_grad = cots + stats_back(grad * gain2, normed, inverse)
            add_rows(2, middle_grad)
            add_rows(3, grad * normed)
            add_rows(4, grad)
            add_rows(5, cots)
            mid[rows] = middle_grad
            cot[full] = middle_grad.astype(BF16)

        token_loop(i, norm_two_back)
        token_exchange(3, cot, i).start()
        if i == 0:
            scatter_tick(13)
    for i in range(images):
        token_exchange(3, cot, i).wait()

    def out_back(u, carry):
        put_grad(16 + u, mm(cot[...], pair(ctx, u), 0, 0))
        value = mm(cot[...], weight(22 + u), 1, 0)
        put_pair(act, 6 + u, value.astype(BF16))
        return carry

    lax.fori_loop(0, 2, out_back, 0)
    scatter_tick(14)

    def attend_back(i, c, p):
        rows = pl.ds(pl.multiple_of(i * 2 * R, 16), 2 * R)
        q = qkv[c * 6 + p, rows].astype(F32) * HD**-0.5
        k = qkv[c * 6 + 2 + p, rows]
        v = qkv[c * 6 + 4 + p, rows]
        up = act[12 + 2 * c + p, rows]
        inner_all = up.astype(F32) * ctx[2 * c + p, rows].astype(F32)
        sums_all = lse[rows]
        bias = key_bias(i)
        q_low = q.astype(BF16)
        q_grads, k_grads, v_grads = [], [], []
        for e in range(2):
            inhead = head_lanes(e, lane)
            at = [lane == extra(e) + n for n in range(4)]
            head = (2 * c + p) * 2 + e
            total = jnp.sum(jnp.where(lane == head, sums_all, 0.0), -1, keepdims=True)
            inner = jnp.sum(jnp.where(inhead, inner_all, 0.0), -1, keepdims=True)
            s1, s2, s3 = three_terms(-total)
            n1, n2, n3 = three_terms(-inner)
            ones = at[1] | at[2] | at[3]
            qa = jnp.where(
                inhead,
                q,
                jnp.where(
                    at[0],
                    1.0,
                    jnp.where(at[1], s1, jnp.where(at[2], s2, jnp.where(at[3], s3, 0.0))),
                ),
            ).astype(BF16)
            ka = jnp.where(
                inhead, k.astype(F32), jnp.where(at[0], bias, jnp.where(ones, 1.0, 0.0))
            ).astype(BF16)
            ua = jnp.where(
                inhead,
                up.astype(F32),
                jnp.where(at[1], n1, jnp.where(at[2], n2, jnp.where(at[3], n3, 0.0))),
            ).astype(BF16)
            va = jnp.where(inhead, v.astype(F32), jnp.where(ones, 1.0, 0.0)).astype(BF16)
            q_grad = None
            k_parts, v_parts = [], []
            for m in range(2):
                tile = slice(m * R, (m + 1) * R)
                probs = jnp.exp(mm(ka[tile], qa, 1, 1))
                grads = (probs * mm(va[tile], ua, 1, 1)).astype(BF16)
                v_parts.append(mm(probs.astype(BF16), up, 1, 0))
                k_parts.append(mm(grads, q_low, 1, 0))
                part = mm(grads, k[tile], 0, 0)
                q_grad = part if q_grad is None else q_grad + part
            q_grads.append(q_grad * HD**-0.5)
            k_grads.append(k_parts)
            v_grads.append(v_parts)
        low = lane < HD
        q_sum = jnp.where(low, q_grads[0], q_grads[1])
        act[c * 6 + p, rows] = q_sum.astype(BF16)
        v_bias = None
        for m in range(2):
            tile = pl.ds(pl.multiple_of(i * 2 * R + m * R, 16), R)
            k_sum = jnp.where(low_lanes, k_grads[0][m], k_grads[1][m])
            v_sum = jnp.where(low_lanes, v_grads[0][m], v_grads[1][m])
            act[c * 6 + 2 + p, tile] = k_sum.astype(BF16)
            act[c * 6 + 4 + p, tile] = v_sum.astype(BF16)
            part = jnp.sum(v_sum, 0, keepdims=True)
            v_bias = part if v_bias is None else v_bias + part
        bias_row = jnp.concatenate([jnp.sum(q_sum, 0, keepdims=True), v_bias], axis=1)
        gvec[pl.ds(24 + 2 * c + p, 1)] += bias_row

    for c in range(2):

        def attend_back_step(n, carry):
            if linked:
                pl.when(n < 3)(lambda: scatter_tick(15 + 3 * c + n))
            attend_back(lax.div(n, 2), c, lax.rem(n, 2))
            return carry

        lax.fori_loop(0, images * 2, attend_back_step, 0)

        def heads_grad(j, carry):
            u = 3 * c + j
            put_grad(18 + u, mm(h1[...], pair(act, u), 0, 0))
            return carry

        lax.fori_loop(0, 3, heads_grad, 0)
    scatter_tick(21)
    project(3, 1, [(act, n) for n in range(12)], list(range(16, 22)), odd_tick(22))
    partial_wait(3, 1)
    for i in range(images):

        def norm_one_back(rows, full):
            grad = summed(1, rows)
            normed, inverse = stats(tok[rows].astype(F32))
            add_rows(0, grad * normed)
            add_rows(1, grad)
            total = mid[rows] + stats_back(grad * gain1, normed, inverse)
            tok_grad[rows] = total.astype(BF16)

        token_loop(i, norm_one_back)
        if i == 0:
            scatter_tick(24)

    for n in range(6):
        total = jnp.sum(acc[n], 0, keepdims=True)
        for k in range(4):
            gvec[4 * n + k : 4 * n + k + 1] = total[:, k * UNIT : (k + 1) * UNIT]

    def sum_copy(k, stage, device):
        return remote(vs.at[stage], vr.at[k], vss.at[k], vsr.at[k], device)

    vs[0] = gvec[...]
    over_core = sum_copy(0, 0, core)
    over_core.start()
    scatter_tick(25)
    over_core.wait()
    shared = lax.broadcasted_iota(jnp.int32, (GVEC_ROWS, UNIT), 0) < 24
    gathered = vs[0] + jnp.where(shared, vr[0], 0.0)
    if linked:
        vs[1] = gathered
        over_x = sum_copy(1, 1, xdev)
        over_x.start()
        scatter_tick(26)
        over_x.wait()
        vs[2] = vs[1] + vr[1]
        over_y = sum_copy(2, 2, ydev)
        over_y.start()
        over_y.wait()
        vs[3] = vs[2] + vr[2]
        over_z = [sum_copy(3 + k, 3, zdev[k]) for k in range(3)]
        start(over_z)
        wait(over_z)
        gvec[...] = vs[3] + vr[3] + vr[4] + vr[5]
    else:
        gvec[...] = gathered


def own_part(values, index, width):
    return lax.dynamic_slice_in_dim(values, index * width, width, axis=1)


def body(
    linked,
    tokens,
    lengths,
    ln1_gain,
    ln1_bias,
    qkv_weight,
    qv_bias,
    out_weight,
    out_bias,
    ln2_gain,
    ln2_bias,
    fc1_weight,
    fc1_bias,
    fc2_weight,
    fc2_bias,
    cotangent,
):
    images, half, D = tokens.shape
    parts = lax.axis_size("dp")
    dp = lax.axis_index("dp")
    heads = qv_bias.shape[0]
    R = -(-half // 16) * 16
    T = images * 2 * R
    share = D // parts
    pad = ((0, 0), (0, R - half), (0, 0))
    tok = jnp.pad(tokens, pad).reshape(images * R, D)
    cot = jnp.pad(cotangent, pad)

    def placed(values, width):
        if linked:
            wide = jnp.tile(values, (1, parts))
            at = lax.broadcasted_iota(jnp.int32, wide.shape, 1) // width == dp
            return jnp.where(at, wide, jnp.zeros_like(wide))
        return lax.all_gather(values, "dp", axis=1, tiled=True)

    norms = placed(
        jnp.stack([ln1_gain, ln1_bias, out_bias, ln2_gain, ln2_bias, fc2_bias]), share
    ).reshape(24, UNIT)
    qv = placed(qv_bias, 2 * HD // parts if linked else 1).reshape(2, 2, 2, 2, HD)
    q_rows = qv[:, :, :, 0].reshape(2, 1, UNIT)
    v_rows = qv[:, :, :, 1].reshape(2, 1, UNIT)
    qkv_rows = jnp.concatenate([q_rows, jnp.zeros_like(q_rows), v_rows], axis=1).reshape(6, UNIT)
    fc1_rows = placed(fc1_bias, 128 // parts if linked else 1).reshape(8, UNIT)
    vec = jnp.concatenate(
        [norms, qkv_rows, fc1_rows, jnp.zeros((VEC_ROWS - 38, UNIT), BF16)], axis=0
    )

    grouped = qkv_weight.reshape(share, heads // 4, 4, 3, HD)
    wq = jnp.swapaxes(grouped, 2, 3).reshape(share, heads * 3 * HD)
    weights = [wq, out_weight, fc1_weight, fc2_weight]
    if not linked:
        weights = [
            lax.all_gather(w, "dp", axis=0, tiled=True).reshape(
                BLOCKS + (D // 16, w.shape[1])
            )
            for w in weights
        ]
    vmem = pl.BlockSpec(memory_space=pltpu.VMEM)
    hbm = pl.BlockSpec(memory_space=pl.ANY)
    if linked:
        grads = [jax.ShapeDtypeStruct(w.shape, F32) for w in weights]
    else:
        grads = [jax.ShapeDtypeStruct(w.shape, BF16) for w in weights]
    grad_spec = vmem if linked else hbm
    dma = pltpu.SemaphoreType.DMA
    block = BLOCKS + (D // 16, UNIT)
    outs = pl.pallas_call(
        functools.partial(layer_kernel, images, half, R, linked),
        out_shape=[
            jax.ShapeDtypeStruct((images * R, D), BF16),
            jax.ShapeDtypeStruct((images * R, D), BF16),
            *grads,
            jax.ShapeDtypeStruct((GVEC_ROWS, UNIT), F32),
        ],
        in_specs=[pl.BlockSpec(memory_space=pltpu.SMEM), vmem, hbm, vmem, hbm, hbm, hbm, hbm],
        out_specs=[vmem, vmem, grad_spec, grad_spec, grad_spec, grad_spec, vmem],
        scratch_shapes=[
            pltpu.VMEM((32,) + block, BF16),
            pltpu.VMEM((T, D), BF16),
            pltpu.VMEM((12, T, SLAB), BF16),
            pltpu.VMEM((4, T, SLAB), BF16),
            pltpu.VMEM((T, D), BF16),
            pltpu.VMEM((16, T, SLAB), BF16),
            pltpu.VMEM((16, T, SLAB), BF16),
            pltpu.VMEM((T, D), BF16),
            pltpu.VMEM((images * R, D), F32),
            pltpu.VMEM((4, images * R, UNIT), F32),
            pltpu.VMEM((4, images * R, UNIT), BF16),
            pltpu.VMEM((2, 4, images * R, UNIT), BF16),
            pltpu.VMEM((T, SLAB), F32),
            pltpu.VMEM((VEC_ROWS, UNIT), F32),
            pltpu.VMEM((6, 8, D), F32),
            pltpu.VMEM((RING, 2, 4, 2, 32, UNIT), BF16),
            pltpu.VMEM((RING, 2, 4, 32, UNIT), BF16),
            pltpu.VMEM((RING, 3, 64, UNIT), BF16),
            pltpu.VMEM((3, VEC_ROWS, UNIT), BF16),
            pltpu.VMEM((5, VEC_ROWS, UNIT), BF16),
            pltpu.VMEM((4, GVEC_ROWS, UNIT), F32),
            pltpu.VMEM((6, GVEC_ROWS, UNIT), F32),
            dma((24,)),
            dma((images,)),
            dma((RING, 7)),
            dma((RING, 7)),
            dma((RING, 7)),
            dma((RING, 7)),
            dma((4, 4)),
            dma((4, 4)),
            dma((4, images)),
            dma((4, images)),
            dma((5,)),
            dma((5,)),
            dma((6,)),
            dma((6,)),
        ],
        compiler_params=pltpu.CompilerParams(
            collective_id=0, has_side_effects=True, vmem_limit_bytes=64 * 2**20 - 2**16
        ),
        name="layer",
    )(lengths, tok, cot, vec, *weights)
    result, tok_grad, gq, go, g1, g2, gvec = outs

    def unpadded(values):
        return values.reshape(images, R, D)[:, :half]

    def owned(values):
        if linked:
            return values
        flat = values.reshape(D, values.shape[-1]).astype(F32)
        return lax.psum_scatter(flat, "dp", scatter_dimension=0, tiled=True)

    gq, go, g1, g2 = owned(gq), owned(go), owned(g1), owned(g2)
    gq = jnp.swapaxes(gq.reshape(share, heads // 4, 3, 4, HD), 2, 3).reshape(share, heads * 3 * HD)
    if not linked:
        gvec = lax.psum(gvec, "dp")
    norms_grad = own_part(gvec[:24].reshape(6, D), dp, share)
    qv_grad = jnp.swapaxes(gvec[24:28].reshape(4, 2, 2, HD), 1, 2).reshape(heads, 2 * HD)
    qv_grad = own_part(qv_grad, dp, 2 * HD // parts)
    fc1_grad = own_part(gvec[28:36].reshape(-1, 128), dp, 128 // parts)
    return (
        unpadded(result),
        unpadded(tok_grad),
        norms_grad[0],
        norms_grad[1],
        gq,
        qv_grad,
        go,
        norms_grad[2],
        norms_grad[3],
        norms_grad[4],
        g1,
        fc1_grad,
        g2,
        norms_grad[5],
    )


def solution(mesh):
    linked = mesh.shape["dp"] == 16
    vector = P("dp")
    weight = P("dp", "tensor")
    bias = P("tensor", "dp")
    tokens = P("dp", "tensor", None)
    in_specs = (
        tokens,
        vector,
        vector,
        vector,
        weight,
        bias,
        weight,
        vector,
        vector,
        vector,
        weight,
        bias,
        weight,
        vector,
        tokens,
    )
    out_specs = (
        tokens,
        tokens,
        vector,
        vector,
        weight,
        bias,
        weight,
        vector,
        vector,
        vector,
        weight,
        bias,
        weight,
        vector,
    )
    return jax.shard_map(
        functools.partial(body, linked),
        mesh=mesh,
        in_specs=in_specs,
        out_specs=out_specs,
        check_vma=False,
    )
```

```python
import functools

import jax
import jax.numpy as jnp
from jax import lax
from jax.experimental import pallas as pl
from jax.experimental.pallas import tpu as pltpu
from jax.sharding import PartitionSpec as P

HD = 64
UNIT = 256
SLAB = 128
LAG = 2
RING = 2 * LAG + 2
STEPS = 24 + 4 * LAG
BLOCKS = (2, 2, 2, 2)
VEC_ROWS = 48
GVEC_ROWS = 40
F32 = jnp.float32
BF16 = jnp.bfloat16
MESH = pl.DeviceIdType.MESH


def mm(left, right, left_dim, right_dim):
    return lax.dot_general(
        left, right, (((left_dim,), (right_dim,)), ((), ())), preferred_element_type=F32
    )


def when(condition, action):
    if isinstance(condition, bool):
        if condition:
            action()
    else:
        pl.when(condition)(action)


def stats(values):
    center = values - jnp.mean(values, -1, keepdims=True)
    inverse = lax.rsqrt(jnp.mean(center * center, -1, keepdims=True) + 1e-05)
    return center * inverse, inverse


def stats_back(scaled, normed, inverse):
    return inverse * (
        scaled
        - jnp.mean(scaled, -1, keepdims=True)
        - normed * jnp.mean(scaled * normed, -1, keepdims=True)
    )


def three_terms(values):
    first = values.astype(BF16).astype(F32)
    second = (values - first).astype(BF16).astype(F32)
    return first, second, values - first - second


def layer_kernel(
    images,
    half,
    rows_half,
    linked,
    lengths,
    tok,
    cot_in,
    vec_in,
    wq_in,
    wo_in,
    w1_in,
    w2_in,
    result,
    tok_grad,
    gq,
    go,
    g1,
    g2,
    gvec,
    buf,
    h1,
    qkv,
    ctx,
    h2,
    act,
    gp,
    cot,
    mid,
    own,
    snd,
    rcv,
    lse,
    vec,
    acc,
    r1,
    r2,
    r3,
    r4,
    vb,
    vbr,
    vs,
    vr,
    local_sem,
    cot_sem,
    gs,
    gr,
    hs,
    hr,
    xs,
    xr,
    ts,
    tr,
    vgs,
    vgr,
    vss,
    vsr,
):
    R = rows_half
    T = images * 2 * R
    D = tok.shape[-1]
    d_idx = lax.axis_index("dp")
    t_idx = lax.axis_index("tensor")
    core = {"dp": d_idx, "tensor": 1 - t_idx}
    if linked:
        x = lax.rem(d_idx, 2)
        y = lax.rem(lax.div(d_idx, 2), 2)
        b = lax.rem(lax.div(d_idx, 4), 2)
        a = lax.div(d_idx, 8)

        def chip(aa, bb, yy, xx):
            return {"dp": ((aa * 2 + bb) * 2 + yy) * 2 + xx, "tensor": t_idx}

        xdev = chip(a, b, y, 1 - x)
        ydev = chip(a, b, 1 - y, x)
        bdev = chip(a, 1 - b, y, x)
        adev = chip(1 - a, b, y, x)
    else:
        a = b = y = x = 0
        xdev = ydev = bdev = adev = None

    def remote(src, dst, send, recv, device):
        return pltpu.make_async_remote_copy(
            src_ref=src,
            dst_ref=dst,
            send_sem=send,
            recv_sem=recv,
            device_id=device,
            device_id_type=MESH,
        )

    def start(copies):
        for copy in copies:
            copy.start()

    def wait(copies):
        for copy in copies:
            copy.wait()

    barrier = pltpu.get_barrier_semaphore()
    peers = [core] + ([xdev, ydev, bdev, adev] if linked else [])
    for peer in peers:
        pl.semaphore_signal(barrier, inc=1, device_id=peer, device_id_type=MESH)

    def unit_source(s):
        ref, u = (
            (wq_in, s)
            if s < 6
            else (wo_in, s - 6)
            if s < 8
            else (w1_in, s - 8)
            if s < 16
            else (w2_in, s - 16)
        )
        cols = pl.ds(u * UNIT, UNIT)
        return ref.at[:, cols] if linked else ref.at[:, :, :, :, :, cols]

    def place(s):
        return s + 16 - 16 * (s // 8)

    def place_dyn(s):
        return s + 16 - 16 * lax.div(s, 8)

    weight_copies = []
    for s in range(24):
        target = buf.at[place(s), a, b, y, x] if linked else buf.at[place(s)]
        weight_copies.append(pltpu.make_async_copy(unit_source(s), target, local_sem.at[s]))
    start(weight_copies)
    cot_copies = [
        pltpu.make_async_copy(cot_in.at[i], cot.at[pl.ds(i * 2 * R, R)], cot_sem.at[i])
        for i in range(images)
    ]
    start(cot_copies)
    pl.semaphore_wait(barrier, len(peers))

    TOP, LOW = pl.ds(0, 32), pl.ds(32, 32)

    def spread(k, s):
        u, slot = place_dyn(s), lax.rem(s, RING)
        if k == 0:
            moves = [(buf.at[u, a, b, y, x], adev)]
        elif k == 1:
            moves = [(buf.at[u, :, b, y, x, TOP], xdev), (buf.at[u, :, b, y, x, LOW], ydev)]
        elif k == 2:
            moves = [(buf.at[u, :, b, y, :, TOP], bdev), (buf.at[u, :, b, :, x, LOW], bdev)]
        else:
            moves = [(buf.at[u, :, :, y, :, TOP], ydev), (buf.at[u, :, :, :, x, LOW], xdev)]
        return [
            remote(ref, ref, gs.at[slot, 2 * k + n], gr.at[slot, 2 * k + n], device)
            for n, (ref, device) in enumerate(moves)
        ]

    def gather_tick(s):
        if not linked:
            return
        s = jnp.int32(s)
        when(s < 24, lambda: start(spread(0, s)))
        for k in range(4):
            unit = s - (k + 1) * LAG

            def further(k=k, unit=unit):
                wait(spread(k, unit))
                if k < 3:
                    start(spread(k + 1, unit))

            when((unit >= 0) & (unit < 24), further)

    def gather_ticks(low, high):
        if not linked or low >= high:
            return

        def one(s, carry):
            gather_tick(s)
            return carry

        lax.fori_loop(low, high, one, 0)

    def grad_place(r):
        return lax.rem(r + 24, 32)

    def collect(k, r):
        g, slot = grad_place(r), lax.rem(r, RING)
        if k == 0:
            moves = [
                (buf.at[g, :, :, 1 - y, :, TOP], r1.at[slot, 0], ydev),
                (buf.at[g, :, :, :, 1 - x, LOW], r1.at[slot, 1], xdev),
            ]
        elif k == 1:
            moves = [
                (buf.at[g, :, 1 - b, y, :, TOP], r2.at[slot, 0], bdev),
                (buf.at[g, :, 1 - b, :, x, LOW], r2.at[slot, 1], bdev),
            ]
        elif k == 2:
            moves = [
                (buf.at[g, :, b, y, 1 - x, TOP], r3.at[slot, 0], xdev),
                (buf.at[g, :, b, 1 - y, x, LOW], r3.at[slot, 1], ydev),
            ]
        else:
            moves = [(buf.at[g, 1 - a, b, y, x], r4.at[slot], adev)]
        return [
            remote(src, dst, hs.at[slot, 2 * k + n], hr.at[slot, 2 * k + n], device)
            for n, (src, dst, device) in enumerate(moves)
        ]

    def add_parts(k, r):
        g, slot = grad_place(r), lax.rem(r, RING)
        if k == 0:
            top, low, parts = (g, slice(None), slice(None), y, slice(None), TOP), (
                (g, slice(None), slice(None), slice(None), x, LOW)
            ), r1
        elif k == 1:
            top, low, parts = (g, slice(None), b, y, slice(None), TOP), (
                (g, slice(None), b, slice(None), x, LOW)
            ), r2
        else:
            top, low, parts = (g, slice(None), b, y, x, TOP), (g, slice(None), b, y, x, LOW), r3
        buf[top] = (buf[top].astype(F32) + parts[slot, 0].astype(F32)).astype(BF16)
        buf[low] = (buf[low].astype(F32) + parts[slot, 1].astype(F32)).astype(BF16)

    def add_last(r):
        g, slot = grad_place(r), lax.rem(r, RING)
        total = buf[g, a, b, y, x].astype(F32) + r4[slot].astype(F32)

        def put(ref, base):
            def store():
                ref[:, pl.ds(pl.multiple_of((r - base) * UNIT, UNIT), UNIT)] = total

            return store

        when(r < 8, put(g2, 0))
        when((r >= 8) & (r < 16), put(g1, 8))
        when((r >= 16) & (r < 18), put(go, 16))
        when(r >= 18, put(gq, 18))

    def scatter_tick(s):
        if not linked:
            return
        s = jnp.int32(s)
        when((s >= 0) & (s < 24), lambda: start(collect(0, s)))
        for k in range(4):
            unit = s - (k + 1) * LAG

            def further(k=k, unit=unit):
                wait(collect(k, unit))
                if k < 3:
                    add_parts(k, unit)
                    start(collect(k + 1, unit))
                else:
                    add_last(unit)

            when((unit >= 0) & (unit < 24), further)

    def scatter_ticks(low, high):
        if not linked or low >= high:
            return

        def one(s, carry):
            scatter_tick(s)
            return carry

        lax.fori_loop(low, high, one, 0)

    def put_grad(r, value):
        buf[grad_place(r)] = value.astype(BF16).reshape(BLOCKS + (D // 16, UNIT))
        if not linked:

            def put(ref, base):
                def store():
                    cols = pl.ds(pl.multiple_of((r - base) * UNIT, UNIT), UNIT)
                    copy = pltpu.make_async_copy(
                        buf.at[grad_place(r)], ref.at[:, :, :, :, :, cols], local_sem.at[0]
                    )
                    copy.start()
                    copy.wait()

                return store

            when(r < 8, put(g2, 0))
            when((r >= 8) & (r < 16), put(g1, 8))
            when((r >= 16) & (r < 18), put(go, 16))
            when(r >= 18, put(gq, 18))

    def weight(place_idx):
        return buf[place_idx].reshape(D, UNIT)

    def pair(ref, n):
        return jnp.concatenate([ref[2 * n], ref[2 * n + 1]], axis=1)

    def put_pair(ref, n, value):
        ref[2 * n] = value[:, :SLAB]
        ref[2 * n + 1] = value[:, SLAB:]

    def token_exchange(which, ref, i):
        return remote(
            ref.at[pl.ds(i * 2 * R, R)],
            ref.at[pl.ds((i * 2 + 1) * R, R)],
            ts.at[which, i],
            tr.at[which, i],
            core,
        )

    def partial_exchange(which, side, j):
        return remote(snd.at[j], rcv.at[side, j], xs.at[which, j], xr.at[which, j], core)

    def project(which, side, slabs, places, tick=None):
        def one(j, carry):
            left = jnp.concatenate([ref[n] for ref, n in slabs], axis=1)
            jh, jl = lax.div(j, 2), lax.rem(j, 2)
            right = jnp.concatenate(
                [buf[u, jh, jl].reshape(UNIT, UNIT) for u in places], axis=1
            )
            total = mm(left, right, 1, 1)
            for i in range(images):
                own[j, pl.ds(i * R, R)] = total[i * 2 * R : (i * 2 + 1) * R]
                snd[j, pl.ds(i * R, R)] = total[(i * 2 + 1) * R : (i * 2 + 2) * R].astype(BF16)
            partial_exchange(which, side, j).start()
            if tick is not None:
                tick(j)
            return carry

        lax.fori_loop(0, D // UNIT, one, 0)

    def partial_wait(which, side):
        for j in range(D // UNIT):
            partial_exchange(which, side, j).wait()

    def summed(side, rows):
        return jnp.concatenate(
            [own[j, rows] + rcv[side, j, rows].astype(F32) for j in range(D // UNIT)], axis=1
        )

    CHUNK = 16

    def token_loop(i, body):
        def step(c, carry):
            r = pl.multiple_of(i * R + c * CHUNK, CHUNK)
            full = pl.multiple_of(i * 2 * R + c * CHUNK, CHUNK)
            body(pl.ds(r, CHUNK), pl.ds(full, CHUNK))
            return carry

        lax.fori_loop(0, R // CHUNK, step, 0, unroll=R // CHUNK)

    def tokens_of(i, rows):
        return tok[rows].astype(F32)

    if linked:
        vb[0] = vec_in[...]

        wait(weight_copies[:6])
        for k, device in enumerate((adev, xdev, bdev, ydev)):
            copy = remote(vb.at[k], vbr.at[k], vgs.at[k], vgr.at[k], device)
            copy.start()
            gather_tick(k)
            copy.wait()
            vb[k + 1] = vb[k] + vbr[k]
        vec[...] = vb[4].astype(F32)
    else:
        wait(weight_copies[:6])
        vec[...] = vec_in[...].astype(F32)

    def vector(n):
        return jnp.concatenate([vec[4 * n + k : 4 * n + k + 1] for k in range(4)], axis=1)

    gain1, shift1, out_bias, gain2, shift2, fc2_bias = [vector(n) for n in range(6)]
    gvec[...] = jnp.zeros_like(gvec)
    acc[...] = jnp.zeros_like(acc)
    lse[...] = jnp.zeros_like(lse)

    for i in range(images):

        def norm_one(rows, full):
            normed, _ = stats(tok[rows].astype(F32))
            h1[full] = (normed * gain1 + shift1).astype(BF16)

        token_loop(i, norm_one)
        token_exchange(0, h1, i).start()
        if i == 0:
            gather_tick(4)
    wait(weight_copies[6:])
    wait(cot_copies)
    for i in range(images):
        token_exchange(1, cot, i).start()
    gather_ticks(5, 3 + 4 * LAG)
    for i in range(images):
        token_exchange(0, h1, i).wait()
        token_exchange(1, cot, i).wait()

    lane = lax.broadcasted_iota(jnp.int32, (2 * R, SLAB), 1)
    row = lax.broadcasted_iota(jnp.int32, (2 * R, SLAB), 0)
    second_half = row >= R
    inside = jnp.where(second_half, row - R, row)
    position = inside + jnp.where(second_half, (1 - t_idx) * half, t_idx * half)
    low_lanes = lane[:R] < HD

    def head_lanes(e, lanes):
        return lanes < HD if e == 0 else lanes >= HD

    def extra(e):
        return HD * (1 - e)

    def key_bias(i):
        valid = (inside < half) & (position < lengths[i])
        return jnp.where(valid, 0.0, -1e30)

    def project_heads(c):
        def one(j, carry):
            u = 3 * c + j
            value = mm(h1[...], weight(16 + u), 1, 0) + vec[pl.ds(24 + u, 1)]
            put_pair(qkv, u, value.astype(BF16))
            return carry

        lax.fori_loop(0, 3, one, 0)

    def attend(i, c, p):
        rows = pl.ds(pl.multiple_of(i * 2 * R, 16), 2 * R)
        q = qkv[c * 6 + p, rows].astype(F32) * HD**-0.5
        k = qkv[c * 6 + 2 + p, rows].astype(F32)
        v = qkv[c * 6 + 4 + p, rows]
        bias = key_bias(i)
        heads = []
        for e in range(2):
            inhead = head_lanes(e, lane)
            first_extra = lane == extra(e)
            qm = jnp.where(inhead, q, jnp.where(first_extra, 1.0, 0.0)).astype(BF16)
            km = jnp.where(inhead, k, jnp.where(first_extra, bias, 0.0)).astype(BF16)
            heads.append((qm, km))
        for m in range(2):
            outs, sums = [], []
            for e in range(2):
                qm, km = heads[e]
                scores = mm(qm[m * R : (m + 1) * R], km, 1, 1)
                peak = jnp.max(scores, -1, keepdims=True)
                exps = jnp.exp(scores - peak)
                total = jnp.sum(exps, -1, keepdims=True)
                outs.append(mm(exps.astype(BF16), v, 1, 0) * (1.0 / total))
                sums.append(peak + jnp.log(total))
            tile = pl.ds(pl.multiple_of(i * 2 * R + m * R, 16), R)
            ctx[2 * c + p, tile] = jnp.where(low_lanes, outs[0], outs[1]).astype(BF16)
            column = lane[:R]
            head = (2 * c + p) * 2
            lse[tile] = jnp.where(
                column == head, sums[0], jnp.where(column == head + 1, sums[1], lse[tile])
            )

    for c in range(2):
        project_heads(c)

        def attend_step(n, carry):
            if linked:
                pl.when(n < 3)(lambda: gather_tick(3 + 4 * LAG + 3 * c + n))
            attend(lax.div(n, 2), c, lax.rem(n, 2))
            return carry

        lax.fori_loop(0, images * 2, attend_step, 0)

    project(0, 0, [(ctx, n) for n in range(4)], [22, 23])
    gather_tick(9 + 4 * LAG)
    partial_wait(0, 0)
    for i in range(images):

        def norm_two(rows, full):
            middle = tok[rows].astype(F32) + summed(0, rows) + out_bias
            mid[rows] = middle
            normed, _ = stats(middle)
            h2[full] = (normed * gain2 + shift2).astype(BF16)

        token_loop(i, norm_two)
        token_exchange(2, h2, i).start()
        if i == 0:
            gather_tick(10 + 4 * LAG)
    gather_tick(11 + 4 * LAG)
    for i in range(images):
        token_exchange(2, h2, i).wait()

    def hidden(u, carry):
        if linked:
            pl.when(lax.rem(u, 2) == 0)(lambda: gather_tick(12 + 4 * LAG + lax.div(u, 2)))
        pre = mm(h2[...], weight(8 + u), 1, 0) + vec[pl.ds(30 + u, 1)]
        sig = 0.5 * jnp.tanh(0.851 * pre) + 0.5
        active = pre * sig
        slope = sig + 1.702 * active * (1.0 - sig)
        put_pair(act, u, active.astype(BF16))
        put_pair(gp, u, slope.astype(BF16))
        return carry

    lax.fori_loop(0, 8, hidden, 0)

    def hidden_back(u, carry):
        put_grad(u, mm(cot[...], pair(act, u), 0, 0))
        gather_tick(16 + 4 * LAG + u)
        pre_grad = mm(cot[...], weight(u), 1, 0) * pair(gp, u).astype(F32)
        gvec[pl.ds(28 + u, 1)] = jnp.sum(pre_grad, 0, keepdims=True)
        put_pair(gp, u, pre_grad.astype(BF16))
        if linked:
            pl.when(lax.rem(u, 2) == 1)(lambda: scatter_tick(lax.div(u, 2)))
        return carry

    lax.fori_loop(0, 8, hidden_back, 0)

    def odd_tick(base):
        if not linked:
            return None

        def tick(j):
            pl.when(lax.rem(j, 2) == 1)(lambda: scatter_tick(base + lax.div(j, 2)))

        return tick

    project(1, 1, [(act, n) for n in range(16)], list(range(8)), odd_tick(4))

    def first_grad(u, carry):
        put_grad(8 + u, mm(h2[...], pair(gp, u), 0, 0))
        if linked:
            pl.when(lax.rem(u, 4) == 3)(lambda: scatter_tick(6 + lax.div(u, 4)))
        return carry

    lax.fori_loop(0, 8, first_grad, 0)
    partial_wait(1, 1)
    for i in range(images):

        def finish(rows, full):
            total = mid[rows] + summed(1, rows) + fc2_bias
            result[rows] = total.astype(BF16)

        token_loop(i, finish)
    project(2, 0, [(gp, n) for n in range(16)], list(range(8, 16)), odd_tick(8))
    partial_wait(2, 0)

    def add_rows(n, value):
        acc[n] += value[:8] + value[8:]

    for i in range(images):

        def norm_two_back(rows, full):
            grad = summed(0, rows)
            normed, inverse = stats(mid[rows])
            cots = cot[full].astype(F32)
            middle_grad = cots + stats_back(grad * gain2, normed, inverse)
            add_rows(2, middle_grad)
            add_rows(3, grad * normed)
            add_rows(4, grad)
            add_rows(5, cots)
            mid[rows] = middle_grad
            cot[full] = middle_grad.astype(BF16)

        token_loop(i, norm_two_back)
        token_exchange(3, cot, i).start()
        if i == 0:
            scatter_tick(10)
    scatter_tick(11)
    for i in range(images):
        token_exchange(3, cot, i).wait()

    def out_back(u, carry):
        put_grad(16 + u, mm(cot[...], pair(ctx, u), 0, 0))
        return carry

    lax.fori_loop(0, 2, out_back, 0)
    scatter_tick(12)

    def context_back(u, carry):
        value = mm(cot[...], weight(22 + u), 1, 0)
        put_pair(act, 6 + u, value.astype(BF16))
        return carry

    lax.fori_loop(0, 2, context_back, 0)

    def attend_back(i, c, p):
        rows = pl.ds(pl.multiple_of(i * 2 * R, 16), 2 * R)
        q = qkv[c * 6 + p, rows].astype(F32) * HD**-0.5
        k = qkv[c * 6 + 2 + p, rows]
        v = qkv[c * 6 + 4 + p, rows]
        up = act[12 + 2 * c + p, rows]
        inner_all = up.astype(F32) * ctx[2 * c + p, rows].astype(F32)
        sums_all = lse[rows]
        bias = key_bias(i)
        q_low = q.astype(BF16)
        q_grads, k_grads, v_grads = [], [], []
        for e in range(2):
            inhead = head_lanes(e, lane)
            at = [lane == extra(e) + n for n in range(4)]
            head = (2 * c + p) * 2 + e
            total = jnp.sum(jnp.where(lane == head, sums_all, 0.0), -1, keepdims=True)
            inner = jnp.sum(jnp.where(inhead, inner_all, 0.0), -1, keepdims=True)
            s1, s2, s3 = three_terms(-total)
            n1, n2, n3 = three_terms(-inner)
            ones = at[1] | at[2] | at[3]
            qa = jnp.where(
                inhead,
                q,
                jnp.where(
                    at[0],
                    1.0,
                    jnp.where(at[1], s1, jnp.where(at[2], s2, jnp.where(at[3], s3, 0.0))),
                ),
            ).astype(BF16)
            ka = jnp.where(
                inhead, k.astype(F32), jnp.where(at[0], bias, jnp.where(ones, 1.0, 0.0))
            ).astype(BF16)
            ua = jnp.where(
                inhead,
                up.astype(F32),
                jnp.where(at[1], n1, jnp.where(at[2], n2, jnp.where(at[3], n3, 0.0))),
            ).astype(BF16)
            va = jnp.where(inhead, v.astype(F32), jnp.where(ones, 1.0, 0.0)).astype(BF16)
            q_grad = None
            k_parts, v_parts = [], []
            for m in range(2):
                tile = slice(m * R, (m + 1) * R)
                probs = jnp.exp(mm(ka[tile], qa, 1, 1))
                grads = (probs * mm(va[tile], ua, 1, 1)).astype(BF16)
                v_parts.append(mm(probs.astype(BF16), up, 1, 0))
                k_parts.append(mm(grads, q_low, 1, 0))
                part = mm(grads, k[tile], 0, 0)
                q_grad = part if q_grad is None else q_grad + part
            q_grads.append(q_grad * HD**-0.5)
            k_grads.append(k_parts)
            v_grads.append(v_parts)
        low = lane < HD
        q_sum = jnp.where(low, q_grads[0], q_grads[1])
        act[c * 6 + p, rows] = q_sum.astype(BF16)
        v_bias = None
        for m in range(2):
            tile = pl.ds(pl.multiple_of(i * 2 * R + m * R, 16), R)
            k_sum = jnp.where(low_lanes, k_grads[0][m], k_grads[1][m])
            v_sum = jnp.where(low_lanes, v_grads[0][m], v_grads[1][m])
            act[c * 6 + 2 + p, tile] = k_sum.astype(BF16)
            act[c * 6 + 4 + p, tile] = v_sum.astype(BF16)
            part = jnp.sum(v_sum, 0, keepdims=True)
            v_bias = part if v_bias is None else v_bias + part
        bias_row = jnp.concatenate([jnp.sum(q_sum, 0, keepdims=True), v_bias], axis=1)
        gvec[pl.ds(24 + 2 * c + p, 1)] += bias_row

    for c in range(2):

        def attend_back_step(n, carry):
            scatter_tick(13 + 4 * c + n)
            attend_back(lax.div(n, 2), c, lax.rem(n, 2))
            return carry

        lax.fori_loop(0, images * 2, attend_back_step, 0)

        def heads_grad(j, carry):
            u = 3 * c + j
            put_grad(18 + u, mm(h1[...], pair(act, u), 0, 0))
            return carry

        lax.fori_loop(0, 3, heads_grad, 0)
    scatter_tick(21)
    project(3, 1, [(act, n) for n in range(12)], list(range(16, 22)), odd_tick(22))
    partial_wait(3, 1)
    for i in range(images):

        def norm_one_back(rows, full):
            grad = summed(1, rows)
            normed, inverse = stats(tok[rows].astype(F32))
            add_rows(0, grad * normed)
            add_rows(1, grad)
            total = mid[rows] + stats_back(grad * gain1, normed, inverse)
            tok_grad[rows] = total.astype(BF16)

        token_loop(i, norm_one_back)
        if i == 0:
            scatter_tick(24)

    for n in range(6):
        total = jnp.sum(acc[n], 0, keepdims=True)
        for k in range(4):
            gvec[4 * n + k : 4 * n + k + 1] = total[:, k * UNIT : (k + 1) * UNIT]

    def sum_copy(k, stage, device):
        return remote(vs.at[stage], vr.at[k], vss.at[k], vsr.at[k], device)

    vs[0] = gvec[...]
    over_core = sum_copy(0, 0, core)
    over_core.start()
    over_core.wait()
    shared = lax.broadcasted_iota(jnp.int32, (GVEC_ROWS, UNIT), 0) < 24
    gathered = vs[0] + jnp.where(shared, vr[0], 0.0)
    if linked:
        vs[1] = gathered
        for k, device in enumerate((adev, xdev, bdev, ydev)):
            copy = sum_copy(k + 1, k + 1, device)
            copy.start()
            if k < 3:
                scatter_tick(25 + k)
            copy.wait()
            vs[k + 2] = vs[k + 1] + vr[k + 1]
        scatter_ticks(28, STEPS)
        gvec[...] = vs[5]
    else:
        gvec[...] = gathered


def own_part(values, index, width):
    return lax.dynamic_slice_in_dim(values, index * width, width, axis=1)


def body(
    linked,
    tokens,
    lengths,
    ln1_gain,
    ln1_bias,
    qkv_weight,
    qv_bias,
    out_weight,
    out_bias,
    ln2_gain,
    ln2_bias,
    fc1_weight,
    fc1_bias,
    fc2_weight,
    fc2_bias,
    cotangent,
):
    images, half, D = tokens.shape
    parts = lax.axis_size("dp")
    dp = lax.axis_index("dp")
    heads = qv_bias.shape[0]
    R = -(-half // 16) * 16
    T = images * 2 * R
    share = D // parts
    pad = ((0, 0), (0, R - half), (0, 0))
    tok = jnp.pad(tokens, pad).reshape(images * R, D)
    cot = jnp.pad(cotangent, pad)

    def placed(values, width):
        if linked:
            wide = jnp.tile(values, (1, parts))
            at = lax.broadcasted_iota(jnp.int32, wide.shape, 1) // width == dp
            return jnp.where(at, wide, jnp.zeros_like(wide))
        return lax.all_gather(values, "dp", axis=1, tiled=True)

    norms = placed(
        jnp.stack([ln1_gain, ln1_bias, out_bias, ln2_gain, ln2_bias, fc2_bias]), share
    ).reshape(24, UNIT)
    qv = placed(qv_bias, 2 * HD // parts if linked else 1).reshape(2, 2, 2, 2, HD)
    q_rows = qv[:, :, :, 0].reshape(2, 1, UNIT)
    v_rows = qv[:, :, :, 1].reshape(2, 1, UNIT)
    qkv_rows = jnp.concatenate([q_rows, jnp.zeros_like(q_rows), v_rows], axis=1).reshape(6, UNIT)
    fc1_rows = placed(fc1_bias, 128 // parts if linked else 1).reshape(8, UNIT)
    vec = jnp.concatenate(
        [norms, qkv_rows, fc1_rows, jnp.zeros((VEC_ROWS - 38, UNIT), BF16)], axis=0
    )

    grouped = qkv_weight.reshape(share, heads // 4, 4, 3, HD)
    wq = jnp.swapaxes(grouped, 2, 3).reshape(share, heads * 3 * HD)
    weights = [wq, out_weight, fc1_weight, fc2_weight]
    if not linked:
        weights = [
            lax.all_gather(w, "dp", axis=0, tiled=True).reshape(
                BLOCKS + (D // 16, w.shape[1])
            )
            for w in weights
        ]
    vmem = pl.BlockSpec(memory_space=pltpu.VMEM)
    hbm = pl.BlockSpec(memory_space=pl.ANY)
    if linked:
        grads = [jax.ShapeDtypeStruct(w.shape, F32) for w in weights]
    else:
        grads = [jax.ShapeDtypeStruct(w.shape, BF16) for w in weights]
    grad_spec = vmem if linked else hbm
    dma = pltpu.SemaphoreType.DMA
    block = BLOCKS + (D // 16, UNIT)
    outs = pl.pallas_call(
        functools.partial(layer_kernel, images, half, R, linked),
        out_shape=[
            jax.ShapeDtypeStruct((images * R, D), BF16),
            jax.ShapeDtypeStruct((images * R, D), BF16),
            *grads,
            jax.ShapeDtypeStruct((GVEC_ROWS, UNIT), F32),
        ],
        in_specs=[pl.BlockSpec(memory_space=pltpu.SMEM), vmem, hbm, vmem, hbm, hbm, hbm, hbm],
        out_specs=[vmem, vmem, grad_spec, grad_spec, grad_spec, grad_spec, vmem],
        scratch_shapes=[
            pltpu.VMEM((32,) + block, BF16),
            pltpu.VMEM((T, D), BF16),
            pltpu.VMEM((12, T, SLAB), BF16),
            pltpu.VMEM((4, T, SLAB), BF16),
            pltpu.VMEM((T, D), BF16),
            pltpu.VMEM((16, T, SLAB), BF16),
            pltpu.VMEM((16, T, SLAB), BF16),
            pltpu.VMEM((T, D), BF16),
            pltpu.VMEM((images * R, D), F32),
            pltpu.VMEM((4, images * R, UNIT), F32),
            pltpu.VMEM((4, images * R, UNIT), BF16),
            pltpu.VMEM((2, 4, images * R, UNIT), BF16),
            pltpu.VMEM((T, SLAB), F32),
            pltpu.VMEM((VEC_ROWS, UNIT), F32),
            pltpu.VMEM((6, 8, D), F32),
            pltpu.VMEM((RING, 2, 2, 2, 2, 32, UNIT), BF16),
            pltpu.VMEM((RING, 2, 2, 2, 32, UNIT), BF16),
            pltpu.VMEM((RING, 2, 2, 32, UNIT), BF16),
            pltpu.VMEM((RING, 64, UNIT), BF16),
            pltpu.VMEM((5, VEC_ROWS, UNIT), BF16),
            pltpu.VMEM((4, VEC_ROWS, UNIT), BF16),
            pltpu.VMEM((6, GVEC_ROWS, UNIT), F32),
            pltpu.VMEM((5, GVEC_ROWS, UNIT), F32),
            dma((24,)),
            dma((images,)),
            dma((RING, 8)),
            dma((RING, 8)),
            dma((RING, 8)),
            dma((RING, 8)),
            dma((4, 4)),
            dma((4, 4)),
            dma((4, images)),
            dma((4, images)),
            dma((5,)),
            dma((5,)),
            dma((6,)),
            dma((6,)),
        ],
        compiler_params=pltpu.CompilerParams(
            collective_id=0, has_side_effects=True, vmem_limit_bytes=64 * 2**20 - 2**16
        ),
        name="layer",
    )(lengths, tok, cot, vec, *weights)
    result, tok_grad, gq, go, g1, g2, gvec = outs

    def unpadded(values):
        return values.reshape(images, R, D)[:, :half]

    def owned(values):
        if linked:
            return values
        flat = values.reshape(D, values.shape[-1]).astype(F32)
        return lax.psum_scatter(flat, "dp", scatter_dimension=0, tiled=True)

    gq, go, g1, g2 = owned(gq), owned(go), owned(g1), owned(g2)
    gq = jnp.swapaxes(gq.reshape(share, heads // 4, 3, 4, HD), 2, 3).reshape(share, heads * 3 * HD)
    if not linked:
        gvec = lax.psum(gvec, "dp")
    norms_grad = own_part(gvec[:24].reshape(6, D), dp, share)
    qv_grad = jnp.swapaxes(gvec[24:28].reshape(4, 2, 2, HD), 1, 2).reshape(heads, 2 * HD)
    qv_grad = own_part(qv_grad, dp, 2 * HD // parts)
    fc1_grad = own_part(gvec[28:36].reshape(-1, 128), dp, 128 // parts)
    return (
        unpadded(result),
        unpadded(tok_grad),
        norms_grad[0],
        norms_grad[1],
        gq,
        qv_grad,
        go,
        norms_grad[2],
        norms_grad[3],
        norms_grad[4],
        g1,
        fc1_grad,
        g2,
        norms_grad[5],
    )


def solution(mesh):
    linked = mesh.shape["dp"] == 16
    vector = P("dp")
    weight = P("dp", "tensor")
    bias = P("tensor", "dp")
    tokens = P("dp", "tensor", None)
    in_specs = (
        tokens,
        vector,
        vector,
        vector,
        weight,
        bias,
        weight,
        vector,
        vector,
        vector,
        weight,
        bias,
        weight,
        vector,
        tokens,
    )
    out_specs = (
        tokens,
        tokens,
        vector,
        vector,
        weight,
        bias,
        weight,
        vector,
        vector,
        vector,
        weight,
        bias,
        weight,
        vector,
    )
    return jax.shard_map(
        functools.partial(body, linked),
        mesh=mesh,
        in_specs=in_specs,
        out_specs=out_specs,
        check_vma=False,
    )
```

```python
import functools

import jax
import jax.numpy as jnp
from jax import lax
from jax.experimental import pallas as pl
from jax.experimental.pallas import tpu as pltpu
from jax.sharding import PartitionSpec as P

HD = 64
UNIT = 256
SLAB = 128
LAG = 2
RING = 2 * LAG + 2
STEPS = 24 + 4 * LAG
BLOCKS = (2, 2, 2, 2)
VEC_ROWS = 48
QKV_ROW, FC1_ROW = 32, 38
GVEC_ROWS = 40
F32 = jnp.float32
BF16 = jnp.bfloat16
MESH = pl.DeviceIdType.MESH


def mm(left, right, left_dim, right_dim):
    return lax.dot_general(
        left, right, (((left_dim,), (right_dim,)), ((), ())), preferred_element_type=F32
    )


def when(condition, action):
    if isinstance(condition, bool):
        if condition:
            action()
    else:
        pl.when(condition)(action)


def stats(values):
    center = values - jnp.mean(values, -1, keepdims=True)
    inverse = lax.rsqrt(jnp.mean(center * center, -1, keepdims=True) + 1e-05)
    return center * inverse, inverse


def stats_back(scaled, normed, inverse):
    return inverse * (
        scaled
        - jnp.mean(scaled, -1, keepdims=True)
        - normed * jnp.mean(scaled * normed, -1, keepdims=True)
    )


def three_terms(values):
    first = values.astype(BF16).astype(F32)
    second = (values - first).astype(BF16).astype(F32)
    return first, second, values - first - second


def layer_kernel(
    images,
    half,
    rows_half,
    linked,
    lengths,
    tok_hbm,
    cot_hbm,
    small_in,
    wq_in,
    wo_in,
    w1_in,
    w2_in,
    result,
    tok_grad,
    gq,
    go,
    g1,
    g2,
    gvec,
    buf,
    tok,
    gq_units,
    small,
    h1,
    qkv,
    ctx,
    h2,
    act,
    gp,
    cot,
    mid,
    own,
    snd,
    rcv,
    lse,
    vec,
    acc,
    r1,
    r2,
    r3,
    r4,
    vb,
    vbr,
    vs,
    vr,
    local_sem,
    cot_sem,
    gs,
    gr,
    hs,
    hr,
    xs,
    xr,
    ts,
    tr,
    vgs,
    vgr,
    vss,
    vsr,
):
    R = rows_half
    T = images * 2 * R
    D = tok_hbm.shape[-1]
    tok_in, cot_in = tok_grad, result
    CHUNK = 16
    chunks = R // CHUNK
    rest = half - (chunks - 1) * CHUNK
    d_idx = lax.axis_index("dp")
    t_idx = lax.axis_index("tensor")
    core = {"dp": d_idx, "tensor": 1 - t_idx}
    if linked:
        x = lax.rem(d_idx, 2)
        y = lax.rem(lax.div(d_idx, 2), 2)
        b = lax.rem(lax.div(d_idx, 4), 2)
        a = lax.div(d_idx, 8)

        def chip(aa, bb, yy, xx):
            return {"dp": ((aa * 2 + bb) * 2 + yy) * 2 + xx, "tensor": t_idx}

        xdev = chip(a, b, y, 1 - x)
        ydev = chip(a, b, 1 - y, x)
        bdev = chip(a, 1 - b, y, x)
        adev = chip(1 - a, b, y, x)
    else:
        a = b = y = x = 0
        xdev = ydev = bdev = adev = None

    def remote(src, dst, send, recv, device):
        return pltpu.make_async_remote_copy(
            src_ref=src,
            dst_ref=dst,
            send_sem=send,
            recv_sem=recv,
            device_id=device,
            device_id_type=MESH,
        )

    def start(copies):
        for copy in copies:
            copy.start()

    def wait(copies):
        for copy in copies:
            copy.wait()

    barrier = pltpu.get_barrier_semaphore()
    peers = [core] + ([xdev, ydev, bdev, adev] if linked else [])
    for peer in peers:
        pl.semaphore_signal(barrier, inc=1, device_id=peer, device_id_type=MESH)

    def unit_source(s):
        ref, u = (
            (wq_in, s)
            if s < 6
            else (wo_in, s - 6)
            if s < 8
            else (w1_in, s - 8)
            if s < 16
            else (w2_in, s - 16)
        )
        cols = pl.ds(u * UNIT, UNIT)
        return ref.at[:, cols] if linked else ref.at[:, :, :, :, :, cols]

    def place(s):
        return s + 16 - 16 * (s // 8)

    def place_dyn(s):
        return s + 16 - 16 * lax.div(s, 8)

    weight_copies = []
    for s in range(6 if linked else 0, 24):
        target = buf.at[place(s), a, b, y, x] if linked else buf.at[place(s)]
        weight_copies.append(pltpu.make_async_copy(unit_source(s), target, local_sem.at[s]))
    start(weight_copies)
    cot_copy = pltpu.make_async_copy(cot_hbm, cot_in, cot_sem.at[0])
    cot_copy.start()
    tok_copy = pltpu.make_async_copy(tok_hbm, tok_in, cot_sem.at[1])
    tok_copy.start()

    half_lane = lax.broadcasted_iota(jnp.int32, (D // 16, SLAB), 1) < HD

    def swap(values):
        return pltpu.roll(values, HD, 1)

    if linked:
        for n in range(4):
            tiles = [
                wq_in[:, (3 * n + k) * SLAB : (3 * n + k + 1) * SLAB].astype(F32) for k in range(3)
            ]
            kinds = (
                jnp.where(half_lane, tiles[0], tiles[1]),
                jnp.where(half_lane, swap(tiles[0]), swap(tiles[2])),
                jnp.where(half_lane, tiles[1], tiles[2]),
            )
            for k, kind in enumerate(kinds):
                lanes = pl.ds((n % 2) * SLAB, SLAB)
                buf[place(3 * (n // 2) + k), a, b, y, x, :, lanes] = kind.astype(BF16)

    def take_tokens(source, target, rows_of, low, high):
        for c in range(low, high):
            for i in range(images):
                base = rows_of(i) + c * CHUNK
                if c < chunks - 1 or rest == CHUNK:
                    target[base : base + CHUNK] = source[c * CHUNK : (c + 1) * CHUNK, i, :]
                else:
                    target[base : base + CHUNK] = jnp.zeros((CHUNK, D), BF16)
                    target[base : base + rest] = source[c * CHUNK : half, i, :]

    def put_tokens(target, c, i, value, last):
        if last and rest < CHUNK:
            target[half - rest : half, i, :] = value[:rest]
        else:
            target[pl.ds(c * CHUNK, CHUNK), i, :] = value

    pl.semaphore_wait(barrier, len(peers))

    TOP, LOW = pl.ds(0, 32), pl.ds(32, 32)

    def spread(k, s):
        u, slot = place_dyn(s), lax.rem(s, RING)
        if k == 0:
            moves = [(buf.at[u, a, b, y, x], adev)]
        elif k == 1:
            moves = [(buf.at[u, :, b, y, x, TOP], xdev), (buf.at[u, :, b, y, x, LOW], ydev)]
        elif k == 2:
            moves = [(buf.at[u, :, b, y, :, TOP], bdev), (buf.at[u, :, b, :, x, LOW], bdev)]
        else:
            moves = [(buf.at[u, :, :, y, :, TOP], ydev), (buf.at[u, :, :, :, x, LOW], xdev)]
        return [
            remote(ref, ref, gs.at[slot, 2 * k + n], gr.at[slot, 2 * k + n], device)
            for n, (ref, device) in enumerate(moves)
        ]

    def gather_tick(s):
        if not linked:
            return
        s = jnp.int32(s)
        when(s < 24, lambda: start(spread(0, s)))
        for k in range(4):
            unit = s - (k + 1) * LAG

            def further(k=k, unit=unit):
                wait(spread(k, unit))
                if k < 3:
                    start(spread(k + 1, unit))

            when((unit >= 0) & (unit < 24), further)

    def gather_ticks(low, high):
        if not linked or low >= high:
            return

        def one(s, carry):
            gather_tick(s)
            return carry

        lax.fori_loop(low, high, one, 0)

    def grad_place(r):
        return lax.rem(r + 24, 32)

    def collect(k, r):
        g, slot = grad_place(r), lax.rem(r, RING)
        if k == 0:
            moves = [
                (buf.at[g, :, :, 1 - y, :, TOP], r1.at[slot, 0], ydev),
                (buf.at[g, :, :, :, 1 - x, LOW], r1.at[slot, 1], xdev),
            ]
        elif k == 1:
            moves = [
                (buf.at[g, :, 1 - b, y, :, TOP], r2.at[slot, 0], bdev),
                (buf.at[g, :, 1 - b, :, x, LOW], r2.at[slot, 1], bdev),
            ]
        elif k == 2:
            moves = [
                (buf.at[g, :, b, y, 1 - x, TOP], r3.at[slot, 0], xdev),
                (buf.at[g, :, b, 1 - y, x, LOW], r3.at[slot, 1], ydev),
            ]
        else:
            moves = [(buf.at[g, 1 - a, b, y, x], r4.at[slot], adev)]
        return [
            remote(src, dst, hs.at[slot, 2 * k + n], hr.at[slot, 2 * k + n], device)
            for n, (src, dst, device) in enumerate(moves)
        ]

    def add_parts(k, r):
        g, slot = grad_place(r), lax.rem(r, RING)
        if k == 0:
            top, low, parts = (g, slice(None), slice(None), y, slice(None), TOP), (
                (g, slice(None), slice(None), slice(None), x, LOW)
            ), r1
        elif k == 1:
            top, low, parts = (g, slice(None), b, y, slice(None), TOP), (
                (g, slice(None), b, slice(None), x, LOW)
            ), r2
        else:
            top, low, parts = (g, slice(None), b, y, x, TOP), (g, slice(None), b, y, x, LOW), r3
        buf[top] = (buf[top].astype(F32) + parts[slot, 0].astype(F32)).astype(BF16)
        buf[low] = (buf[low].astype(F32) + parts[slot, 1].astype(F32)).astype(BF16)

    def add_last(r):
        g, slot = grad_place(r), lax.rem(r, RING)
        total = buf[g, a, b, y, x].astype(F32) + r4[slot].astype(F32)

        def put(ref, base):
            def store():
                ref[:, pl.ds(pl.multiple_of((r - base) * UNIT, UNIT), UNIT)] = total

            return store

        when(r < 8, put(g2, 0))
        when((r >= 8) & (r < 16), put(g1, 8))
        when((r >= 16) & (r < 18), put(go, 16))
        when(r >= 18, put(gq_units, 18))

    def scatter_tick(s):
        if not linked:
            return
        s = jnp.int32(s)
        when((s >= 0) & (s < 24), lambda: start(collect(0, s)))
        for k in range(4):
            unit = s - (k + 1) * LAG

            def further(k=k, unit=unit):
                wait(collect(k, unit))
                if k < 3:
                    add_parts(k, unit)
                    start(collect(k + 1, unit))
                else:
                    add_last(unit)

            when((unit >= 0) & (unit < 24), further)

    def scatter_ticks(low, high):
        if not linked or low >= high:
            return

        def one(s, carry):
            scatter_tick(s)
            return carry

        lax.fori_loop(low, high, one, 0)

    def put_grad(r, value):
        buf[grad_place(r)] = value.astype(BF16).reshape(BLOCKS + (D // 16, UNIT))
        if not linked:

            def put(ref, base):
                def store():
                    cols = pl.ds(pl.multiple_of((r - base) * UNIT, UNIT), UNIT)
                    copy = pltpu.make_async_copy(
                        buf.at[grad_place(r)], ref.at[:, :, :, :, :, cols], local_sem.at[0]
                    )
                    copy.start()
                    copy.wait()

                return store

            when(r < 8, put(g2, 0))
            when((r >= 8) & (r < 16), put(g1, 8))
            when((r >= 16) & (r < 18), put(go, 16))
            when(r >= 18, put(gq, 18))

    def weight(place_idx):
        return buf[place_idx].reshape(D, UNIT)

    def pair(ref, n):
        return jnp.concatenate([ref[2 * n], ref[2 * n + 1]], axis=1)

    def put_pair(ref, n, value):
        ref[2 * n] = value[:, :SLAB]
        ref[2 * n + 1] = value[:, SLAB:]

    def token_exchange(which, ref, i):
        return remote(
            ref.at[pl.ds(i * 2 * R, R)],
            ref.at[pl.ds((i * 2 + 1) * R, R)],
            ts.at[which, i],
            tr.at[which, i],
            core,
        )

    def partial_exchange(which, side, j):
        return remote(snd.at[j], rcv.at[side, j], xs.at[which, j], xr.at[which, j], core)

    def project(which, side, slabs, places, tick=None):
        def one(j, carry):
            left = jnp.concatenate([ref[n] for ref, n in slabs], axis=1)
            jh, jl = lax.div(j, 2), lax.rem(j, 2)
            right = jnp.concatenate(
                [buf[u, jh, jl].reshape(UNIT, UNIT) for u in places], axis=1
            )
            total = mm(left, right, 1, 1)
            for i in range(images):
                own[j, pl.ds(i * R, R)] = total[i * 2 * R : (i * 2 + 1) * R]
                snd[j, pl.ds(i * R, R)] = total[(i * 2 + 1) * R : (i * 2 + 2) * R].astype(BF16)
            partial_exchange(which, side, j).start()
            if tick is not None:
                tick(j)
            return carry

        lax.fori_loop(0, D // UNIT, one, 0)

    def partial_wait(which, side):
        for j in range(D // UNIT):
            partial_exchange(which, side, j).wait()

    def summed(side, rows):
        return jnp.concatenate(
            [own[j, rows] + rcv[side, j, rows].astype(F32) for j in range(D // UNIT)], axis=1
        )

    def token_loop(i, body):
        def step(c, carry):
            r = pl.multiple_of(i * R + c * CHUNK, CHUNK)
            full = pl.multiple_of(i * 2 * R + c * CHUNK, CHUNK)
            body(pl.ds(r, CHUNK), pl.ds(full, CHUNK), c, False)
            return carry

        lax.fori_loop(0, chunks - 1, step, 0, unroll=chunks - 1)
        c = chunks - 1
        body(pl.ds(i * R + c * CHUNK, CHUNK), pl.ds(i * 2 * R + c * CHUNK, CHUNK), c, True)

    def compact(i):
        return i * R

    if linked:
        small[...] = jnp.zeros_like(small)
        for n in range(6):
            small[n : n + 1, : D // 16] = small_in[n][...].astype(F32)
        small[8:16, :8] = small_in[6][...].astype(F32)
        small[32:40, :16] = small_in[7][...].astype(F32)
        small[16:32, :8] = jnp.transpose(small[32:40])[:16, :8]
        vb[0] = jnp.zeros((VEC_ROWS, UNIT), BF16)
        twice = small[:8] + swap(small[:8])
        wide_lane = lax.broadcasted_iota(jnp.int32, (8, D), 1)
        wide = jnp.concatenate([twice] * (D // SLAB), axis=1)
        wide = jnp.where(lax.div(wide_lane, HD) == d_idx, wide, 0.0)
        for k in range(4):
            vb[0, 8 * k : 8 * k + 8] = wide[:, k * UNIT : (k + 1) * UNIT].astype(BF16)
        heads_bias = pltpu.roll(small[8:16], d_idx * 8, 1)
        heads_swap = swap(heads_bias)
        row_low = half_lane[:1]
        for c in range(2):
            q_parts, v_parts = [], []
            for p in range(2):
                n = 4 * c + 2 * p
                q_parts.append(
                    jnp.where(row_low, heads_bias[n : n + 1], heads_swap[n + 1 : n + 2])
                )
                v_parts.append(
                    jnp.where(row_low, heads_swap[n : n + 1], heads_bias[n + 1 : n + 2])
                )
            base = QKV_ROW + 3 * c
            vb[0, base : base + 1] = jnp.concatenate(q_parts, axis=1).astype(BF16)
            vb[0, base + 2 : base + 3] = jnp.concatenate(v_parts, axis=1).astype(BF16)
        hidden_bias = pltpu.roll(small[16:32], d_idx * 8, 1)
        for u in range(8):
            vb[0, FC1_ROW + u : FC1_ROW + u + 1] = jnp.concatenate(
                [hidden_bias[2 * u : 2 * u + 1], hidden_bias[2 * u + 1 : 2 * u + 2]], axis=1
            ).astype(BF16)
        for k, device in enumerate((adev, xdev, bdev, ydev)):
            copy = remote(vb.at[k], vbr.at[k], vgs.at[k], vgr.at[k], device)
            copy.start()
            if k == 3:
                wait(weight_copies)
            gather_ticks(2 * k, 2 * k + 2)
            if k == 0:
                tok_copy.wait()
            if k < 2:
                cuts = (0, chunks // 2, chunks)
                take_tokens(tok_in, tok, compact, cuts[k], cuts[k + 1])
            copy.wait()
            vb[k + 1] = vb[k] + vbr[k]
        vec[...] = vb[4].astype(F32)
    else:
        wait(weight_copies)
        tok_copy.wait()
        take_tokens(tok_in, tok, compact, 0, chunks)
        vec[...] = small_in[0][...].astype(F32)

    def vector(n):
        return jnp.concatenate([vec[8 * k + n : 8 * k + n + 1] for k in range(4)], axis=1)

    gain1, shift1, out_bias, gain2, shift2, fc2_bias = [vector(n) for n in range(6)]
    gvec[...] = jnp.zeros_like(gvec)
    acc[...] = jnp.zeros_like(acc)
    lse[...] = jnp.zeros_like(lse)

    for i in range(images):

        def norm_one(rows, full, c, last):
            normed, _ = stats(tok[rows].astype(F32))
            h1[full] = (normed * gain1 + shift1).astype(BF16)

        token_loop(i, norm_one)
        token_exchange(0, h1, i).start()
        gather_tick(8 + i)
    cot_copy.wait()
    take_tokens(cot_in, cot, lambda i: i * 2 * R, 0, chunks)
    for i in range(images):
        token_exchange(1, cot, i).start()
    gather_ticks(8 + images, 3 + 4 * LAG)
    for i in range(images):
        token_exchange(0, h1, i).wait()
        token_exchange(1, cot, i).wait()

    lane = lax.broadcasted_iota(jnp.int32, (2 * R, SLAB), 1)
    row = lax.broadcasted_iota(jnp.int32, (2 * R, SLAB), 0)
    second_half = row >= R
    inside = jnp.where(second_half, row - R, row)
    position = inside + jnp.where(second_half, (1 - t_idx) * half, t_idx * half)
    low_lanes = lane[:R] < HD

    def head_lanes(e, lanes):
        return lanes < HD if e == 0 else lanes >= HD

    def extra(e):
        return HD * (1 - e)

    def key_bias(i):
        valid = (inside < half) & (position < lengths[i])
        return jnp.where(valid, 0.0, -1e30)

    def project_heads(c):
        def one(j, carry):
            u = 3 * c + j
            value = mm(h1[...], weight(16 + u), 1, 0) + vec[pl.ds(QKV_ROW + u, 1)]
            put_pair(qkv, u, value.astype(BF16))
            return carry

        lax.fori_loop(0, 3, one, 0)

    def attend(i, c, p):
        rows = pl.ds(pl.multiple_of(i * 2 * R, 16), 2 * R)
        q = qkv[c * 6 + p, rows].astype(F32) * HD**-0.5
        k = qkv[c * 6 + 2 + p, rows].astype(F32)
        v = qkv[c * 6 + 4 + p, rows]
        bias = key_bias(i)
        heads = []
        for e in range(2):
            inhead = head_lanes(e, lane)
            first_extra = lane == extra(e)
            qm = jnp.where(inhead, q, jnp.where(first_extra, 1.0, 0.0)).astype(BF16)
            km = jnp.where(inhead, k, jnp.where(first_extra, bias, 0.0)).astype(BF16)
            heads.append((qm, km))
        for m in range(2):
            outs, sums = [], []
            for e in range(2):
                qm, km = heads[e]
                scores = mm(qm[m * R : (m + 1) * R], km, 1, 1)
                peak = jnp.max(scores, -1, keepdims=True)
                exps = jnp.exp(scores - peak)
                total = jnp.sum(exps, -1, keepdims=True)
                outs.append(mm(exps.astype(BF16), v, 1, 0) * (1.0 / total))
                sums.append(peak + jnp.log(total))
            tile = pl.ds(pl.multiple_of(i * 2 * R + m * R, 16), R)
            ctx[2 * c + p, tile] = jnp.where(low_lanes, outs[0], outs[1]).astype(BF16)
            column = lane[:R]
            head = (2 * c + p) * 2
            lse[tile] = jnp.where(
                column == head, sums[0], jnp.where(column == head + 1, sums[1], lse[tile])
            )

    for c in range(2):
        project_heads(c)

        def attend_step(n, carry):
            if linked:
                pl.when(n < 3)(lambda: gather_tick(3 + 4 * LAG + 3 * c + n))
            attend(lax.div(n, 2), c, lax.rem(n, 2))
            return carry

        lax.fori_loop(0, images * 2, attend_step, 0)

    project(0, 0, [(ctx, n) for n in range(4)], [22, 23])
    gather_ticks(9 + 4 * LAG, 11 + 4 * LAG)
    partial_wait(0, 0)
    for i in range(images):

        def norm_two(rows, full, c, last):
            middle = tok[rows].astype(F32) + summed(0, rows) + out_bias
            mid[rows] = middle
            normed, _ = stats(middle)
            h2[full] = (normed * gain2 + shift2).astype(BF16)

        token_loop(i, norm_two)
        token_exchange(2, h2, i).start()
        if i == 0:
            gather_tick(11 + 4 * LAG)
    gather_tick(12 + 4 * LAG)
    for i in range(images):
        token_exchange(2, h2, i).wait()

    def hidden(u, carry):
        if linked:
            pl.when(lax.rem(u, 2) == 0)(lambda: gather_tick(13 + 4 * LAG + lax.div(u, 2)))
        pre = mm(h2[...], weight(8 + u), 1, 0) + vec[pl.ds(FC1_ROW + u, 1)]
        sig = 0.5 * jnp.tanh(0.851 * pre) + 0.5
        active = pre * sig
        slope = sig + 1.702 * active * (1.0 - sig)
        put_pair(act, u, active.astype(BF16))
        put_pair(gp, u, slope.astype(BF16))
        return carry

    lax.fori_loop(0, 8, hidden, 0)

    def hidden_back(u, carry):
        put_grad(u, mm(cot[...], pair(act, u), 0, 0))
        gather_tick(17 + 4 * LAG + u)
        pre_grad = mm(cot[...], weight(u), 1, 0) * pair(gp, u).astype(F32)
        gvec[pl.ds(28 + u, 1)] = jnp.sum(pre_grad, 0, keepdims=True)
        put_pair(gp, u, pre_grad.astype(BF16))
        if linked:
            pl.when(lax.rem(u, 2) == 1)(lambda: scatter_tick(lax.div(u, 2)))
        return carry

    lax.fori_loop(0, 8, hidden_back, 0)

    def odd_tick(base):
        if not linked:
            return None

        def tick(j):
            pl.when(lax.rem(j, 2) == 1)(lambda: scatter_tick(base + lax.div(j, 2)))

        return tick

    project(1, 1, [(act, n) for n in range(16)], list(range(8)), odd_tick(4))

    def first_grad(u, carry):
        put_grad(8 + u, mm(h2[...], pair(gp, u), 0, 0))
        if linked:
            pl.when(lax.rem(u, 4) == 3)(lambda: scatter_tick(6 + lax.div(u, 4)))
        return carry

    lax.fori_loop(0, 8, first_grad, 0)
    partial_wait(1, 1)
    for i in range(images):

        def finish(rows, full, c, last):
            total = mid[rows] + summed(1, rows) + fc2_bias
            put_tokens(result, c, i, total.astype(BF16), last)

        token_loop(i, finish)
    project(2, 0, [(gp, n) for n in range(16)], list(range(8, 16)), odd_tick(8))
    partial_wait(2, 0)

    def add_rows(n, value):
        acc[n] += value[:8] + value[8:]

    for i in range(images):

        def norm_two_back(rows, full, c, last):
            grad = summed(0, rows)
            normed, inverse = stats(mid[rows])
            cots = cot[full].astype(F32)
            middle_grad = cots + stats_back(grad * gain2, normed, inverse)
            add_rows(2, middle_grad)
            add_rows(3, grad * normed)
            add_rows(4, grad)
            add_rows(5, cots)
            mid[rows] = middle_grad
            cot[full] = middle_grad.astype(BF16)

        token_loop(i, norm_two_back)
        token_exchange(3, cot, i).start()
        if i == 0:
            scatter_tick(10)
    scatter_tick(11)
    for i in range(images):
        token_exchange(3, cot, i).wait()

    def out_back(u, carry):
        put_grad(16 + u, mm(cot[...], pair(ctx, u), 0, 0))
        return carry

    lax.fori_loop(0, 2, out_back, 0)
    scatter_tick(12)

    def context_back(u, carry):
        value = mm(cot[...], weight(22 + u), 1, 0)
        put_pair(act, 6 + u, value.astype(BF16))
        return carry

    lax.fori_loop(0, 2, context_back, 0)

    def attend_back(i, c, p):
        rows = pl.ds(pl.multiple_of(i * 2 * R, 16), 2 * R)
        q = qkv[c * 6 + p, rows].astype(F32) * HD**-0.5
        k = qkv[c * 6 + 2 + p, rows]
        v = qkv[c * 6 + 4 + p, rows]
        up = act[12 + 2 * c + p, rows]
        inner_all = up.astype(F32) * ctx[2 * c + p, rows].astype(F32)
        sums_all = lse[rows]
        bias = key_bias(i)
        q_low = q.astype(BF16)
        q_grads, k_grads, v_grads = [], [], []
        for e in range(2):
            inhead = head_lanes(e, lane)
            at = [lane == extra(e) + n for n in range(4)]
            head = (2 * c + p) * 2 + e
            total = jnp.sum(jnp.where(lane == head, sums_all, 0.0), -1, keepdims=True)
            inner = jnp.sum(jnp.where(inhead, inner_all, 0.0), -1, keepdims=True)
            s1, s2, s3 = three_terms(-total)
            n1, n2, n3 = three_terms(-inner)
            ones = at[1] | at[2] | at[3]
            qa = jnp.where(
                inhead,
                q,
                jnp.where(
                    at[0],
                    1.0,
                    jnp.where(at[1], s1, jnp.where(at[2], s2, jnp.where(at[3], s3, 0.0))),
                ),
            ).astype(BF16)
            ka = jnp.where(
                inhead, k.astype(F32), jnp.where(at[0], bias, jnp.where(ones, 1.0, 0.0))
            ).astype(BF16)
            ua = jnp.where(
                inhead,
                up.astype(F32),
                jnp.where(at[1], n1, jnp.where(at[2], n2, jnp.where(at[3], n3, 0.0))),
            ).astype(BF16)
            va = jnp.where(inhead, v.astype(F32), jnp.where(ones, 1.0, 0.0)).astype(BF16)
            q_grad = None
            k_parts, v_parts = [], []
            for m in range(2):
                tile = slice(m * R, (m + 1) * R)
                probs = jnp.exp(mm(ka[tile], qa, 1, 1))
                grads = (probs * mm(va[tile], ua, 1, 1)).astype(BF16)
                v_parts.append(mm(probs.astype(BF16), up, 1, 0))
                k_parts.append(mm(grads, q_low, 1, 0))
                part = mm(grads, k[tile], 0, 0)
                q_grad = part if q_grad is None else q_grad + part
            q_grads.append(q_grad * HD**-0.5)
            k_grads.append(k_parts)
            v_grads.append(v_parts)
        low = lane < HD
        q_sum = jnp.where(low, q_grads[0], q_grads[1])
        act[c * 6 + p, rows] = q_sum.astype(BF16)
        v_bias = None
        for m in range(2):
            tile = pl.ds(pl.multiple_of(i * 2 * R + m * R, 16), R)
            k_sum = jnp.where(low_lanes, k_grads[0][m], k_grads[1][m])
            v_sum = jnp.where(low_lanes, v_grads[0][m], v_grads[1][m])
            act[c * 6 + 2 + p, tile] = k_sum.astype(BF16)
            act[c * 6 + 4 + p, tile] = v_sum.astype(BF16)
            part = jnp.sum(v_sum, 0, keepdims=True)
            v_bias = part if v_bias is None else v_bias + part
        bias_row = jnp.concatenate([jnp.sum(q_sum, 0, keepdims=True), v_bias], axis=1)
        gvec[pl.ds(24 + 2 * c + p, 1)] += bias_row

    for c in range(2):

        def attend_back_step(n, carry):
            scatter_tick(13 + 4 * c + n)
            attend_back(lax.div(n, 2), c, lax.rem(n, 2))
            return carry

        lax.fori_loop(0, images * 2, attend_back_step, 0)

        def heads_grad(j, carry):
            u = 3 * c + j
            put_grad(18 + u, mm(h1[...], pair(act, u), 0, 0))
            return carry

        lax.fori_loop(0, 3, heads_grad, 0)
    scatter_tick(21)
    project(3, 1, [(act, n) for n in range(12)], list(range(16, 22)), odd_tick(22))
    partial_wait(3, 1)
    for i in range(images):

        def norm_one_back(rows, full, c, last):
            grad = summed(1, rows)
            normed, inverse = stats(tok[rows].astype(F32))
            add_rows(0, grad * normed)
            add_rows(1, grad)
            total = mid[rows] + stats_back(grad * gain1, normed, inverse)
            put_tokens(tok_grad, c, i, total.astype(BF16), last)

        token_loop(i, norm_one_back)
        if i == 0:
            scatter_tick(24)

    for n in range(6):
        total = jnp.sum(acc[n], 0, keepdims=True)
        for k in range(4):
            gvec[4 * n + k : 4 * n + k + 1] = total[:, k * UNIT : (k + 1) * UNIT]

    def sum_copy(k, stage, device):
        return remote(vs.at[stage], vr.at[k], vss.at[k], vsr.at[k], device)

    vs[0] = gvec[...]
    over_core = sum_copy(0, 0, core)
    over_core.start()
    scatter_tick(25)
    over_core.wait()
    shared = lax.broadcasted_iota(jnp.int32, (GVEC_ROWS, UNIT), 0) < 24
    gathered = vs[0] + jnp.where(shared, vr[0], 0.0)
    if linked:
        vs[1] = gathered
        for k, device in enumerate((adev, xdev, bdev, ydev)):
            copy = sum_copy(k + 1, k + 1, device)
            copy.start()
            scatter_ticks(26 + k, 27 + k)
            copy.wait()
            vs[k + 2] = vs[k + 1] + vr[k + 1]
        scatter_ticks(30, STEPS)
        gvec[...] = vs[5]
        for n in range(4):
            kinds = [
                gq_units[
                    :,
                    (3 * (n // 2) + k) * UNIT + (n % 2) * SLAB : (3 * (n // 2) + k) * UNIT
                    + (n % 2 + 1) * SLAB,
                ]
                for k in range(3)
            ]
            keys = swap(kinds[1])
            tiles = (
                jnp.where(half_lane, kinds[0], keys),
                jnp.where(half_lane, kinds[2], kinds[0]),
                jnp.where(half_lane, keys, kinds[2]),
            )
            for k, tile in enumerate(tiles):
                gq[:, (3 * n + k) * SLAB : (3 * n + k + 1) * SLAB] = tile
    else:
        gvec[...] = gathered


def output_kernel(result, tok_grad, gq, go, g1, g2, gvec, *refs):
    outs, held, sems = refs[:14], refs[14:20], refs[20]
    sources = (result, tok_grad, gq, go, g1, g2)
    arrive = [
        pltpu.make_async_copy(source, target, sems.at[0, n])
        for n, (source, target) in enumerate(zip(sources, held))
    ]
    leave = [
        pltpu.make_async_copy(source, target, sems.at[1, n])
        for n, (source, target) in enumerate(zip(held, outs[:6]))
    ]
    for copy in arrive:
        copy.start()
    d_idx = lax.axis_index("dp")
    values = gvec[...]
    low = lax.broadcasted_iota(jnp.int32, (8, SLAB), 1) < HD
    rows = [
        jnp.concatenate([values[4 * n + k : 4 * n + k + 1] for k in range(4)], axis=1)
        for n in range(6)
    ]
    wide = jnp.concatenate(rows + [jnp.zeros_like(rows[0])] * 2, axis=0)
    mine = jnp.zeros((8, SLAB), F32)
    for n in range(wide.shape[1] // SLAB):
        tile = wide[:, n * SLAB : (n + 1) * SLAB]
        mine = jnp.where(lax.div(d_idx, 2) == n, tile, mine)
    mine = jnp.where(lax.rem(d_idx, 2) == 1, pltpu.roll(mine, HD, 1), mine)
    for n in range(6):
        outs[6 + n][...] = mine[n : n + 1, : outs[6 + n].shape[1]]
    head_rows = []
    for n in range(4):
        row = values[24 + n : 25 + n]
        q, v = row[:, :SLAB], row[:, SLAB:]
        head_rows.append(jnp.where(low[:1], q, pltpu.roll(v, HD, 1)))
        head_rows.append(jnp.where(low[:1], pltpu.roll(q, HD, 1), v))
    back = SLAB - d_idx * 8
    mine = pltpu.roll(jnp.concatenate(head_rows, axis=0), back, 1)
    outs[12][...] = mine[:, : outs[12].shape[1]]
    hidden_rows = []
    for n in range(8):
        row = values[28 + n : 29 + n]
        hidden_rows += [row[:, :SLAB], row[:, SLAB:]]
    mine = pltpu.roll(jnp.concatenate(hidden_rows, axis=0), back, 1)
    outs[13][...] = jnp.transpose(mine)[: outs[13].shape[0]]
    for n in range(6):
        arrive[n].wait()
        leave[n].start()
    for copy in leave:
        copy.wait()


def own_part(values, index, width):
    return lax.dynamic_slice_in_dim(values, index * width, width, axis=1)


def body(
    linked,
    tokens,
    lengths,
    ln1_gain,
    ln1_bias,
    qkv_weight,
    qv_bias,
    out_weight,
    out_bias,
    ln2_gain,
    ln2_bias,
    fc1_weight,
    fc1_bias,
    fc2_weight,
    fc2_bias,
    cotangent,
):
    images, half, D = tokens.shape
    parts = lax.axis_size("dp")
    dp = lax.axis_index("dp")
    heads = qv_bias.shape[0]
    R = -(-half // 16) * 16
    T = images * 2 * R
    share = D // parts
    tok = jnp.swapaxes(tokens, 0, 1)
    cot = jnp.swapaxes(cotangent, 0, 1)
    norms = (ln1_gain, ln1_bias, out_bias, ln2_gain, ln2_bias, fc2_bias)
    if linked:
        vec = (*[v.reshape(1, share) for v in norms], qv_bias, jnp.transpose(fc1_bias))
        wq = qkv_weight
    else:
        norms = lax.all_gather(jnp.stack(norms), "dp", axis=1, tiled=True).reshape(6, 4, UNIT)
        norms = jnp.pad(jnp.swapaxes(norms, 0, 1), ((0, 0), (0, 2), (0, 0))).reshape(32, UNIT)
        qv = lax.all_gather(qv_bias, "dp", axis=1, tiled=True).reshape(2, 2, 2, 2, HD)
        q_rows = qv[:, :, :, 0].reshape(2, 1, UNIT)
        v_rows = qv[:, :, :, 1].reshape(2, 1, UNIT)
        qkv_rows = jnp.concatenate([q_rows, jnp.zeros_like(q_rows), v_rows], axis=1)
        fc1_rows = lax.all_gather(fc1_bias, "dp", axis=1, tiled=True).reshape(8, UNIT)
        unused = jnp.zeros((VEC_ROWS - 46, UNIT), BF16)
        vec = (jnp.concatenate([norms, qkv_rows.reshape(6, UNIT), fc1_rows, unused]),)
        grouped = qkv_weight.reshape(share, heads // 4, 4, 3, HD)
        wq = jnp.swapaxes(grouped, 2, 3).reshape(share, heads * 3 * HD)
    weights = [wq, out_weight, fc1_weight, fc2_weight]
    if not linked:
        weights = [
            lax.all_gather(w, "dp", axis=0, tiled=True).reshape(
                BLOCKS + (D // 16, w.shape[1])
            )
            for w in weights
        ]
    vmem = pl.BlockSpec(memory_space=pltpu.VMEM)
    hbm = pl.BlockSpec(memory_space=pl.ANY)
    if linked:
        grads = [jax.ShapeDtypeStruct(w.shape, F32) for w in weights]
    else:
        grads = [jax.ShapeDtypeStruct(w.shape, BF16) for w in weights]
    grad_spec = vmem if linked else hbm
    dma = pltpu.SemaphoreType.DMA
    block = BLOCKS + (D // 16, UNIT)
    outs = pl.pallas_call(
        functools.partial(layer_kernel, images, half, R, linked),
        out_shape=[
            jax.ShapeDtypeStruct((half, images, D), BF16),
            jax.ShapeDtypeStruct((half, images, D), BF16),
            *grads,
            jax.ShapeDtypeStruct((GVEC_ROWS, UNIT), F32),
        ],
        in_specs=[
            pl.BlockSpec(memory_space=pltpu.SMEM),
            hbm,
            hbm,
            tuple(vmem for _ in vec),
            vmem if linked else hbm,
            hbm,
            hbm,
            hbm,
        ],
        out_specs=[vmem, vmem, grad_spec, grad_spec, grad_spec, grad_spec, vmem],
        scratch_shapes=[
            pltpu.VMEM((32,) + block, BF16),
            pltpu.VMEM((images * R, D), BF16),
            pltpu.VMEM((D // 16, 6 * UNIT), F32),
            pltpu.VMEM((40, SLAB), F32),
            pltpu.VMEM((T, D), BF16),
            pltpu.VMEM((12, T, SLAB), BF16),
            pltpu.VMEM((4, T, SLAB), BF16),
            pltpu.VMEM((T, D), BF16),
            pltpu.VMEM((16, T, SLAB), BF16),
            pltpu.VMEM((16, T, SLAB), BF16),
            pltpu.VMEM((T, D), BF16),
            pltpu.VMEM((images * R, D), F32),
            pltpu.VMEM((4, images * R, UNIT), F32),
            pltpu.VMEM((4, images * R, UNIT), BF16),
            pltpu.VMEM((2, 4, images * R, UNIT), BF16),
            pltpu.VMEM((T, SLAB), F32),
            pltpu.VMEM((VEC_ROWS, UNIT), F32),
            pltpu.VMEM((6, 8, D), F32),
            pltpu.VMEM((RING, 2, 2, 2, 2, 32, UNIT), BF16),
            pltpu.VMEM((RING, 2, 2, 2, 32, UNIT), BF16),
            pltpu.VMEM((RING, 2, 2, 32, UNIT), BF16),
            pltpu.VMEM((RING, 64, UNIT), BF16),
            pltpu.VMEM((5, VEC_ROWS, UNIT), BF16),
            pltpu.VMEM((4, VEC_ROWS, UNIT), BF16),
            pltpu.VMEM((6, GVEC_ROWS, UNIT), F32),
            pltpu.VMEM((5, GVEC_ROWS, UNIT), F32),
            dma((24,)),
            dma((2,)),
            dma((RING, 8)),
            dma((RING, 8)),
            dma((RING, 8)),
            dma((RING, 8)),
            dma((4, 4)),
            dma((4, 4)),
            dma((4, images)),
            dma((4, images)),
            dma((5,)),
            dma((5,)),
            dma((6,)),
            dma((6,)),
        ],
        compiler_params=pltpu.CompilerParams(
            collective_id=0, has_side_effects=True, vmem_limit_bytes=64 * 2**20 - 2**16
        ),
        name="layer",
    )(lengths, tok, cot, vec, *weights)
    result, tok_grad, gq, go, g1, g2, gvec = outs
    if linked:
        large = (result, tok_grad, gq, go, g1, g2)
        result, tok_grad, gq, go, g1, g2, *norms_grad, qv_grad, fc1_grad = pl.pallas_call(
            output_kernel,
            out_shape=[
                *[jax.ShapeDtypeStruct(v.shape, v.dtype) for v in large],
                *[jax.ShapeDtypeStruct((1, share), F32)] * 6,
                jax.ShapeDtypeStruct((heads, 2 * HD // parts), F32),
                jax.ShapeDtypeStruct((128 // parts, fc1_bias.shape[0]), F32),
            ],
            in_specs=[hbm] * 6 + [vmem],
            out_specs=[hbm] * 6 + [vmem] * 8,
            scratch_shapes=[*[pltpu.VMEM(v.shape, v.dtype) for v in large], dma((2, 6))],
            name="outputs",
        )(*large, gvec)
        norms_grad = [v.reshape(share) for v in norms_grad]
        fc1_grad = jnp.transpose(fc1_grad)
    else:

        def owned(values):
            flat = values.reshape(D, values.shape[-1]).astype(F32)
            return lax.psum_scatter(flat, "dp", scatter_dimension=0, tiled=True)

        gq, go, g1, g2 = owned(gq), owned(go), owned(g1), owned(g2)
        gq = jnp.swapaxes(gq.reshape(share, heads // 4, 3, 4, HD), 2, 3)
        gq = gq.reshape(share, heads * 3 * HD)
        gvec = lax.psum(gvec, "dp")
        norms_grad = own_part(gvec[:24].reshape(6, D), dp, share)
        qv_grad = jnp.swapaxes(gvec[24:28].reshape(4, 2, 2, HD), 1, 2).reshape(heads, 2 * HD)
        qv_grad = own_part(qv_grad, dp, 2 * HD // parts)
        fc1_grad = own_part(gvec[28:36].reshape(-1, 128), dp, 128 // parts)
    return (
        jnp.swapaxes(result, 0, 1),
        jnp.swapaxes(tok_grad, 0, 1),
        norms_grad[0],
        norms_grad[1],
        gq,
        qv_grad,
        go,
        norms_grad[2],
        norms_grad[3],
        norms_grad[4],
        g1,
        fc1_grad,
        g2,
        norms_grad[5],
    )


def solution(mesh):
    linked = mesh.shape["dp"] == 16
    vector = P("dp")
    weight = P("dp", "tensor")
    bias = P("tensor", "dp")
    tokens = P("dp", "tensor", None)
    in_specs = (
        tokens,
        vector,
        vector,
        vector,
        weight,
        bias,
        weight,
        vector,
        vector,
        vector,
        weight,
        bias,
        weight,
        vector,
        tokens,
    )
    out_specs = (
        tokens,
        tokens,
        vector,
        vector,
        weight,
        bias,
        weight,
        vector,
        vector,
        vector,
        weight,
        bias,
        weight,
        vector,
    )
    return jax.shard_map(
        functools.partial(body, linked),
        mesh=mesh,
        in_specs=in_specs,
        out_specs=out_specs,
        check_vma=False,
    )
```

```python
import functools

import jax
import jax.numpy as jnp
from jax import lax
from jax.experimental import pallas as pl
from jax.experimental.pallas import tpu as pltpu
from jax.sharding import PartitionSpec as P

HD = 64
UNIT = 256
SLAB = 128
LAG = 2
RING = 2 * LAG + 1
STEPS = 24 + 4 * LAG
BLOCKS = (2, 2, 2, 2)
VEC_ROWS = 48
QKV_ROW, FC1_ROW = 32, 38
GVEC_ROWS = 40
F32 = jnp.float32
BF16 = jnp.bfloat16
MESH = pl.DeviceIdType.MESH


def mm(left, right, left_dim, right_dim):
    return lax.dot_general(
        left, right, (((left_dim,), (right_dim,)), ((), ())), preferred_element_type=F32
    )


def when(condition, action):
    if isinstance(condition, bool):
        if condition:
            action()
    else:
        pl.when(condition)(action)


def stats(values):
    center = values - jnp.mean(values, -1, keepdims=True)
    inverse = lax.rsqrt(jnp.mean(center * center, -1, keepdims=True) + 1e-05)
    return center * inverse, inverse


def stats_back(scaled, normed, inverse):
    return inverse * (
        scaled
        - jnp.mean(scaled, -1, keepdims=True)
        - normed * jnp.mean(scaled * normed, -1, keepdims=True)
    )


def three_terms(values):
    first = values.astype(BF16).astype(F32)
    second = (values - first).astype(BF16).astype(F32)
    return first, second, values - first - second


def layer_kernel(
    images,
    half,
    rows_half,
    linked,
    lengths,
    tok_hbm,
    cot_hbm,
    small_in,
    wq_in,
    wo_in,
    w1_in,
    w2_in,
    result,
    tok_grad,
    gq,
    go,
    g1,
    g2,
    gvec,
    buf,
    tok,
    gq_units,
    small,
    h1,
    qkv,
    ctx,
    h2,
    act,
    gp,
    cot,
    mid,
    own,
    snd,
    rcv,
    lse,
    vec,
    acc,
    r1,
    r2,
    r3,
    r4,
    vb,
    vbr,
    vs,
    vr,
    local_sem,
    cot_sem,
    gs,
    gr,
    hs,
    hr,
    xs,
    xr,
    ts,
    tr,
    vgs,
    vgr,
    vss,
    vsr,
):
    R = rows_half
    T = images * 2 * R
    D = tok_hbm.shape[-1]
    tok_in, cot_in = tok_grad, result
    CHUNK = 16
    chunks = R // CHUNK
    rest = half - (chunks - 1) * CHUNK
    d_idx = lax.axis_index("dp")
    t_idx = lax.axis_index("tensor")
    core = {"dp": d_idx, "tensor": 1 - t_idx}
    if linked:
        x = lax.rem(d_idx, 2)
        y = lax.rem(lax.div(d_idx, 2), 2)
        b = lax.rem(lax.div(d_idx, 4), 2)
        a = lax.div(d_idx, 8)

        def chip(aa, bb, yy, xx):
            return {"dp": ((aa * 2 + bb) * 2 + yy) * 2 + xx, "tensor": t_idx}

        xdev = chip(a, b, y, 1 - x)
        ydev = chip(a, b, 1 - y, x)
        bdev = chip(a, 1 - b, y, x)
        adev = chip(1 - a, b, y, x)
        column = [adev, bdev, chip(1 - a, 1 - b, y, x)]
        plane = [xdev, ydev, chip(a, b, 1 - y, 1 - x)]
    else:
        a = b = y = x = 0
        xdev = ydev = bdev = adev = None

    def remote(src, dst, send, recv, device):
        return pltpu.make_async_remote_copy(
            src_ref=src,
            dst_ref=dst,
            send_sem=send,
            recv_sem=recv,
            device_id=device,
            device_id_type=MESH,
        )

    def start(copies):
        for copy in copies:
            copy.start()

    def wait(copies):
        for copy in copies:
            copy.wait()

    barrier = pltpu.get_barrier_semaphore()
    peers = [core] + (column + plane if linked else [])
    for peer in peers:
        pl.semaphore_signal(barrier, inc=1, device_id=peer, device_id_type=MESH)

    def unit_source(s):
        ref, u = (
            (wq_in, s)
            if s < 6
            else (wo_in, s - 6)
            if s < 8
            else (w1_in, s - 8)
            if s < 16
            else (w2_in, s - 16)
        )
        cols = pl.ds(u * UNIT, UNIT)
        return ref.at[:, cols] if linked else ref.at[:, :, :, :, :, cols]

    def place(s):
        return s + 16 - 16 * (s // 8)

    def place_dyn(s):
        return s + 16 - 16 * lax.div(s, 8)

    weight_copies = []
    for s in range(6 if linked else 0, 24):
        target = buf.at[place(s), a, b, y, x] if linked else buf.at[place(s)]
        weight_copies.append(pltpu.make_async_copy(unit_source(s), target, local_sem.at[s]))
    start(weight_copies)
    cot_copy = pltpu.make_async_copy(cot_hbm, cot_in, cot_sem.at[0])
    cot_copy.start()
    tok_copy = pltpu.make_async_copy(tok_hbm, tok_in, cot_sem.at[1])
    tok_copy.start()

    half_lane = lax.broadcasted_iota(jnp.int32, (D // 16, SLAB), 1) < HD

    def swap(values):
        return pltpu.roll(values, HD, 1)

    if linked:
        for n in range(4):
            tiles = [
                wq_in[:, (3 * n + k) * SLAB : (3 * n + k + 1) * SLAB].astype(F32) for k in range(3)
            ]
            kinds = (
                jnp.where(half_lane, tiles[0], tiles[1]),
                jnp.where(half_lane, swap(tiles[0]), swap(tiles[2])),
                jnp.where(half_lane, tiles[1], tiles[2]),
            )
            for k, kind in enumerate(kinds):
                lanes = pl.ds((n % 2) * SLAB, SLAB)
                buf[place(3 * (n // 2) + k), a, b, y, x, :, lanes] = kind.astype(BF16)

    def take_tokens(source, target, rows_of, low, high):
        for c in range(low, high):
            for i in range(images):
                base = rows_of(i) + c * CHUNK
                if c < chunks - 1 or rest == CHUNK:
                    target[base : base + CHUNK] = source[c * CHUNK : (c + 1) * CHUNK, i, :]
                else:
                    target[base : base + CHUNK] = jnp.zeros((CHUNK, D), BF16)
                    target[base : base + rest] = source[c * CHUNK : half, i, :]

    def put_tokens(target, c, i, value, last):
        if last and rest < CHUNK:
            target[half - rest : half, i, :] = value[:rest]
        else:
            target[pl.ds(c * CHUNK, CHUNK), i, :] = value

    pl.semaphore_wait(barrier, len(peers))

    TOP, LOW = pl.ds(0, 32), pl.ds(32, 32)

    def spread(k, s):
        u, slot = place_dyn(s), lax.rem(s, RING)
        if k == 0:
            moves = [(buf.at[u, a, b, y, x], adev)]
        elif k == 1:
            moves = [(buf.at[u, :, b, y, x, TOP], xdev), (buf.at[u, :, b, y, x, LOW], ydev)]
        elif k == 2:
            moves = [(buf.at[u, :, b, y, :, TOP], bdev), (buf.at[u, :, b, :, x, LOW], bdev)]
        else:
            moves = [(buf.at[u, :, :, y, :, TOP], ydev), (buf.at[u, :, :, :, x, LOW], xdev)]
        return [
            remote(ref, ref, gs.at[slot, 2 * k + n], gr.at[slot, 2 * k + n], device)
            for n, (ref, device) in enumerate(moves)
        ]

    def gather_tick(s):
        if not linked:
            return
        s = jnp.int32(s)
        for k in (3, 2, 1, 0):
            unit = s - (k + 1) * LAG

            def further(k=k, unit=unit):
                wait(spread(k, unit))
                if k < 3:
                    start(spread(k + 1, unit))

            when((unit >= 0) & (unit < 24), further)
        when(s < 24, lambda: start(spread(0, s)))

    def gather_ticks(low, high):
        if not linked or low >= high:
            return

        def one(s, carry):
            gather_tick(s)
            return carry

        lax.fori_loop(low, high, one, 0)

    def grad_place(r):
        return lax.rem(r + 24, 32)

    def collect(k, r):
        g, slot = grad_place(r), lax.rem(r, RING)
        if k == 0:
            moves = [
                (buf.at[g, :, :, 1 - y, :, TOP], r1.at[slot, 0], ydev),
                (buf.at[g, :, :, :, 1 - x, LOW], r1.at[slot, 1], xdev),
            ]
        elif k == 1:
            moves = [
                (buf.at[g, :, 1 - b, y, :, TOP], r2.at[slot, 0], bdev),
                (buf.at[g, :, 1 - b, :, x, LOW], r2.at[slot, 1], bdev),
            ]
        elif k == 2:
            moves = [
                (buf.at[g, :, b, y, 1 - x, TOP], r3.at[slot, 0], xdev),
                (buf.at[g, :, b, 1 - y, x, LOW], r3.at[slot, 1], ydev),
            ]
        else:
            moves = [(buf.at[g, 1 - a, b, y, x], r4.at[slot], adev)]
        return [
            remote(src, dst, hs.at[slot, 2 * k + n], hr.at[slot, 2 * k + n], device)
            for n, (src, dst, device) in enumerate(moves)
        ]

    def add_parts(k, r):
        g, slot = grad_place(r), lax.rem(r, RING)
        if k == 0:
            top, low, parts = (g, slice(None), slice(None), y, slice(None), TOP), (
                (g, slice(None), slice(None), slice(None), x, LOW)
            ), r1
        elif k == 1:
            top, low, parts = (g, slice(None), b, y, slice(None), TOP), (
                (g, slice(None), b, slice(None), x, LOW)
            ), r2
        else:
            top, low, parts = (g, slice(None), b, y, x, TOP), (g, slice(None), b, y, x, LOW), r3
        buf[top] = buf[top] + parts[slot, 0]
        buf[low] = buf[low] + parts[slot, 1]

    def add_last(r):
        g, slot = grad_place(r), lax.rem(r, RING)
        total = buf[g, a, b, y, x].astype(F32) + r4[slot].astype(F32)

        def put(ref, base):
            def store():
                ref[:, pl.ds(pl.multiple_of((r - base) * UNIT, UNIT), UNIT)] = total

            return store

        when(r < 8, put(g2, 0))
        when((r >= 8) & (r < 16), put(g1, 8))
        when((r >= 16) & (r < 18), put(go, 16))
        when(r >= 18, put(gq_units, 18))

    def scatter_tick(s):
        if not linked:
            return
        s = jnp.int32(s)
        for k in (3, 2, 1, 0):
            unit = s - (k + 1) * LAG

            def further(k=k, unit=unit):
                wait(collect(k, unit))
                if k < 3:
                    add_parts(k, unit)
                    start(collect(k + 1, unit))
                else:
                    add_last(unit)

            when((unit >= 0) & (unit < 24), further)
        when((s >= 0) & (s < 24), lambda: start(collect(0, s)))

    def scatter_ticks(low, high):
        if not linked or low >= high:
            return

        def one(s, carry):
            scatter_tick(s)
            return carry

        lax.fori_loop(low, high, one, 0)

    def put_grad(r, value):
        buf[grad_place(r)] = value.astype(BF16).reshape(BLOCKS + (D // 16, UNIT))
        if not linked:

            def put(ref, base):
                def store():
                    cols = pl.ds(pl.multiple_of((r - base) * UNIT, UNIT), UNIT)
                    copy = pltpu.make_async_copy(
                        buf.at[grad_place(r)], ref.at[:, :, :, :, :, cols], local_sem.at[0]
                    )
                    copy.start()
                    copy.wait()

                return store

            when(r < 8, put(g2, 0))
            when((r >= 8) & (r < 16), put(g1, 8))
            when((r >= 16) & (r < 18), put(go, 16))
            when(r >= 18, put(gq, 18))

    def weight(place_idx):
        return buf[place_idx].reshape(D, UNIT)

    def pair(ref, n):
        return jnp.concatenate([ref[2 * n], ref[2 * n + 1]], axis=1)

    def put_pair(ref, n, value):
        ref[2 * n] = value[:, :SLAB]
        ref[2 * n + 1] = value[:, SLAB:]

    def token_exchange(which, ref, i):
        return remote(
            ref.at[pl.ds(i * 2 * R, R)],
            ref.at[pl.ds((i * 2 + 1) * R, R)],
            ts.at[which, i],
            tr.at[which, i],
            core,
        )

    def partial_exchange(which, side, j):
        return remote(snd.at[j], rcv.at[side, j], xs.at[which, j], xr.at[which, j], core)

    def project(which, side, slabs, places, tick=None):
        def one(j, carry):
            left = jnp.concatenate([ref[n] for ref, n in slabs], axis=1)
            jh, jl = lax.div(j, 2), lax.rem(j, 2)
            right = jnp.concatenate(
                [buf[u, jh, jl].reshape(UNIT, UNIT) for u in places], axis=1
            )
            total = mm(left, right, 1, 1)
            for i in range(images):
                own[j, pl.ds(i * R, R)] = total[i * 2 * R : (i * 2 + 1) * R]
                snd[j, pl.ds(i * R, R)] = total[(i * 2 + 1) * R : (i * 2 + 2) * R].astype(BF16)
            partial_exchange(which, side, j).start()
            if tick is not None:
                tick(j)
            return carry

        lax.fori_loop(0, D // UNIT, one, 0)

    def partial_wait(which, side):
        for j in range(D // UNIT):
            partial_exchange(which, side, j).wait()

    def summed(side, rows):
        return jnp.concatenate(
            [own[j, rows] + rcv[side, j, rows].astype(F32) for j in range(D // UNIT)], axis=1
        )

    def token_loop(i, body):
        def step(c, carry):
            r = pl.multiple_of(i * R + c * CHUNK, CHUNK)
            full = pl.multiple_of(i * 2 * R + c * CHUNK, CHUNK)
            body(pl.ds(r, CHUNK), pl.ds(full, CHUNK), c, False)
            return carry

        lax.fori_loop(0, chunks - 1, step, 0, unroll=chunks - 1)
        c = chunks - 1
        body(pl.ds(i * R + c * CHUNK, CHUNK), pl.ds(i * 2 * R + c * CHUNK, CHUNK), c, True)

    def compact(i):
        return i * R

    if linked:
        small[...] = jnp.zeros_like(small)
        for n in range(6):
            small[n : n + 1, : D // 16] = small_in[n][...].astype(F32)
        small[8:16, :8] = small_in[6][...].astype(F32)
        small[32:40, :16] = small_in[7][...].astype(F32)
        small[16:32, :8] = jnp.transpose(small[32:40])[:16, :8]
        vb[0] = jnp.zeros((VEC_ROWS, UNIT), BF16)
        twice = small[:8] + swap(small[:8])
        wide_lane = lax.broadcasted_iota(jnp.int32, (8, D), 1)
        wide = jnp.concatenate([twice] * (D // SLAB), axis=1)
        wide = jnp.where(lax.div(wide_lane, HD) == d_idx, wide, 0.0)
        for k in range(4):
            vb[0, 8 * k : 8 * k + 8] = wide[:, k * UNIT : (k + 1) * UNIT].astype(BF16)
        heads_bias = pltpu.roll(small[8:16], d_idx * 8, 1)
        heads_swap = swap(heads_bias)
        row_low = half_lane[:1]
        for c in range(2):
            q_parts, v_parts = [], []
            for p in range(2):
                n = 4 * c + 2 * p
                q_parts.append(
                    jnp.where(row_low, heads_bias[n : n + 1], heads_swap[n + 1 : n + 2])
                )
                v_parts.append(
                    jnp.where(row_low, heads_swap[n : n + 1], heads_bias[n + 1 : n + 2])
                )
            base = QKV_ROW + 3 * c
            vb[0, base : base + 1] = jnp.concatenate(q_parts, axis=1).astype(BF16)
            vb[0, base + 2 : base + 3] = jnp.concatenate(v_parts, axis=1).astype(BF16)
        hidden_bias = pltpu.roll(small[16:32], d_idx * 8, 1)
        for u in range(8):
            vb[0, FC1_ROW + u : FC1_ROW + u + 1] = jnp.concatenate(
                [hidden_bias[2 * u : 2 * u + 1], hidden_bias[2 * u + 1 : 2 * u + 2]], axis=1
            ).astype(BF16)
        for k, devices in enumerate((column, plane)):
            copies = [
                remote(vb.at[k], vbr.at[k, n], vgs.at[k, n], vgr.at[k, n], device)
                for n, device in enumerate(devices)
            ]
            start(copies)
            if k == 0:
                gather_ticks(0, 3)
                tok_copy.wait()
            else:
                wait(weight_copies)
                gather_ticks(3, 5)
            cuts = (0, chunks // 2, chunks)
            take_tokens(tok_in, tok, compact, cuts[k], cuts[k + 1])
            wait(copies)
            vb[k + 1] = vb[k] + vbr[k, 0] + vbr[k, 1] + vbr[k, 2]
        gather_ticks(5, 8)
        vec[...] = vb[2].astype(F32)
    else:
        wait(weight_copies)
        tok_copy.wait()
        take_tokens(tok_in, tok, compact, 0, chunks)
        vec[...] = small_in[0][...].astype(F32)

    def vector(n):
        return jnp.concatenate([vec[8 * k + n : 8 * k + n + 1] for k in range(4)], axis=1)

    gain1, shift1, out_bias, gain2, shift2, fc2_bias = [vector(n) for n in range(6)]
    gvec[...] = jnp.zeros_like(gvec)
    acc[...] = jnp.zeros_like(acc)
    lse[...] = jnp.zeros_like(lse)

    for i in range(images):

        def norm_one(rows, full, c, last):
            normed, _ = stats(tok[rows].astype(F32))
            h1[full] = (normed * gain1 + shift1).astype(BF16)

        token_loop(i, norm_one)
        token_exchange(0, h1, i).start()
        gather_tick(8 + i)
    cot_copy.wait()
    take_tokens(cot_in, cot, lambda i: i * 2 * R, 0, chunks)
    for i in range(images):
        token_exchange(1, cot, i).start()
    gather_ticks(8 + images, 3 + 4 * LAG)
    for i in range(images):
        token_exchange(0, h1, i).wait()
        token_exchange(1, cot, i).wait()

    lane = lax.broadcasted_iota(jnp.int32, (2 * R, SLAB), 1)
    row = lax.broadcasted_iota(jnp.int32, (2 * R, SLAB), 0)
    second_half = row >= R
    inside = jnp.where(second_half, row - R, row)
    position = inside + jnp.where(second_half, (1 - t_idx) * half, t_idx * half)
    low_lanes = lane[:R] < HD

    def head_lanes(e, lanes):
        return lanes < HD if e == 0 else lanes >= HD

    def extra(e):
        return HD * (1 - e)

    def key_bias(i):
        valid = (inside < half) & (position < lengths[i])
        return jnp.where(valid, 0.0, -1e30)

    def project_heads(c):
        def one(j, carry):
            u = 3 * c + j
            value = mm(h1[...], weight(16 + u), 1, 0) + vec[pl.ds(QKV_ROW + u, 1)]
            put_pair(qkv, u, value.astype(BF16))
            return carry

        lax.fori_loop(0, 3, one, 0)

    def attend(i, c, p):
        rows = pl.ds(pl.multiple_of(i * 2 * R, 16), 2 * R)
        q = qkv[c * 6 + p, rows].astype(F32) * HD**-0.5
        k = qkv[c * 6 + 2 + p, rows].astype(F32)
        v = qkv[c * 6 + 4 + p, rows]
        bias = key_bias(i)
        heads = []
        for e in range(2):
            inhead = head_lanes(e, lane)
            first_extra = lane == extra(e)
            qm = jnp.where(inhead, q, jnp.where(first_extra, 1.0, 0.0)).astype(BF16)
            km = jnp.where(inhead, k, jnp.where(first_extra, bias, 0.0)).astype(BF16)
            heads.append((qm, km))
        for m in range(2):
            outs, sums = [], []
            for e in range(2):
                qm, km = heads[e]
                scores = mm(qm[m * R : (m + 1) * R], km, 1, 1)
                peak = jnp.max(scores, -1, keepdims=True)
                exps = jnp.exp(scores - peak)
                total = jnp.sum(exps, -1, keepdims=True)
                outs.append(mm(exps.astype(BF16), v, 1, 0) * (1.0 / total))
                sums.append(peak + jnp.log(total))
            tile = pl.ds(pl.multiple_of(i * 2 * R + m * R, 16), R)
            ctx[2 * c + p, tile] = jnp.where(low_lanes, outs[0], outs[1]).astype(BF16)
            column = lane[:R]
            head = (2 * c + p) * 2
            lse[tile] = jnp.where(
                column == head, sums[0], jnp.where(column == head + 1, sums[1], lse[tile])
            )

    for c in range(2):
        project_heads(c)

        def attend_step(n, carry):
            if linked:
                pl.when(n < 3)(lambda: gather_tick(3 + 4 * LAG + 3 * c + n))
            attend(lax.div(n, 2), c, lax.rem(n, 2))
            return carry

        lax.fori_loop(0, images * 2, attend_step, 0)

    project(0, 0, [(ctx, n) for n in range(4)], [22, 23])
    gather_ticks(9 + 4 * LAG, 11 + 4 * LAG)
    partial_wait(0, 0)
    for i in range(images):

        def norm_two(rows, full, c, last):
            middle = tok[rows].astype(F32) + summed(0, rows) + out_bias
            mid[rows] = middle
            normed, _ = stats(middle)
            h2[full] = (normed * gain2 + shift2).astype(BF16)

        token_loop(i, norm_two)
        token_exchange(2, h2, i).start()
        if i == 0:
            gather_tick(11 + 4 * LAG)
    gather_tick(12 + 4 * LAG)
    for i in range(images):
        token_exchange(2, h2, i).wait()

    def hidden(u, carry):
        if linked:
            pl.when(lax.rem(u, 2) == 0)(lambda: gather_tick(13 + 4 * LAG + lax.div(u, 2)))
        pre = mm(h2[...], weight(8 + u), 1, 0) + vec[pl.ds(FC1_ROW + u, 1)]
        sig = 0.5 * jnp.tanh(0.851 * pre) + 0.5
        active = pre * sig
        slope = sig + 1.702 * active * (1.0 - sig)
        put_pair(act, u, active.astype(BF16))
        put_pair(gp, u, slope.astype(BF16))
        return carry

    lax.fori_loop(0, 8, hidden, 0)

    def hidden_back(u, carry):
        put_grad(u, mm(cot[...], pair(act, u), 0, 0))
        gather_tick(17 + 4 * LAG + u)
        pre_grad = mm(cot[...], weight(u), 1, 0) * pair(gp, u).astype(F32)
        gvec[pl.ds(28 + u, 1)] = jnp.sum(pre_grad, 0, keepdims=True)
        put_pair(gp, u, pre_grad.astype(BF16))
        if linked:
            pl.when(u >= 3)(lambda: scatter_tick(u - 3))
        return carry

    lax.fori_loop(0, 8, hidden_back, 0)

    def odd_tick(base):
        if not linked:
            return None

        def tick(j):
            pl.when(lax.rem(j, 2) == 1)(lambda: scatter_tick(base + lax.div(j, 2)))

        return tick

    project(1, 1, [(act, n) for n in range(16)], list(range(8)), odd_tick(5))

    def first_grad(u, carry):
        put_grad(8 + u, mm(h2[...], pair(gp, u), 0, 0))
        if linked:
            pl.when(lax.rem(u, 4) == 3)(lambda: scatter_tick(7 + lax.div(u, 4)))
        return carry

    lax.fori_loop(0, 8, first_grad, 0)
    partial_wait(1, 1)
    for i in range(images):

        def finish(rows, full, c, last):
            total = mid[rows] + summed(1, rows) + fc2_bias
            put_tokens(result, c, i, total.astype(BF16), last)

        token_loop(i, finish)
    project(2, 0, [(gp, n) for n in range(16)], list(range(8, 16)), odd_tick(9))
    partial_wait(2, 0)

    def add_rows(n, value):
        acc[n] += value[:8] + value[8:]

    for i in range(images):

        def norm_two_back(rows, full, c, last):
            grad = summed(0, rows)
            normed, inverse = stats(mid[rows])
            cots = cot[full].astype(F32)
            middle_grad = cots + stats_back(grad * gain2, normed, inverse)
            add_rows(2, middle_grad)
            add_rows(3, grad * normed)
            add_rows(4, grad)
            add_rows(5, cots)
            mid[rows] = middle_grad
            cot[full] = middle_grad.astype(BF16)

        token_loop(i, norm_two_back)
        token_exchange(3, cot, i).start()
        if i == 0:
            scatter_tick(11)
    scatter_tick(12)
    for i in range(images):
        token_exchange(3, cot, i).wait()

    def out_back(u, carry):
        put_grad(16 + u, mm(cot[...], pair(ctx, u), 0, 0))
        return carry

    lax.fori_loop(0, 2, out_back, 0)
    scatter_tick(13)

    def context_back(u, carry):
        value = mm(cot[...], weight(22 + u), 1, 0)
        put_pair(act, 6 + u, value.astype(BF16))
        return carry

    lax.fori_loop(0, 2, context_back, 0)

    def attend_back(i, c, p):
        rows = pl.ds(pl.multiple_of(i * 2 * R, 16), 2 * R)
        q = qkv[c * 6 + p, rows].astype(F32) * HD**-0.5
        k = qkv[c * 6 + 2 + p, rows]
        v = qkv[c * 6 + 4 + p, rows]
        up = act[12 + 2 * c + p, rows]
        inner_all = up.astype(F32) * ctx[2 * c + p, rows].astype(F32)
        sums_all = lse[rows]
        bias = key_bias(i)
        q_low = q.astype(BF16)
        q_grads, k_grads, v_grads = [], [], []
        for e in range(2):
            inhead = head_lanes(e, lane)
            at = [lane == extra(e) + n for n in range(4)]
            head = (2 * c + p) * 2 + e
            total = jnp.sum(jnp.where(lane == head, sums_all, 0.0), -1, keepdims=True)
            inner = jnp.sum(jnp.where(inhead, inner_all, 0.0), -1, keepdims=True)
            s1, s2, s3 = three_terms(-total)
            n1, n2, n3 = three_terms(-inner)
            ones = at[1] | at[2] | at[3]
            qa = jnp.where(
                inhead,
                q,
                jnp.where(
                    at[0],
                    1.0,
                    jnp.where(at[1], s1, jnp.where(at[2], s2, jnp.where(at[3], s3, 0.0))),
                ),
            ).astype(BF16)
            ka = jnp.where(
                inhead, k.astype(F32), jnp.where(at[0], bias, jnp.where(ones, 1.0, 0.0))
            ).astype(BF16)
            ua = jnp.where(
                inhead,
                up.astype(F32),
                jnp.where(at[1], n1, jnp.where(at[2], n2, jnp.where(at[3], n3, 0.0))),
            ).astype(BF16)
            va = jnp.where(inhead, v.astype(F32), jnp.where(ones, 1.0, 0.0)).astype(BF16)
            q_grad = None
            k_parts, v_parts = [], []
            for m in range(2):
                tile = slice(m * R, (m + 1) * R)
                probs = jnp.exp(mm(ka[tile], qa, 1, 1))
                grads = (probs * mm(va[tile], ua, 1, 1)).astype(BF16)
                v_parts.append(mm(probs.astype(BF16), up, 1, 0))
                k_parts.append(mm(grads, q_low, 1, 0))
                part = mm(grads, k[tile], 0, 0)
                q_grad = part if q_grad is None else q_grad + part
            q_grads.append(q_grad * HD**-0.5)
            k_grads.append(k_parts)
            v_grads.append(v_parts)
        low = lane < HD
        q_sum = jnp.where(low, q_grads[0], q_grads[1])
        act[c * 6 + p, rows] = q_sum.astype(BF16)
        v_bias = None
        for m in range(2):
            tile = pl.ds(pl.multiple_of(i * 2 * R + m * R, 16), R)
            k_sum = jnp.where(low_lanes, k_grads[0][m], k_grads[1][m])
            v_sum = jnp.where(low_lanes, v_grads[0][m], v_grads[1][m])
            act[c * 6 + 2 + p, tile] = k_sum.astype(BF16)
            act[c * 6 + 4 + p, tile] = v_sum.astype(BF16)
            part = jnp.sum(v_sum, 0, keepdims=True)
            v_bias = part if v_bias is None else v_bias + part
        bias_row = jnp.concatenate([jnp.sum(q_sum, 0, keepdims=True), v_bias], axis=1)
        gvec[pl.ds(24 + 2 * c + p, 1)] += bias_row

    for c in range(2):

        def attend_back_step(n, carry):
            if linked and c == 0:
                scatter_tick(14 + n)
            if linked and c == 1:
                pl.when(n < 3)(lambda: scatter_tick(18 + n))
            attend_back(lax.div(n, 2), c, lax.rem(n, 2))
            return carry

        lax.fori_loop(0, images * 2, attend_back_step, 0)

        def heads_grad(j, carry):
            u = 3 * c + j
            put_grad(18 + u, mm(h1[...], pair(act, u), 0, 0))
            return carry

        lax.fori_loop(0, 3, heads_grad, 0)
    scatter_tick(21)
    project(3, 1, [(act, n) for n in range(12)], list(range(16, 22)), odd_tick(22))
    partial_wait(3, 1)
    for i in range(images):

        def norm_one_back(rows, full, c, last):
            grad = summed(1, rows)
            normed, inverse = stats(tok[rows].astype(F32))
            add_rows(0, grad * normed)
            add_rows(1, grad)
            total = mid[rows] + stats_back(grad * gain1, normed, inverse)
            put_tokens(tok_grad, c, i, total.astype(BF16), last)

        token_loop(i, norm_one_back)
        if i == 0:
            scatter_tick(24)

    for n in range(6):
        total = jnp.sum(acc[n], 0, keepdims=True)
        for k in range(4):
            gvec[4 * n + k : 4 * n + k + 1] = total[:, k * UNIT : (k + 1) * UNIT]

    def sum_copy(k, stage, device):
        return remote(vs.at[stage], vr.at[k], vss.at[k], vsr.at[k], device)

    vs[0] = gvec[...]
    over_core = sum_copy(0, 0, core)
    over_core.start()
    scatter_tick(25)
    over_core.wait()
    shared = lax.broadcasted_iota(jnp.int32, (GVEC_ROWS, UNIT), 0) < 24
    gathered = vs[0] + jnp.where(shared, vr[0], 0.0)
    if linked:
        vs[1] = gathered
        for k, devices in enumerate((column, plane)):
            copies = [sum_copy(3 * k + n + 1, k + 1, device) for n, device in enumerate(devices)]
            start(copies)
            scatter_ticks(26 + 2 * k, 28 + 2 * k)
            wait(copies)
            parts = [vr[3 * k + n] for n in (1, 2, 3)]
            vs[k + 2] = vs[k + 1] + parts[0] + parts[1] + parts[2]
        scatter_ticks(30, STEPS)
        gvec[...] = vs[3]
        for n in range(4):
            kinds = [
                gq_units[
                    :,
                    (3 * (n // 2) + k) * UNIT + (n % 2) * SLAB : (3 * (n // 2) + k) * UNIT
                    + (n % 2 + 1) * SLAB,
                ]
                for k in range(3)
            ]
            keys = swap(kinds[1])
            tiles = (
                jnp.where(half_lane, kinds[0], keys),
                jnp.where(half_lane, kinds[2], kinds[0]),
                jnp.where(half_lane, keys, kinds[2]),
            )
            for k, tile in enumerate(tiles):
                gq[:, (3 * n + k) * SLAB : (3 * n + k + 1) * SLAB] = tile
    else:
        gvec[...] = gathered


def output_kernel(result, tok_grad, gq, go, g1, g2, gvec, *refs):
    outs, held, sems = refs[:14], refs[14:20], refs[20]
    sources = (result, tok_grad, gq, go, g1, g2)
    arrive = [
        pltpu.make_async_copy(source, target, sems.at[0, n])
        for n, (source, target) in enumerate(zip(sources, held))
    ]
    leave = [
        pltpu.make_async_copy(source, target, sems.at[1, n])
        for n, (source, target) in enumerate(zip(held, outs[:6]))
    ]
    for copy in arrive:
        copy.start()
    d_idx = lax.axis_index("dp")
    values = gvec[...]
    low = lax.broadcasted_iota(jnp.int32, (8, SLAB), 1) < HD
    rows = [
        jnp.concatenate([values[4 * n + k : 4 * n + k + 1] for k in range(4)], axis=1)
        for n in range(6)
    ]
    wide = jnp.concatenate(rows + [jnp.zeros_like(rows[0])] * 2, axis=0)
    mine = jnp.zeros((8, SLAB), F32)
    for n in range(wide.shape[1] // SLAB):
        tile = wide[:, n * SLAB : (n + 1) * SLAB]
        mine = jnp.where(lax.div(d_idx, 2) == n, tile, mine)
    mine = jnp.where(lax.rem(d_idx, 2) == 1, pltpu.roll(mine, HD, 1), mine)
    for n in range(6):
        outs[6 + n][...] = mine[n : n + 1, : outs[6 + n].shape[1]]
    head_rows = []
    for n in range(4):
        row = values[24 + n : 25 + n]
        q, v = row[:, :SLAB], row[:, SLAB:]
        head_rows.append(jnp.where(low[:1], q, pltpu.roll(v, HD, 1)))
        head_rows.append(jnp.where(low[:1], pltpu.roll(q, HD, 1), v))
    back = SLAB - d_idx * 8
    mine = pltpu.roll(jnp.concatenate(head_rows, axis=0), back, 1)
    outs[12][...] = mine[:, : outs[12].shape[1]]
    hidden_rows = []
    for n in range(8):
        row = values[28 + n : 29 + n]
        hidden_rows += [row[:, :SLAB], row[:, SLAB:]]
    mine = pltpu.roll(jnp.concatenate(hidden_rows, axis=0), back, 1)
    outs[13][...] = jnp.transpose(mine)[: outs[13].shape[0]]
    for n in range(6):
        arrive[n].wait()
        leave[n].start()
    for copy in leave:
        copy.wait()


def own_part(values, index, width):
    return lax.dynamic_slice_in_dim(values, index * width, width, axis=1)


def body(
    linked,
    tokens,
    lengths,
    ln1_gain,
    ln1_bias,
    qkv_weight,
    qv_bias,
    out_weight,
    out_bias,
    ln2_gain,
    ln2_bias,
    fc1_weight,
    fc1_bias,
    fc2_weight,
    fc2_bias,
    cotangent,
):
    images, half, D = tokens.shape
    parts = lax.axis_size("dp")
    dp = lax.axis_index("dp")
    heads = qv_bias.shape[0]
    R = -(-half // 16) * 16
    T = images * 2 * R
    share = D // parts
    tok = jnp.swapaxes(tokens, 0, 1)
    cot = jnp.swapaxes(cotangent, 0, 1)
    norms = (ln1_gain, ln1_bias, out_bias, ln2_gain, ln2_bias, fc2_bias)
    if linked:
        vec = (*[v.reshape(1, share) for v in norms], qv_bias, jnp.transpose(fc1_bias))
        wq = qkv_weight
    else:
        norms = lax.all_gather(jnp.stack(norms), "dp", axis=1, tiled=True).reshape(6, 4, UNIT)
        norms = jnp.pad(jnp.swapaxes(norms, 0, 1), ((0, 0), (0, 2), (0, 0))).reshape(32, UNIT)
        qv = lax.all_gather(qv_bias, "dp", axis=1, tiled=True).reshape(2, 2, 2, 2, HD)
        q_rows = qv[:, :, :, 0].reshape(2, 1, UNIT)
        v_rows = qv[:, :, :, 1].reshape(2, 1, UNIT)
        qkv_rows = jnp.concatenate([q_rows, jnp.zeros_like(q_rows), v_rows], axis=1)
        fc1_rows = lax.all_gather(fc1_bias, "dp", axis=1, tiled=True).reshape(8, UNIT)
        unused = jnp.zeros((VEC_ROWS - 46, UNIT), BF16)
        vec = (jnp.concatenate([norms, qkv_rows.reshape(6, UNIT), fc1_rows, unused]),)
        grouped = qkv_weight.reshape(share, heads // 4, 4, 3, HD)
        wq = jnp.swapaxes(grouped, 2, 3).reshape(share, heads * 3 * HD)
    weights = [wq, out_weight, fc1_weight, fc2_weight]
    if not linked:
        weights = [
            lax.all_gather(w, "dp", axis=0, tiled=True).reshape(
                BLOCKS + (D // 16, w.shape[1])
            )
            for w in weights
        ]
    vmem = pl.BlockSpec(memory_space=pltpu.VMEM)
    hbm = pl.BlockSpec(memory_space=pl.ANY)
    if linked:
        grads = [jax.ShapeDtypeStruct(w.shape, F32) for w in weights]
    else:
        grads = [jax.ShapeDtypeStruct(w.shape, BF16) for w in weights]
    grad_spec = vmem if linked else hbm
    dma = pltpu.SemaphoreType.DMA
    block = BLOCKS + (D // 16, UNIT)
    outs = pl.pallas_call(
        functools.partial(layer_kernel, images, half, R, linked),
        out_shape=[
            jax.ShapeDtypeStruct((half, images, D), BF16),
            jax.ShapeDtypeStruct((half, images, D), BF16),
            *grads,
            jax.ShapeDtypeStruct((GVEC_ROWS, UNIT), F32),
        ],
        in_specs=[
            pl.BlockSpec(memory_space=pltpu.SMEM),
            hbm,
            hbm,
            tuple(vmem for _ in vec),
            vmem if linked else hbm,
            hbm,
            hbm,
            hbm,
        ],
        out_specs=[vmem, vmem, grad_spec, grad_spec, grad_spec, grad_spec, vmem],
        scratch_shapes=[
            pltpu.VMEM((32,) + block, BF16),
            pltpu.VMEM((images * R, D), BF16),
            pltpu.VMEM((D // 16, 6 * UNIT), F32),
            pltpu.VMEM((40, SLAB), F32),
            pltpu.VMEM((T, D), BF16),
            pltpu.VMEM((12, T, SLAB), BF16),
            pltpu.VMEM((4, T, SLAB), BF16),
            pltpu.VMEM((T, D), BF16),
            pltpu.VMEM((16, T, SLAB), BF16),
            pltpu.VMEM((16, T, SLAB), BF16),
            pltpu.VMEM((T, D), BF16),
            pltpu.VMEM((images * R, D), F32),
            pltpu.VMEM((4, images * R, UNIT), F32),
            pltpu.VMEM((4, images * R, UNIT), BF16),
            pltpu.VMEM((2, 4, images * R, UNIT), BF16),
            pltpu.VMEM((T, SLAB), F32),
            pltpu.VMEM((VEC_ROWS, UNIT), F32),
            pltpu.VMEM((6, 8, D), F32),
            pltpu.VMEM((RING, 2, 2, 2, 2, 32, UNIT), BF16),
            pltpu.VMEM((RING, 2, 2, 2, 32, UNIT), BF16),
            pltpu.VMEM((RING, 2, 2, 32, UNIT), BF16),
            pltpu.VMEM((RING, 64, UNIT), BF16),
            pltpu.VMEM((3, VEC_ROWS, UNIT), BF16),
            pltpu.VMEM((2, 3, VEC_ROWS, UNIT), BF16),
            pltpu.VMEM((4, GVEC_ROWS, UNIT), F32),
            pltpu.VMEM((7, GVEC_ROWS, UNIT), F32),
            dma((24,)),
            dma((2,)),
            dma((RING, 8)),
            dma((RING, 8)),
            dma((RING, 8)),
            dma((RING, 8)),
            dma((4, 4)),
            dma((4, 4)),
            dma((4, images)),
            dma((4, images)),
            dma((2, 3)),
            dma((2, 3)),
            dma((7,)),
            dma((7,)),
        ],
        compiler_params=pltpu.CompilerParams(
            collective_id=0, has_side_effects=True, vmem_limit_bytes=64 * 2**20 - 2**16
        ),
        name="layer",
    )(lengths, tok, cot, vec, *weights)
    result, tok_grad, gq, go, g1, g2, gvec = outs
    if linked:
        large = (result, tok_grad, gq, go, g1, g2)
        result, tok_grad, gq, go, g1, g2, *norms_grad, qv_grad, fc1_grad = pl.pallas_call(
            output_kernel,
            out_shape=[
                *[jax.ShapeDtypeStruct(v.shape, v.dtype) for v in large],
                *[jax.ShapeDtypeStruct((1, share), F32)] * 6,
                jax.ShapeDtypeStruct((heads, 2 * HD // parts), F32),
                jax.ShapeDtypeStruct((128 // parts, fc1_bias.shape[0]), F32),
            ],
            in_specs=[hbm] * 6 + [vmem],
            out_specs=[hbm] * 6 + [vmem] * 8,
            scratch_shapes=[*[pltpu.VMEM(v.shape, v.dtype) for v in large], dma((2, 6))],
            name="outputs",
        )(*large, gvec)
        norms_grad = [v.reshape(share) for v in norms_grad]
        fc1_grad = jnp.transpose(fc1_grad)
    else:

        def owned(values):
            flat = values.reshape(D, values.shape[-1]).astype(F32)
            return lax.psum_scatter(flat, "dp", scatter_dimension=0, tiled=True)

        gq, go, g1, g2 = owned(gq), owned(go), owned(g1), owned(g2)
        gq = jnp.swapaxes(gq.reshape(share, heads // 4, 3, 4, HD), 2, 3)
        gq = gq.reshape(share, heads * 3 * HD)
        gvec = lax.psum(gvec, "dp")
        norms_grad = own_part(gvec[:24].reshape(6, D), dp, share)
        qv_grad = jnp.swapaxes(gvec[24:28].reshape(4, 2, 2, HD), 1, 2).reshape(heads, 2 * HD)
        qv_grad = own_part(qv_grad, dp, 2 * HD // parts)
        fc1_grad = own_part(gvec[28:36].reshape(-1, 128), dp, 128 // parts)
    return (
        jnp.swapaxes(result, 0, 1),
        jnp.swapaxes(tok_grad, 0, 1),
        norms_grad[0],
        norms_grad[1],
        gq,
        qv_grad,
        go,
        norms_grad[2],
        norms_grad[3],
        norms_grad[4],
        g1,
        fc1_grad,
        g2,
        norms_grad[5],
    )


def solution(mesh):
    linked = mesh.shape["dp"] == 16
    vector = P("dp")
    weight = P("dp", "tensor")
    bias = P("tensor", "dp")
    tokens = P("dp", "tensor", None)
    in_specs = (
        tokens,
        vector,
        vector,
        vector,
        weight,
        bias,
        weight,
        vector,
        vector,
        vector,
        weight,
        bias,
        weight,
        vector,
        tokens,
    )
    out_specs = (
        tokens,
        tokens,
        vector,
        vector,
        weight,
        bias,
        weight,
        vector,
        vector,
        vector,
        weight,
        bias,
        weight,
        vector,
    )
    return jax.shard_map(
        functools.partial(body, linked),
        mesh=mesh,
        in_specs=in_specs,
        out_specs=out_specs,
        check_vma=False,
    )
```

```python
import functools

import jax
import jax.numpy as jnp
from jax import lax
from jax.experimental import pallas as pl
from jax.experimental.pallas import tpu as pltpu
from jax.sharding import PartitionSpec as P

HD = 64
UNIT = 256
SLAB = 128
LAG = 2
RING = 2 * LAG + 1
STEPS = 24 + 4 * LAG
BLOCKS = (2, 2, 2, 2)
VEC_ROWS = 48
QKV_ROW, FC1_ROW = 32, 38
GVEC_ROWS = 40
F32 = jnp.float32
BF16 = jnp.bfloat16
MESH = pl.DeviceIdType.MESH


def mm(left, right, left_dim, right_dim):
    return lax.dot_general(
        left, right, (((left_dim,), (right_dim,)), ((), ())), preferred_element_type=F32
    )


def when(condition, action):
    if isinstance(condition, bool):
        if condition:
            action()
    else:
        pl.when(condition)(action)


def stats(values):
    center = values - jnp.mean(values, -1, keepdims=True)
    inverse = lax.rsqrt(jnp.mean(center * center, -1, keepdims=True) + 1e-05)
    return center * inverse, inverse


def stats_back(scaled, normed, inverse):
    return inverse * (
        scaled
        - jnp.mean(scaled, -1, keepdims=True)
        - normed * jnp.mean(scaled * normed, -1, keepdims=True)
    )


def three_terms(values):
    first = values.astype(BF16).astype(F32)
    second = (values - first).astype(BF16).astype(F32)
    return first, second, values - first - second


def layer_kernel(
    images,
    half,
    rows_half,
    linked,
    lengths,
    tok_hbm,
    cot_hbm,
    small_in,
    wq_in,
    wo_in,
    w1_in,
    w2_in,
    result,
    tok_grad,
    gq,
    go,
    g1,
    g2,
    gvec,
    buf,
    tok,
    gq_units,
    small,
    h1,
    qkv,
    ctx,
    h2,
    act,
    gp,
    cot,
    mid,
    own,
    snd,
    rcv,
    lse,
    vec,
    acc,
    r1,
    r2,
    r3,
    r4,
    vb,
    vbr,
    vs,
    vr,
    local_sem,
    cot_sem,
    gs,
    gr,
    hs,
    hr,
    xs,
    xr,
    ts,
    tr,
    vgs,
    vgr,
    vss,
    vsr,
):
    R = rows_half
    T = images * 2 * R
    D = tok_hbm.shape[-1]
    tok_in, cot_in = tok_grad, result
    CHUNK = 16
    chunks = R // CHUNK
    rest = half - (chunks - 1) * CHUNK
    d_idx = lax.axis_index("dp")
    t_idx = lax.axis_index("tensor")
    core = {"dp": d_idx, "tensor": 1 - t_idx}
    if linked:
        x = lax.rem(d_idx, 2)
        y = lax.rem(lax.div(d_idx, 2), 2)
        b = lax.rem(lax.div(d_idx, 4), 2)
        a = lax.div(d_idx, 8)

        def chip(aa, bb, yy, xx):
            return {"dp": ((aa * 2 + bb) * 2 + yy) * 2 + xx, "tensor": t_idx}

        xdev = chip(a, b, y, 1 - x)
        ydev = chip(a, b, 1 - y, x)
        bdev = chip(a, 1 - b, y, x)
        adev = chip(1 - a, b, y, x)
        column = [adev, bdev, chip(1 - a, 1 - b, y, x)]
        plane = [xdev, ydev, chip(a, b, 1 - y, 1 - x)]
    else:
        a = b = y = x = 0
        xdev = ydev = bdev = adev = None

    def remote(src, dst, send, recv, device):
        return pltpu.make_async_remote_copy(
            src_ref=src,
            dst_ref=dst,
            send_sem=send,
            recv_sem=recv,
            device_id=device,
            device_id_type=MESH,
        )

    def start(copies):
        for copy in copies:
            copy.start()

    def wait(copies):
        for copy in copies:
            copy.wait()

    barrier = pltpu.get_barrier_semaphore()
    peers = [core] + (column + plane if linked else [])
    for peer in peers:
        pl.semaphore_signal(barrier, inc=1, device_id=peer, device_id_type=MESH)

    def unit_source(s):
        ref, u = (
            (wq_in, s)
            if s < 6
            else (wo_in, s - 6)
            if s < 8
            else (w1_in, s - 8)
            if s < 16
            else (w2_in, s - 16)
        )
        cols = pl.ds(u * UNIT, UNIT)
        return ref.at[:, cols] if linked else ref.at[:, :, :, :, :, cols]

    def place(s):
        return s + 16 - 16 * (s // 8)

    def place_dyn(s):
        return s + 16 - 16 * lax.div(s, 8)

    weight_copies = []
    for s in range(6 if linked else 0, 24):
        target = buf.at[place(s), a, b, y, x] if linked else buf.at[place(s)]
        weight_copies.append(pltpu.make_async_copy(unit_source(s), target, local_sem.at[s]))
    start(weight_copies)
    cot_copy = pltpu.make_async_copy(cot_hbm, cot_in, cot_sem.at[0])
    cot_copy.start()
    tok_copy = pltpu.make_async_copy(tok_hbm, tok_in, cot_sem.at[1])
    tok_copy.start()

    half_lane = lax.broadcasted_iota(jnp.int32, (D // 16, SLAB), 1) < HD

    def swap(values):
        return pltpu.roll(values, HD, 1)

    if linked:
        for n in range(4):
            tiles = [
                wq_in[:, (3 * n + k) * SLAB : (3 * n + k + 1) * SLAB].astype(F32) for k in range(3)
            ]
            kinds = (
                jnp.where(half_lane, tiles[0], tiles[1]),
                jnp.where(half_lane, swap(tiles[0]), swap(tiles[2])),
                jnp.where(half_lane, tiles[1], tiles[2]),
            )
            for k, kind in enumerate(kinds):
                lanes = pl.ds((n % 2) * SLAB, SLAB)
                buf[place(3 * (n // 2) + k), a, b, y, x, :, lanes] = kind.astype(BF16)

    def take_tokens(source, target, rows_of, low, high):
        for c in range(low, high):
            for i in range(images):
                base = rows_of(i) + c * CHUNK
                if c < chunks - 1 or rest == CHUNK:
                    target[base : base + CHUNK] = source[c * CHUNK : (c + 1) * CHUNK, i, :]
                else:
                    target[base : base + CHUNK] = jnp.zeros((CHUNK, D), BF16)
                    target[base : base + rest] = source[c * CHUNK : half, i, :]

    def put_tokens(target, c, i, value, last):
        if last and rest < CHUNK:
            target[half - rest : half, i, :] = value[:rest]
        else:
            target[pl.ds(c * CHUNK, CHUNK), i, :] = value

    pl.semaphore_wait(barrier, len(peers))

    TOP, LOW = pl.ds(0, 32), pl.ds(32, 32)

    def spread(k, s):
        u, slot = place_dyn(s), lax.rem(s, RING)
        if k == 0:
            moves = [(buf.at[u, a, b, y, x], adev)]
        elif k == 1:
            moves = [(buf.at[u, :, b, y, x, TOP], xdev), (buf.at[u, :, b, y, x, LOW], ydev)]
        elif k == 2:
            moves = [(buf.at[u, :, b, y, :, TOP], bdev), (buf.at[u, :, b, :, x, LOW], bdev)]
        else:
            moves = [(buf.at[u, :, :, y, :, TOP], ydev), (buf.at[u, :, :, :, x, LOW], xdev)]
        return [
            remote(ref, ref, gs.at[slot, k], gr.at[slot, k], device) for ref, device in moves
        ]

    def spread_wait(k, s):
        u, slot = place_dyn(s), lax.rem(s, RING)
        ref = (
            buf.at[u, a, b, y, x],
            buf.at[u, :, b, y, x],
            buf.at[u, :, b, y],
            buf.at[u, :, :, y],
        )[k]
        remote(ref, ref, gs.at[slot, k], gr.at[slot, k], adev).wait()

    def gather_tick(s):
        if not linked:
            return
        s = jnp.int32(s)
        for k in (3, 2, 1, 0):
            unit = s - (k + 1) * LAG

            def further(k=k, unit=unit):
                spread_wait(k, unit)
                if k < 3:
                    start(spread(k + 1, unit))

            when((unit >= 0) & (unit < 24), further)
        when(s < 24, lambda: start(spread(0, s)))

    def gather_ticks(low, high):
        if not linked or low >= high:
            return

        def one(s, carry):
            gather_tick(s)
            return carry

        lax.fori_loop(low, high, one, 0)

    def grad_place(r):
        return lax.rem(r + 24, 32)

    def collect(k, r):
        g, slot = grad_place(r), lax.rem(r, RING)
        if k == 0:
            moves = [
                (buf.at[g, :, :, 1 - y, :, TOP], r1.at[slot, 0], ydev),
                (buf.at[g, :, :, :, 1 - x, LOW], r1.at[slot, 1], xdev),
            ]
        elif k == 1:
            moves = [
                (buf.at[g, :, 1 - b, y, :, TOP], r2.at[slot, 0], bdev),
                (buf.at[g, :, 1 - b, :, x, LOW], r2.at[slot, 1], bdev),
            ]
        elif k == 2:
            moves = [
                (buf.at[g, :, b, y, 1 - x, TOP], r3.at[slot, 0], xdev),
                (buf.at[g, :, b, 1 - y, x, LOW], r3.at[slot, 1], ydev),
            ]
        else:
            moves = [(buf.at[g, 1 - a, b, y, x], r4.at[slot], adev)]
        return [
            remote(src, dst, hs.at[slot, k], hr.at[slot, k], device) for src, dst, device in moves
        ]

    def collect_wait(k, r):
        slot = lax.rem(r, RING)
        ref = (r1, r2, r3, r4)[k].at[slot]
        remote(ref, ref, hs.at[slot, k], hr.at[slot, k], adev).wait()

    def add_parts(k, r):
        g, slot = grad_place(r), lax.rem(r, RING)
        if k == 0:
            top, low, parts = (g, slice(None), slice(None), y, slice(None), TOP), (
                (g, slice(None), slice(None), slice(None), x, LOW)
            ), r1
        elif k == 1:
            top, low, parts = (g, slice(None), b, y, slice(None), TOP), (
                (g, slice(None), b, slice(None), x, LOW)
            ), r2
        else:
            top, low, parts = (g, slice(None), b, y, x, TOP), (g, slice(None), b, y, x, LOW), r3
        buf[top] = buf[top] + parts[slot, 0]
        buf[low] = buf[low] + parts[slot, 1]

    def add_last(r):
        g, slot = grad_place(r), lax.rem(r, RING)
        total = buf[g, a, b, y, x].astype(F32) + r4[slot].astype(F32)

        def put(ref, base):
            def store():
                ref[:, pl.ds(pl.multiple_of((r - base) * UNIT, UNIT), UNIT)] = total

            return store

        when(r < 8, put(g2, 0))
        when((r >= 8) & (r < 16), put(g1, 8))
        when((r >= 16) & (r < 18), put(go, 16))
        when(r >= 18, put(gq_units, 18))

    def scatter_tick(s):
        if not linked:
            return
        s = jnp.int32(s)
        for k in (3, 2, 1, 0):
            unit = s - (k + 1) * LAG

            def further(k=k, unit=unit):
                collect_wait(k, unit)
                if k < 3:
                    add_parts(k, unit)
                    start(collect(k + 1, unit))
                else:
                    add_last(unit)

            when((unit >= 0) & (unit < 24), further)
        when((s >= 0) & (s < 24), lambda: start(collect(0, s)))

    def scatter_ticks(low, high):
        if not linked or low >= high:
            return

        def one(s, carry):
            scatter_tick(s)
            return carry

        lax.fori_loop(low, high, one, 0)

    def put_grad(r, value):
        buf[grad_place(r)] = value.astype(BF16).reshape(BLOCKS + (D // 16, UNIT))
        if not linked:

            def put(ref, base):
                def store():
                    cols = pl.ds(pl.multiple_of((r - base) * UNIT, UNIT), UNIT)
                    copy = pltpu.make_async_copy(
                        buf.at[grad_place(r)], ref.at[:, :, :, :, :, cols], local_sem.at[0]
                    )
                    copy.start()
                    copy.wait()

                return store

            when(r < 8, put(g2, 0))
            when((r >= 8) & (r < 16), put(g1, 8))
            when((r >= 16) & (r < 18), put(go, 16))
            when(r >= 18, put(gq, 18))

    def weight(place_idx):
        return buf[place_idx].reshape(D, UNIT)

    def pair(ref, n):
        return jnp.concatenate([ref[2 * n], ref[2 * n + 1]], axis=1)

    def put_pair(ref, n, value):
        ref[2 * n] = value[:, :SLAB]
        ref[2 * n + 1] = value[:, SLAB:]

    def token_exchange(which, ref, i):
        return remote(
            ref.at[pl.ds(i * 2 * R, R)],
            ref.at[pl.ds((i * 2 + 1) * R, R)],
            ts.at[which, i],
            tr.at[which, i],
            core,
        )

    def partial_exchange(which, side, j):
        return remote(snd.at[j], rcv.at[side, j], xs.at[which, j], xr.at[which, j], core)

    def project(which, side, slabs, places, tick=None):
        def one(j, carry):
            left = jnp.concatenate([ref[n] for ref, n in slabs], axis=1)
            jh, jl = lax.div(j, 2), lax.rem(j, 2)
            right = jnp.concatenate(
                [buf[u, jh, jl].reshape(UNIT, UNIT) for u in places], axis=1
            )
            total = mm(left, right, 1, 1)
            for i in range(images):
                own[j, pl.ds(i * R, R)] = total[i * 2 * R : (i * 2 + 1) * R]
                snd[j, pl.ds(i * R, R)] = total[(i * 2 + 1) * R : (i * 2 + 2) * R].astype(BF16)
            partial_exchange(which, side, j).start()
            if tick is not None:
                tick(j)
            return carry

        lax.fori_loop(0, D // UNIT, one, 0)

    def partial_wait(which, side):
        for j in range(D // UNIT):
            partial_exchange(which, side, j).wait()

    def summed(side, rows):
        return jnp.concatenate(
            [own[j, rows] + rcv[side, j, rows].astype(F32) for j in range(D // UNIT)], axis=1
        )

    def token_loop(i, body):
        def step(c, carry):
            r = pl.multiple_of(i * R + c * CHUNK, CHUNK)
            full = pl.multiple_of(i * 2 * R + c * CHUNK, CHUNK)
            body(pl.ds(r, CHUNK), pl.ds(full, CHUNK), c, False)
            return carry

        lax.fori_loop(0, chunks - 1, step, 0, unroll=chunks - 1)
        c = chunks - 1
        body(pl.ds(i * R + c * CHUNK, CHUNK), pl.ds(i * 2 * R + c * CHUNK, CHUNK), c, True)

    def compact(i):
        return i * R

    if linked:
        small[...] = jnp.zeros_like(small)
        for n in range(6):
            small[n : n + 1, : D // 16] = small_in[n][...].astype(F32)
        small[8:16, :8] = small_in[6][...].astype(F32)
        small[32:40, :16] = small_in[7][...].astype(F32)
        small[16:32, :8] = jnp.transpose(small[32:40])[:16, :8]
        vb[0] = jnp.zeros((VEC_ROWS, UNIT), BF16)
        twice = small[:8] + swap(small[:8])
        wide_lane = lax.broadcasted_iota(jnp.int32, (8, D), 1)
        wide = jnp.concatenate([twice] * (D // SLAB), axis=1)
        wide = jnp.where(lax.div(wide_lane, HD) == d_idx, wide, 0.0)
        for k in range(4):
            vb[0, 8 * k : 8 * k + 8] = wide[:, k * UNIT : (k + 1) * UNIT].astype(BF16)
        heads_bias = pltpu.roll(small[8:16], d_idx * 8, 1)
        heads_swap = swap(heads_bias)
        row_low = half_lane[:1]
        for c in range(2):
            q_parts, v_parts = [], []
            for p in range(2):
                n = 4 * c + 2 * p
                q_parts.append(
                    jnp.where(row_low, heads_bias[n : n + 1], heads_swap[n + 1 : n + 2])
                )
                v_parts.append(
                    jnp.where(row_low, heads_swap[n : n + 1], heads_bias[n + 1 : n + 2])
                )
            base = QKV_ROW + 3 * c
            vb[0, base : base + 1] = jnp.concatenate(q_parts, axis=1).astype(BF16)
            vb[0, base + 2 : base + 3] = jnp.concatenate(v_parts, axis=1).astype(BF16)
        hidden_bias = pltpu.roll(small[16:32], d_idx * 8, 1)
        for u in range(8):
            vb[0, FC1_ROW + u : FC1_ROW + u + 1] = jnp.concatenate(
                [hidden_bias[2 * u : 2 * u + 1], hidden_bias[2 * u + 1 : 2 * u + 2]], axis=1
            ).astype(BF16)
        for k, devices in enumerate((column, plane)):
            copies = [
                remote(vb.at[k], vbr.at[k, n], vgs.at[k, n], vgr.at[k, n], device)
                for n, device in enumerate(devices)
            ]
            start(copies)
            if k == 0:
                gather_ticks(0, 3)
                tok_copy.wait()
            else:
                wait(weight_copies)
                gather_ticks(3, 5)
            cuts = (0, chunks // 2, chunks)
            take_tokens(tok_in, tok, compact, cuts[k], cuts[k + 1])
            wait(copies)
            vb[k + 1] = vb[k] + vbr[k, 0] + vbr[k, 1] + vbr[k, 2]
        gather_ticks(5, 8)
        vec[...] = vb[2].astype(F32)
    else:
        wait(weight_copies)
        tok_copy.wait()
        take_tokens(tok_in, tok, compact, 0, chunks)
        vec[...] = small_in[0][...].astype(F32)

    def vector(n):
        return jnp.concatenate([vec[8 * k + n : 8 * k + n + 1] for k in range(4)], axis=1)

    gain1, shift1, out_bias, gain2, shift2, fc2_bias = [vector(n) for n in range(6)]
    gvec[...] = jnp.zeros_like(gvec)
    acc[...] = jnp.zeros_like(acc)
    lse[...] = jnp.zeros_like(lse)

    for i in range(images):

        def norm_one(rows, full, c, last):
            normed, _ = stats(tok[rows].astype(F32))
            h1[full] = (normed * gain1 + shift1).astype(BF16)

        token_loop(i, norm_one)
        token_exchange(0, h1, i).start()
        gather_tick(8 + i)
    cot_copy.wait()
    take_tokens(cot_in, cot, lambda i: i * 2 * R, 0, chunks)
    for i in range(images):
        token_exchange(1, cot, i).start()
    gather_ticks(8 + images, 3 + 4 * LAG)
    for i in range(images):
        token_exchange(0, h1, i).wait()
        token_exchange(1, cot, i).wait()

    lane = lax.broadcasted_iota(jnp.int32, (2 * R, SLAB), 1)
    row = lax.broadcasted_iota(jnp.int32, (2 * R, SLAB), 0)
    second_half = row >= R
    inside = jnp.where(second_half, row - R, row)
    position = inside + jnp.where(second_half, (1 - t_idx) * half, t_idx * half)
    low_lanes = lane[:R] < HD

    def head_lanes(e, lanes):
        return lanes < HD if e == 0 else lanes >= HD

    def extra(e):
        return HD * (1 - e)

    def key_bias(i):
        valid = (inside < half) & (position < lengths[i])
        return jnp.where(valid, 0.0, -1e30)

    def project_heads(c):
        def one(j, carry):
            u = 3 * c + j
            value = mm(h1[...], weight(16 + u), 1, 0) + vec[pl.ds(QKV_ROW + u, 1)]
            put_pair(qkv, u, value.astype(BF16))
            return carry

        lax.fori_loop(0, 3, one, 0)

    def attend(i, c, p):
        rows = pl.ds(pl.multiple_of(i * 2 * R, 16), 2 * R)
        q = qkv[c * 6 + p, rows].astype(F32) * HD**-0.5
        k = qkv[c * 6 + 2 + p, rows].astype(F32)
        v = qkv[c * 6 + 4 + p, rows]
        bias = key_bias(i)
        heads = []
        for e in range(2):
            inhead = head_lanes(e, lane)
            first_extra = lane == extra(e)
            qm = jnp.where(inhead, q, jnp.where(first_extra, 1.0, 0.0)).astype(BF16)
            km = jnp.where(inhead, k, jnp.where(first_extra, bias, 0.0)).astype(BF16)
            heads.append((qm, km))
        for m in range(2):
            outs, sums = [], []
            for e in range(2):
                qm, km = heads[e]
                scores = mm(qm[m * R : (m + 1) * R], km, 1, 1)
                peak = jnp.max(scores, -1, keepdims=True)
                exps = jnp.exp(scores - peak)
                total = jnp.sum(exps, -1, keepdims=True)
                outs.append(mm(exps.astype(BF16), v, 1, 0) * (1.0 / total))
                sums.append(peak + jnp.log(total))
            tile = pl.ds(pl.multiple_of(i * 2 * R + m * R, 16), R)
            ctx[2 * c + p, tile] = jnp.where(low_lanes, outs[0], outs[1]).astype(BF16)
            column = lane[:R]
            head = (2 * c + p) * 2
            lse[tile] = jnp.where(
                column == head, sums[0], jnp.where(column == head + 1, sums[1], lse[tile])
            )

    for c in range(2):
        project_heads(c)

        def attend_step(n, carry):
            if linked:
                pl.when(n < 3)(lambda: gather_tick(3 + 4 * LAG + 3 * c + n))
            attend(lax.div(n, 2), c, lax.rem(n, 2))
            return carry

        lax.fori_loop(0, images * 2, attend_step, 0)

    project(0, 0, [(ctx, n) for n in range(4)], [22, 23])
    gather_ticks(9 + 4 * LAG, 11 + 4 * LAG)
    partial_wait(0, 0)
    for i in range(images):

        def norm_two(rows, full, c, last):
            middle = tok[rows].astype(F32) + summed(0, rows) + out_bias
            mid[rows] = middle
            normed, _ = stats(middle)
            h2[full] = (normed * gain2 + shift2).astype(BF16)

        token_loop(i, norm_two)
        token_exchange(2, h2, i).start()
        if i == 0:
            gather_tick(11 + 4 * LAG)
    gather_tick(12 + 4 * LAG)
    for i in range(images):
        token_exchange(2, h2, i).wait()

    def hidden(u, carry):
        if linked:
            pl.when(lax.rem(u, 2) == 0)(lambda: gather_tick(13 + 4 * LAG + lax.div(u, 2)))
        pre = mm(h2[...], weight(8 + u), 1, 0) + vec[pl.ds(FC1_ROW + u, 1)]
        sig = 0.5 * jnp.tanh(0.851 * pre) + 0.5
        active = pre * sig
        slope = sig + 1.702 * active * (1.0 - sig)
        put_pair(act, u, active.astype(BF16))
        put_pair(gp, u, slope.astype(BF16))
        return carry

    lax.fori_loop(0, 8, hidden, 0)

    def hidden_back(u, carry):
        put_grad(u, mm(cot[...], pair(act, u), 0, 0))
        gather_tick(17 + 4 * LAG + u)
        pre_grad = mm(cot[...], weight(u), 1, 0) * pair(gp, u).astype(F32)
        gvec[pl.ds(28 + u, 1)] = jnp.sum(pre_grad, 0, keepdims=True)
        put_pair(gp, u, pre_grad.astype(BF16))
        if linked:
            pl.when(u >= 3)(lambda: scatter_tick(u - 3))
        return carry

    lax.fori_loop(0, 8, hidden_back, 0)

    def odd_tick(base):
        if not linked:
            return None

        def tick(j):
            pl.when(lax.rem(j, 2) == 1)(lambda: scatter_tick(base + lax.div(j, 2)))

        return tick

    project(1, 1, [(act, n) for n in range(16)], list(range(8)), odd_tick(5))

    def first_grad(u, carry):
        put_grad(8 + u, mm(h2[...], pair(gp, u), 0, 0))
        return carry

    lax.fori_loop(0, 4, first_grad, 0)
    scatter_tick(7)
    partial_wait(1, 1)
    for i in range(images):

        def finish(rows, full, c, last):
            total = mid[rows] + summed(1, rows) + fc2_bias
            put_tokens(result, c, i, total.astype(BF16), last)

        token_loop(i, finish)
    scatter_tick(8)
    project(2, 0, [(gp, n) for n in range(16)], list(range(8, 16)), odd_tick(9))
    lax.fori_loop(4, 6, first_grad, 0)
    partial_wait(2, 0)

    def add_rows(n, value):
        acc[n] += value[:8] + value[8:]

    for i in range(images):

        def norm_two_back(rows, full, c, last):
            grad = summed(0, rows)
            normed, inverse = stats(mid[rows])
            cots = cot[full].astype(F32)
            middle_grad = cots + stats_back(grad * gain2, normed, inverse)
            add_rows(2, middle_grad)
            add_rows(3, grad * normed)
            add_rows(4, grad)
            add_rows(5, cots)
            mid[rows] = middle_grad
            cot[full] = middle_grad.astype(BF16)

        token_loop(i, norm_two_back)
        token_exchange(3, cot, i).start()
        if i == 0:
            scatter_tick(11)
    scatter_tick(12)
    lax.fori_loop(6, 8, first_grad, 0)
    for i in range(images):
        token_exchange(3, cot, i).wait()

    def out_back(u, carry):
        put_grad(16 + u, mm(cot[...], pair(ctx, u), 0, 0))
        return carry

    lax.fori_loop(0, 2, out_back, 0)
    scatter_tick(13)

    def context_back(u, carry):
        value = mm(cot[...], weight(22 + u), 1, 0)
        put_pair(act, 6 + u, value.astype(BF16))
        return carry

    lax.fori_loop(0, 2, context_back, 0)

    def attend_back(i, c, p):
        rows = pl.ds(pl.multiple_of(i * 2 * R, 16), 2 * R)
        q = qkv[c * 6 + p, rows].astype(F32) * HD**-0.5
        k = qkv[c * 6 + 2 + p, rows]
        v = qkv[c * 6 + 4 + p, rows]
        up = act[12 + 2 * c + p, rows]
        inner_all = up.astype(F32) * ctx[2 * c + p, rows].astype(F32)
        sums_all = lse[rows]
        bias = key_bias(i)
        q_low = q.astype(BF16)
        q_grads, k_grads, v_grads = [], [], []
        for e in range(2):
            inhead = head_lanes(e, lane)
            at = [lane == extra(e) + n for n in range(4)]
            head = (2 * c + p) * 2 + e
            total = jnp.sum(jnp.where(lane == head, sums_all, 0.0), -1, keepdims=True)
            inner = jnp.sum(jnp.where(inhead, inner_all, 0.0), -1, keepdims=True)
            s1, s2, s3 = three_terms(-total)
            n1, n2, n3 = three_terms(-inner)
            ones = at[1] | at[2] | at[3]
            qa = jnp.where(
                inhead,
                q,
                jnp.where(
                    at[0],
                    1.0,
                    jnp.where(at[1], s1, jnp.where(at[2], s2, jnp.where(at[3], s3, 0.0))),
                ),
            ).astype(BF16)
            ka = jnp.where(
                inhead, k.astype(F32), jnp.where(at[0], bias, jnp.where(ones, 1.0, 0.0))
            ).astype(BF16)
            ua = jnp.where(
                inhead,
                up.astype(F32),
                jnp.where(at[1], n1, jnp.where(at[2], n2, jnp.where(at[3], n3, 0.0))),
            ).astype(BF16)
            va = jnp.where(inhead, v.astype(F32), jnp.where(ones, 1.0, 0.0)).astype(BF16)
            q_grad = None
            k_parts, v_parts = [], []
            for m in range(2):
                tile = slice(m * R, (m + 1) * R)
                probs = jnp.exp(mm(ka[tile], qa, 1, 1))
                grads = (probs * mm(va[tile], ua, 1, 1)).astype(BF16)
                v_parts.append(mm(probs.astype(BF16), up, 1, 0))
                k_parts.append(mm(grads, q_low, 1, 0))
                part = mm(grads, k[tile], 0, 0)
                q_grad = part if q_grad is None else q_grad + part
            q_grads.append(q_grad * HD**-0.5)
            k_grads.append(k_parts)
            v_grads.append(v_parts)
        low = lane < HD
        q_sum = jnp.where(low, q_grads[0], q_grads[1])
        act[c * 6 + p, rows] = q_sum.astype(BF16)
        v_bias = None
        for m in range(2):
            tile = pl.ds(pl.multiple_of(i * 2 * R + m * R, 16), R)
            k_sum = jnp.where(low_lanes, k_grads[0][m], k_grads[1][m])
            v_sum = jnp.where(low_lanes, v_grads[0][m], v_grads[1][m])
            act[c * 6 + 2 + p, tile] = k_sum.astype(BF16)
            act[c * 6 + 4 + p, tile] = v_sum.astype(BF16)
            part = jnp.sum(v_sum, 0, keepdims=True)
            v_bias = part if v_bias is None else v_bias + part
        bias_row = jnp.concatenate([jnp.sum(q_sum, 0, keepdims=True), v_bias], axis=1)
        gvec[pl.ds(24 + 2 * c + p, 1)] += bias_row

    for c in range(2):

        def attend_back_step(n, carry):
            if linked and c == 0:
                scatter_tick(14 + n)
            if linked and c == 1:
                pl.when(n < 3)(lambda: scatter_tick(18 + n))
            attend_back(lax.div(n, 2), c, lax.rem(n, 2))
            return carry

        lax.fori_loop(0, images * 2, attend_back_step, 0)

        def heads_grad(j, carry):
            u = 3 * c + j
            put_grad(18 + u, mm(h1[...], pair(act, u), 0, 0))
            return carry

        lax.fori_loop(0, 3, heads_grad, 0)
    scatter_tick(21)
    project(3, 1, [(act, n) for n in range(12)], list(range(16, 22)), odd_tick(22))
    partial_wait(3, 1)
    for i in range(images):

        def norm_one_back(rows, full, c, last):
            grad = summed(1, rows)
            normed, inverse = stats(tok[rows].astype(F32))
            add_rows(0, grad * normed)
            add_rows(1, grad)
            total = mid[rows] + stats_back(grad * gain1, normed, inverse)
            put_tokens(tok_grad, c, i, total.astype(BF16), last)

        token_loop(i, norm_one_back)
        if i == 0:
            scatter_tick(24)

    for n in range(6):
        total = jnp.sum(acc[n], 0, keepdims=True)
        for k in range(4):
            gvec[4 * n + k : 4 * n + k + 1] = total[:, k * UNIT : (k + 1) * UNIT]

    def sum_copy(k, stage, device):
        return remote(vs.at[stage], vr.at[k], vss.at[k], vsr.at[k], device)

    vs[0] = gvec[...]
    over_core = sum_copy(0, 0, core)
    over_core.start()
    scatter_tick(25)
    over_core.wait()
    shared = lax.broadcasted_iota(jnp.int32, (GVEC_ROWS, UNIT), 0) < 24
    gathered = vs[0] + jnp.where(shared, vr[0], 0.0)
    if linked:
        vs[1] = gathered
        for k, devices in enumerate((column, plane)):
            copies = [sum_copy(3 * k + n + 1, k + 1, device) for n, device in enumerate(devices)]
            start(copies)
            scatter_ticks(26 + 2 * k, 28 + 2 * k)
            wait(copies)
            parts = [vr[3 * k + n] for n in (1, 2, 3)]
            vs[k + 2] = vs[k + 1] + parts[0] + parts[1] + parts[2]
        scatter_ticks(30, STEPS)
        gvec[...] = vs[3]
        for n in range(4):
            kinds = [
                gq_units[
                    :,
                    (3 * (n // 2) + k) * UNIT + (n % 2) * SLAB : (3 * (n // 2) + k) * UNIT
                    + (n % 2 + 1) * SLAB,
                ]
                for k in range(3)
            ]
            keys = swap(kinds[1])
            tiles = (
                jnp.where(half_lane, kinds[0], keys),
                jnp.where(half_lane, kinds[2], kinds[0]),
                jnp.where(half_lane, keys, kinds[2]),
            )
            for k, tile in enumerate(tiles):
                gq[:, (3 * n + k) * SLAB : (3 * n + k + 1) * SLAB] = tile
    else:
        gvec[...] = gathered


def output_kernel(result, tok_grad, gq, go, g1, g2, gvec, *refs):
    outs, held, sems = refs[:14], refs[14:20], refs[20]
    sources = (result, tok_grad, gq, go, g1, g2)
    arrive = [
        pltpu.make_async_copy(source, target, sems.at[0, n])
        for n, (source, target) in enumerate(zip(sources, held))
    ]
    leave = [
        pltpu.make_async_copy(source, target, sems.at[1, n])
        for n, (source, target) in enumerate(zip(held, outs[:6]))
    ]
    for copy in arrive:
        copy.start()
    d_idx = lax.axis_index("dp")
    values = gvec[...]
    low = lax.broadcasted_iota(jnp.int32, (8, SLAB), 1) < HD
    rows = [
        jnp.concatenate([values[4 * n + k : 4 * n + k + 1] for k in range(4)], axis=1)
        for n in range(6)
    ]
    wide = jnp.concatenate(rows + [jnp.zeros_like(rows[0])] * 2, axis=0)
    mine = jnp.zeros((8, SLAB), F32)
    for n in range(wide.shape[1] // SLAB):
        tile = wide[:, n * SLAB : (n + 1) * SLAB]
        mine = jnp.where(lax.div(d_idx, 2) == n, tile, mine)
    mine = jnp.where(lax.rem(d_idx, 2) == 1, pltpu.roll(mine, HD, 1), mine)
    for n in range(6):
        outs[6 + n][...] = mine[n : n + 1, : outs[6 + n].shape[1]]
    head_rows = []
    for n in range(4):
        row = values[24 + n : 25 + n]
        q, v = row[:, :SLAB], row[:, SLAB:]
        head_rows.append(jnp.where(low[:1], q, pltpu.roll(v, HD, 1)))
        head_rows.append(jnp.where(low[:1], pltpu.roll(q, HD, 1), v))
    back = SLAB - d_idx * 8
    mine = pltpu.roll(jnp.concatenate(head_rows, axis=0), back, 1)
    outs[12][...] = mine[:, : outs[12].shape[1]]
    hidden_rows = []
    for n in range(8):
        row = values[28 + n : 29 + n]
        hidden_rows += [row[:, :SLAB], row[:, SLAB:]]
    mine = pltpu.roll(jnp.concatenate(hidden_rows, axis=0), back, 1)
    outs[13][...] = jnp.transpose(mine)[: outs[13].shape[0]]
    for n in range(6):
        arrive[n].wait()
        leave[n].start()
    for copy in leave:
        copy.wait()


def own_part(values, index, width):
    return lax.dynamic_slice_in_dim(values, index * width, width, axis=1)


def body(
    linked,
    tokens,
    lengths,
    ln1_gain,
    ln1_bias,
    qkv_weight,
    qv_bias,
    out_weight,
    out_bias,
    ln2_gain,
    ln2_bias,
    fc1_weight,
    fc1_bias,
    fc2_weight,
    fc2_bias,
    cotangent,
):
    images, half, D = tokens.shape
    parts = lax.axis_size("dp")
    dp = lax.axis_index("dp")
    heads = qv_bias.shape[0]
    R = -(-half // 16) * 16
    T = images * 2 * R
    share = D // parts
    tok = jnp.swapaxes(tokens, 0, 1)
    cot = jnp.swapaxes(cotangent, 0, 1)
    norms = (ln1_gain, ln1_bias, out_bias, ln2_gain, ln2_bias, fc2_bias)
    if linked:
        vec = (*[v.reshape(1, share) for v in norms], qv_bias, jnp.transpose(fc1_bias))
        wq = qkv_weight
    else:
        norms = lax.all_gather(jnp.stack(norms), "dp", axis=1, tiled=True).reshape(6, 4, UNIT)
        norms = jnp.pad(jnp.swapaxes(norms, 0, 1), ((0, 0), (0, 2), (0, 0))).reshape(32, UNIT)
        qv = lax.all_gather(qv_bias, "dp", axis=1, tiled=True).reshape(2, 2, 2, 2, HD)
        q_rows = qv[:, :, :, 0].reshape(2, 1, UNIT)
        v_rows = qv[:, :, :, 1].reshape(2, 1, UNIT)
        qkv_rows = jnp.concatenate([q_rows, jnp.zeros_like(q_rows), v_rows], axis=1)
        fc1_rows = lax.all_gather(fc1_bias, "dp", axis=1, tiled=True).reshape(8, UNIT)
        unused = jnp.zeros((VEC_ROWS - 46, UNIT), BF16)
        vec = (jnp.concatenate([norms, qkv_rows.reshape(6, UNIT), fc1_rows, unused]),)
        grouped = qkv_weight.reshape(share, heads // 4, 4, 3, HD)
        wq = jnp.swapaxes(grouped, 2, 3).reshape(share, heads * 3 * HD)
    weights = [wq, out_weight, fc1_weight, fc2_weight]
    if not linked:
        weights = [
            lax.all_gather(w, "dp", axis=0, tiled=True).reshape(
                BLOCKS + (D // 16, w.shape[1])
            )
            for w in weights
        ]
    vmem = pl.BlockSpec(memory_space=pltpu.VMEM)
    hbm = pl.BlockSpec(memory_space=pl.ANY)
    if linked:
        grads = [jax.ShapeDtypeStruct(w.shape, F32) for w in weights]
    else:
        grads = [jax.ShapeDtypeStruct(w.shape, BF16) for w in weights]
    grad_spec = vmem if linked else hbm
    dma = pltpu.SemaphoreType.DMA
    block = BLOCKS + (D // 16, UNIT)
    outs = pl.pallas_call(
        functools.partial(layer_kernel, images, half, R, linked),
        out_shape=[
            jax.ShapeDtypeStruct((half, images, D), BF16),
            jax.ShapeDtypeStruct((half, images, D), BF16),
            *grads,
            jax.ShapeDtypeStruct((GVEC_ROWS, UNIT), F32),
        ],
        in_specs=[
            pl.BlockSpec(memory_space=pltpu.SMEM),
            hbm,
            hbm,
            tuple(vmem for _ in vec),
            vmem if linked else hbm,
            hbm,
            hbm,
            hbm,
        ],
        out_specs=[vmem, vmem, grad_spec, grad_spec, grad_spec, grad_spec, vmem],
        scratch_shapes=[
            pltpu.VMEM((32,) + block, BF16),
            pltpu.VMEM((images * R, D), BF16),
            pltpu.VMEM((D // 16, 6 * UNIT), F32),
            pltpu.VMEM((40, SLAB), F32),
            pltpu.VMEM((T, D), BF16),
            pltpu.VMEM((12, T, SLAB), BF16),
            pltpu.VMEM((4, T, SLAB), BF16),
            pltpu.VMEM((T, D), BF16),
            pltpu.VMEM((16, T, SLAB), BF16),
            pltpu.VMEM((16, T, SLAB), BF16),
            pltpu.VMEM((T, D), BF16),
            pltpu.VMEM((images * R, D), F32),
            pltpu.VMEM((4, images * R, UNIT), F32),
            pltpu.VMEM((4, images * R, UNIT), BF16),
            pltpu.VMEM((2, 4, images * R, UNIT), BF16),
            pltpu.VMEM((T, SLAB), F32),
            pltpu.VMEM((VEC_ROWS, UNIT), F32),
            pltpu.VMEM((6, 8, D), F32),
            pltpu.VMEM((RING, 2, 2, 2, 2, 32, UNIT), BF16),
            pltpu.VMEM((RING, 2, 2, 2, 32, UNIT), BF16),
            pltpu.VMEM((RING, 2, 2, 32, UNIT), BF16),
            pltpu.VMEM((RING, 64, UNIT), BF16),
            pltpu.VMEM((3, VEC_ROWS, UNIT), BF16),
            pltpu.VMEM((2, 3, VEC_ROWS, UNIT), BF16),
            pltpu.VMEM((4, GVEC_ROWS, UNIT), F32),
            pltpu.VMEM((7, GVEC_ROWS, UNIT), F32),
            dma((24,)),
            dma((2,)),
            dma((RING, 4)),
            dma((RING, 4)),
            dma((RING, 4)),
            dma((RING, 4)),
            dma((4, 4)),
            dma((4, 4)),
            dma((4, images)),
            dma((4, images)),
            dma((2, 3)),
            dma((2, 3)),
            dma((7,)),
            dma((7,)),
        ],
        compiler_params=pltpu.CompilerParams(
            collective_id=0, has_side_effects=True, vmem_limit_bytes=64 * 2**20 - 2**16
        ),
        name="layer",
    )(lengths, tok, cot, vec, *weights)
    result, tok_grad, gq, go, g1, g2, gvec = outs
    if linked:
        large = (result, tok_grad, gq, go, g1, g2)
        result, tok_grad, gq, go, g1, g2, *norms_grad, qv_grad, fc1_grad = pl.pallas_call(
            output_kernel,
            out_shape=[
                *[jax.ShapeDtypeStruct(v.shape, v.dtype) for v in large],
                *[jax.ShapeDtypeStruct((1, share), F32)] * 6,
                jax.ShapeDtypeStruct((heads, 2 * HD // parts), F32),
                jax.ShapeDtypeStruct((128 // parts, fc1_bias.shape[0]), F32),
            ],
            in_specs=[hbm] * 6 + [vmem],
            out_specs=[hbm] * 6 + [vmem] * 8,
            scratch_shapes=[*[pltpu.VMEM(v.shape, v.dtype) for v in large], dma((2, 6))],
            name="outputs",
        )(*large, gvec)
        norms_grad = [v.reshape(share) for v in norms_grad]
        fc1_grad = jnp.transpose(fc1_grad)
    else:

        def owned(values):
            flat = values.reshape(D, values.shape[-1]).astype(F32)
            return lax.psum_scatter(flat, "dp", scatter_dimension=0, tiled=True)

        gq, go, g1, g2 = owned(gq), owned(go), owned(g1), owned(g2)
        gq = jnp.swapaxes(gq.reshape(share, heads // 4, 3, 4, HD), 2, 3)
        gq = gq.reshape(share, heads * 3 * HD)
        gvec = lax.psum(gvec, "dp")
        norms_grad = own_part(gvec[:24].reshape(6, D), dp, share)
        qv_grad = jnp.swapaxes(gvec[24:28].reshape(4, 2, 2, HD), 1, 2).reshape(heads, 2 * HD)
        qv_grad = own_part(qv_grad, dp, 2 * HD // parts)
        fc1_grad = own_part(gvec[28:36].reshape(-1, 128), dp, 128 // parts)
    return (
        jnp.swapaxes(result, 0, 1),
        jnp.swapaxes(tok_grad, 0, 1),
        norms_grad[0],
        norms_grad[1],
        gq,
        qv_grad,
        go,
        norms_grad[2],
        norms_grad[3],
        norms_grad[4],
        g1,
        fc1_grad,
        g2,
        norms_grad[5],
    )


def solution(mesh):
    linked = mesh.shape["dp"] == 16
    vector = P("dp")
    weight = P("dp", "tensor")
    bias = P("tensor", "dp")
    tokens = P("dp", "tensor", None)
    in_specs = (
        tokens,
        vector,
        vector,
        vector,
        weight,
        bias,
        weight,
        vector,
        vector,
        vector,
        weight,
        bias,
        weight,
        vector,
        tokens,
    )
    out_specs = (
        tokens,
        tokens,
        vector,
        vector,
        weight,
        bias,
        weight,
        vector,
        vector,
        vector,
        weight,
        bias,
        weight,
        vector,
    )
    return jax.shard_map(
        functools.partial(body, linked),
        mesh=mesh,
        in_specs=in_specs,
        out_specs=out_specs,
        check_vma=False,
    )
```

```python
import functools

import jax
import jax.numpy as jnp
from jax import lax
from jax.experimental import pallas as pl
from jax.experimental.pallas import tpu as pltpu
from jax.sharding import PartitionSpec as P

HD = 64
UNIT = 256
SLAB = 128
LAG = 2
RING = 2 * LAG + 1
STEPS = 24 + 4 * LAG
BLOCKS = (2, 2, 2, 2)
VEC_ROWS = 48
QKV_ROW, FC1_ROW = 32, 38
GVEC_ROWS = 40
F32 = jnp.float32
BF16 = jnp.bfloat16
MESH = pl.DeviceIdType.MESH


def mm(left, right, left_dim, right_dim):
    return lax.dot_general(
        left, right, (((left_dim,), (right_dim,)), ((), ())), preferred_element_type=F32
    )


def when(condition, action):
    if isinstance(condition, bool):
        if condition:
            action()
    else:
        pl.when(condition)(action)


def stats(values):
    center = values - jnp.mean(values, -1, keepdims=True)
    inverse = lax.rsqrt(jnp.mean(center * center, -1, keepdims=True) + 1e-05)
    return center * inverse, inverse


def stats_back(scaled, normed, inverse):
    return inverse * (
        scaled
        - jnp.mean(scaled, -1, keepdims=True)
        - normed * jnp.mean(scaled * normed, -1, keepdims=True)
    )


def three_terms(values):
    first = values.astype(BF16).astype(F32)
    second = (values - first).astype(BF16).astype(F32)
    return first, second, values - first - second


def layer_kernel(
    images,
    half,
    rows_half,
    linked,
    lengths,
    tok_hbm,
    cot_hbm,
    small_in,
    wq_in,
    wo_in,
    w1_in,
    w2_in,
    result,
    tok_grad,
    gq,
    go,
    g1,
    g2,
    gvec,
    buf,
    tok,
    gq_units,
    small,
    h1,
    qkv,
    ctx,
    h2,
    act,
    gp,
    cot,
    mid,
    own,
    snd,
    rcv,
    lse,
    vec,
    acc,
    r1,
    r2,
    r3,
    r4,
    vb,
    vbr,
    vs,
    vr,
    local_sem,
    cot_sem,
    gs,
    gr,
    hs,
    hr,
    xs,
    xr,
    ts,
    tr,
    vgs,
    vgr,
    vss,
    vsr,
):
    R = rows_half
    T = images * 2 * R
    D = tok_hbm.shape[-1]
    tok_in, cot_in = tok_grad, result
    CHUNK = 16
    chunks = R // CHUNK
    rest = half - (chunks - 1) * CHUNK
    d_idx = lax.axis_index("dp")
    t_idx = lax.axis_index("tensor")
    core = {"dp": d_idx, "tensor": 1 - t_idx}
    if linked:
        x = lax.rem(d_idx, 2)
        y = lax.rem(lax.div(d_idx, 2), 2)
        b = lax.rem(lax.div(d_idx, 4), 2)
        a = lax.div(d_idx, 8)

        def chip(aa, bb, yy, xx):
            return {"dp": ((aa * 2 + bb) * 2 + yy) * 2 + xx, "tensor": t_idx}

        xdev = chip(a, b, y, 1 - x)
        ydev = chip(a, b, 1 - y, x)
        bdev = chip(a, 1 - b, y, x)
        adev = chip(1 - a, b, y, x)
        column = [adev, bdev, chip(1 - a, 1 - b, y, x)]
        plane = [xdev, ydev, chip(a, b, 1 - y, 1 - x)]
    else:
        a = b = y = x = 0
        xdev = ydev = bdev = adev = None

    def remote(src, dst, send, recv, device):
        return pltpu.make_async_remote_copy(
            src_ref=src,
            dst_ref=dst,
            send_sem=send,
            recv_sem=recv,
            device_id=device,
            device_id_type=MESH,
        )

    def start(copies):
        for copy in copies:
            copy.start()

    def wait(copies):
        for copy in copies:
            copy.wait()

    barrier = pltpu.get_barrier_semaphore()
    peers = [core] + (column + plane if linked else [])
    for peer in peers:
        pl.semaphore_signal(barrier, inc=1, device_id=peer, device_id_type=MESH)

    def unit_source(s):
        ref, u = (
            (wq_in, s)
            if s < 6
            else (wo_in, s - 6)
            if s < 8
            else (w1_in, s - 8)
            if s < 16
            else (w2_in, s - 16)
        )
        cols = pl.ds(u * UNIT, UNIT)
        return ref.at[:, cols] if linked else ref.at[:, :, :, :, :, cols]

    def place(s):
        return s + 16 - 16 * (s // 8)

    def place_dyn(s):
        return s + 16 - 16 * lax.div(s, 8)

    weight_copies = []
    for s in range(6 if linked else 0, 24):
        target = buf.at[place(s), a, b, y, x] if linked else buf.at[place(s)]
        weight_copies.append(pltpu.make_async_copy(unit_source(s), target, local_sem.at[s]))
    start(weight_copies)
    cot_copy = pltpu.make_async_copy(cot_hbm, cot_in, cot_sem.at[0])
    cot_copy.start()
    tok_copy = pltpu.make_async_copy(tok_hbm, tok_in, cot_sem.at[1])
    tok_copy.start()

    half_lane = lax.broadcasted_iota(jnp.int32, (D // 16, SLAB), 1) < HD

    def swap(values):
        return pltpu.roll(values, HD, 1)

    if linked:
        for n in range(4):
            tiles = [
                wq_in[:, (3 * n + k) * SLAB : (3 * n + k + 1) * SLAB].astype(F32) for k in range(3)
            ]
            kinds = (
                jnp.where(half_lane, tiles[0], tiles[1]),
                jnp.where(half_lane, swap(tiles[0]), swap(tiles[2])),
                jnp.where(half_lane, tiles[1], tiles[2]),
            )
            for k, kind in enumerate(kinds):
                lanes = pl.ds((n % 2) * SLAB, SLAB)
                buf[place(3 * (n // 2) + k), a, b, y, x, :, lanes] = kind.astype(BF16)

    def take_tokens(source, target, rows_of, low, high):
        for c in range(low, high):
            for i in range(images):
                base = rows_of(i) + c * CHUNK
                if c < chunks - 1 or rest == CHUNK:
                    target[base : base + CHUNK] = source[c * CHUNK : (c + 1) * CHUNK, i, :]
                else:
                    target[base : base + CHUNK] = jnp.zeros((CHUNK, D), BF16)
                    target[base : base + rest] = source[c * CHUNK : half, i, :]

    def put_tokens(target, c, i, value, last):
        if last and rest < CHUNK:
            target[half - rest : half, i, :] = value[:rest]
        else:
            target[pl.ds(c * CHUNK, CHUNK), i, :] = value

    pl.semaphore_wait(barrier, len(peers))

    TOP, LOW = pl.ds(0, 32), pl.ds(32, 32)

    def spread(k, s):
        u, slot = place_dyn(s), lax.rem(s, RING)
        if k == 0:
            moves = [(buf.at[u, a, b, y, x], adev)]
        elif k == 1:
            moves = [(buf.at[u, :, b, y, x, TOP], xdev), (buf.at[u, :, b, y, x, LOW], ydev)]
        elif k == 2:
            moves = [(buf.at[u, :, b, y, :, TOP], bdev), (buf.at[u, :, b, :, x, LOW], bdev)]
        else:
            moves = [(buf.at[u, :, :, y, :, TOP], ydev), (buf.at[u, :, :, :, x, LOW], xdev)]
        return [
            remote(ref, ref, gs.at[slot, k], gr.at[slot, k], device) for ref, device in moves
        ]

    def spread_wait(k, s):
        u, slot = place_dyn(s), lax.rem(s, RING)
        ref = (
            buf.at[u, a, b, y, x],
            buf.at[u, :, b, y, x],
            buf.at[u, :, b, y],
            buf.at[u, :, :, y],
        )[k]
        remote(ref, ref, gs.at[slot, k], gr.at[slot, k], adev).wait()

    def gather_tick(s):
        if not linked:
            return
        s = jnp.int32(s)
        for k in (3, 2, 1, 0):
            unit = s - (k + 1) * LAG

            def further(k=k, unit=unit):
                spread_wait(k, unit)
                if k < 3:
                    start(spread(k + 1, unit))

            when((unit >= 0) & (unit < 24), further)
        when(s < 24, lambda: start(spread(0, s)))

    def gather_ticks(low, high):
        if not linked or low >= high:
            return

        def one(s, carry):
            gather_tick(s)
            return carry

        lax.fori_loop(low, high, one, 0)

    def grad_place(r):
        return lax.rem(r + 24, 32)

    def collect(k, r):
        g, slot = grad_place(r), lax.rem(r, RING)
        if k == 0:
            moves = [
                (buf.at[g, :, :, 1 - y, :, TOP], r1.at[slot, 0], ydev),
                (buf.at[g, :, :, :, 1 - x, LOW], r1.at[slot, 1], xdev),
            ]
        elif k == 1:
            moves = [
                (buf.at[g, :, 1 - b, y, :, TOP], r2.at[slot, 0], bdev),
                (buf.at[g, :, 1 - b, :, x, LOW], r2.at[slot, 1], bdev),
            ]
        elif k == 2:
            moves = [
                (buf.at[g, :, b, y, 1 - x, TOP], r3.at[slot, 0], xdev),
                (buf.at[g, :, b, 1 - y, x, LOW], r3.at[slot, 1], ydev),
            ]
        else:
            moves = [(buf.at[g, 1 - a, b, y, x], r4.at[slot], adev)]
        return [
            remote(src, dst, hs.at[slot, k], hr.at[slot, k], device) for src, dst, device in moves
        ]

    def collect_wait(k, r):
        slot = lax.rem(r, RING)
        ref = (r1, r2, r3, r4)[k].at[slot]
        remote(ref, ref, hs.at[slot, k], hr.at[slot, k], adev).wait()

    def add_parts(k, r):
        g, slot = grad_place(r), lax.rem(r, RING)
        if k == 0:
            top, low, parts = (g, slice(None), slice(None), y, slice(None), TOP), (
                (g, slice(None), slice(None), slice(None), x, LOW)
            ), r1
        elif k == 1:
            top, low, parts = (g, slice(None), b, y, slice(None), TOP), (
                (g, slice(None), b, slice(None), x, LOW)
            ), r2
        else:
            top, low, parts = (g, slice(None), b, y, x, TOP), (g, slice(None), b, y, x, LOW), r3
        buf[top] = buf[top] + parts[slot, 0]
        buf[low] = buf[low] + parts[slot, 1]

    def add_last(r):
        g, slot = grad_place(r), lax.rem(r, RING)
        total = buf[g, a, b, y, x].astype(F32) + r4[slot].astype(F32)

        def put(ref, base):
            def store():
                ref[:, pl.ds(pl.multiple_of((r - base) * UNIT, UNIT), UNIT)] = total

            return store

        when(r < 8, put(g2, 0))
        when((r >= 8) & (r < 16), put(g1, 8))
        when((r >= 16) & (r < 18), put(go, 16))
        when(r >= 18, put(gq_units, 18))

    def scatter_tick(s):
        if not linked:
            return
        s = jnp.int32(s)
        for k in (3, 2, 1, 0):
            unit = s - (k + 1) * LAG

            def further(k=k, unit=unit):
                collect_wait(k, unit)
                if k < 3:
                    add_parts(k, unit)
                    start(collect(k + 1, unit))
                else:
                    add_last(unit)

            when((unit >= 0) & (unit < 24), further)
        when((s >= 0) & (s < 24), lambda: start(collect(0, s)))

    def scatter_ticks(low, high):
        if not linked or low >= high:
            return

        def one(s, carry):
            scatter_tick(s)
            return carry

        lax.fori_loop(low, high, one, 0)

    def put_grad(r, value):
        buf[grad_place(r)] = value.astype(BF16).reshape(BLOCKS + (D // 16, UNIT))
        if not linked:

            def put(ref, base):
                def store():
                    cols = pl.ds(pl.multiple_of((r - base) * UNIT, UNIT), UNIT)
                    copy = pltpu.make_async_copy(
                        buf.at[grad_place(r)], ref.at[:, :, :, :, :, cols], local_sem.at[0]
                    )
                    copy.start()
                    copy.wait()

                return store

            when(r < 8, put(g2, 0))
            when((r >= 8) & (r < 16), put(g1, 8))
            when((r >= 16) & (r < 18), put(go, 16))
            when(r >= 18, put(gq, 18))

    def weight(place_idx):
        return buf[place_idx].reshape(D, UNIT)

    def pair(ref, n):
        return jnp.concatenate([ref[2 * n], ref[2 * n + 1]], axis=1)

    def put_pair(ref, n, value):
        ref[2 * n] = value[:, :SLAB]
        ref[2 * n + 1] = value[:, SLAB:]

    def token_exchange(which, ref, i):
        return remote(
            ref.at[pl.ds(i * 2 * R, R)],
            ref.at[pl.ds((i * 2 + 1) * R, R)],
            ts.at[which, i],
            tr.at[which, i],
            core,
        )

    def partial_exchange(which, side, j):
        return remote(snd.at[j], rcv.at[side, j], xs.at[which, j], xr.at[which, j], core)

    def project(which, side, slabs, places, tick=None):
        def one(j, carry):
            left = jnp.concatenate([ref[n] for ref, n in slabs], axis=1)
            jh, jl = lax.div(j, 2), lax.rem(j, 2)
            right = jnp.concatenate(
                [buf[u, jh, jl].reshape(UNIT, UNIT) for u in places], axis=1
            )
            total = mm(left, right, 1, 1)
            for i in range(images):
                own[j, pl.ds(i * R, R)] = total[i * 2 * R : (i * 2 + 1) * R]
                snd[j, pl.ds(i * R, R)] = total[(i * 2 + 1) * R : (i * 2 + 2) * R].astype(BF16)
            partial_exchange(which, side, j).start()
            if tick is not None:
                tick(j)
            return carry

        lax.fori_loop(0, D // UNIT, one, 0)

    def partial_wait(which, side):
        for j in range(D // UNIT):
            partial_exchange(which, side, j).wait()

    def summed(side, rows):
        return jnp.concatenate(
            [own[j, rows] + rcv[side, j, rows].astype(F32) for j in range(D // UNIT)], axis=1
        )

    def token_loop(i, body):
        def step(c, carry):
            r = pl.multiple_of(i * R + c * CHUNK, CHUNK)
            full = pl.multiple_of(i * 2 * R + c * CHUNK, CHUNK)
            body(pl.ds(r, CHUNK), pl.ds(full, CHUNK), c, False)
            return carry

        lax.fori_loop(0, chunks - 1, step, 0, unroll=chunks - 1)
        c = chunks - 1
        body(pl.ds(i * R + c * CHUNK, CHUNK), pl.ds(i * 2 * R + c * CHUNK, CHUNK), c, True)

    def compact(i):
        return i * R

    if linked:
        small[...] = jnp.zeros_like(small)
        for n in range(6):
            small[n : n + 1, : D // 16] = small_in[n][...].astype(F32)
        small[8:16, :8] = small_in[6][...].astype(F32)
        small[32:40, :16] = small_in[7][...].astype(F32)
        small[16:32, :8] = jnp.transpose(small[32:40])[:16, :8]
        vb[0] = jnp.zeros((VEC_ROWS, UNIT), BF16)
        twice = small[:8] + swap(small[:8])
        wide_lane = lax.broadcasted_iota(jnp.int32, (8, D), 1)
        wide = jnp.concatenate([twice] * (D // SLAB), axis=1)
        wide = jnp.where(lax.div(wide_lane, HD) == d_idx, wide, 0.0)
        for k in range(4):
            vb[0, 8 * k : 8 * k + 8] = wide[:, k * UNIT : (k + 1) * UNIT].astype(BF16)
        heads_bias = pltpu.roll(small[8:16], d_idx * 8, 1)
        heads_swap = swap(heads_bias)
        row_low = half_lane[:1]
        for c in range(2):
            q_parts, v_parts = [], []
            for p in range(2):
                n = 4 * c + 2 * p
                q_parts.append(
                    jnp.where(row_low, heads_bias[n : n + 1], heads_swap[n + 1 : n + 2])
                )
                v_parts.append(
                    jnp.where(row_low, heads_swap[n : n + 1], heads_bias[n + 1 : n + 2])
                )
            base = QKV_ROW + 3 * c
            vb[0, base : base + 1] = jnp.concatenate(q_parts, axis=1).astype(BF16)
            vb[0, base + 2 : base + 3] = jnp.concatenate(v_parts, axis=1).astype(BF16)
        hidden_bias = pltpu.roll(small[16:32], d_idx * 8, 1)
        for u in range(8):
            vb[0, FC1_ROW + u : FC1_ROW + u + 1] = jnp.concatenate(
                [hidden_bias[2 * u : 2 * u + 1], hidden_bias[2 * u + 1 : 2 * u + 2]], axis=1
            ).astype(BF16)
        for k, devices in enumerate((column, plane)):
            copies = [
                remote(vb.at[k], vbr.at[k, n], vgs.at[k, n], vgr.at[k, n], device)
                for n, device in enumerate(devices)
            ]
            start(copies)
            if k == 0:
                gather_ticks(0, 3)
                tok_copy.wait()
            else:
                wait(weight_copies)
                gather_ticks(3, 5)
            cuts = (0, chunks // 2, chunks)
            take_tokens(tok_in, tok, compact, cuts[k], cuts[k + 1])
            wait(copies)
            vb[k + 1] = vb[k] + vbr[k, 0] + vbr[k, 1] + vbr[k, 2]
        gather_ticks(5, 8)
        vec[...] = vb[2].astype(F32)
    else:
        wait(weight_copies)
        tok_copy.wait()
        take_tokens(tok_in, tok, compact, 0, chunks)
        vec[...] = small_in[0][...].astype(F32)

    def vector(n):
        return jnp.concatenate([vec[8 * k + n : 8 * k + n + 1] for k in range(4)], axis=1)

    gain1, shift1, out_bias, gain2, shift2, fc2_bias = [vector(n) for n in range(6)]
    gvec[...] = jnp.zeros_like(gvec)
    acc[...] = jnp.zeros_like(acc)
    lse[...] = jnp.zeros_like(lse)

    for i in range(images):

        def norm_one(rows, full, c, last):
            normed, _ = stats(tok[rows].astype(F32))
            h1[full] = (normed * gain1 + shift1).astype(BF16)

        token_loop(i, norm_one)
        token_exchange(0, h1, i).start()
        gather_tick(8 + i)
    gather_ticks(8 + images, 3 + 4 * LAG)
    for i in range(images):
        token_exchange(0, h1, i).wait()

    lane = lax.broadcasted_iota(jnp.int32, (2 * R, SLAB), 1)
    row = lax.broadcasted_iota(jnp.int32, (2 * R, SLAB), 0)
    second_half = row >= R
    inside = jnp.where(second_half, row - R, row)
    position = inside + jnp.where(second_half, (1 - t_idx) * half, t_idx * half)
    low_lanes = lane[:R] < HD

    def head_lanes(e, lanes):
        return lanes < HD if e == 0 else lanes >= HD

    def extra(e):
        return HD * (1 - e)

    def key_bias(i):
        valid = (inside < half) & (position < lengths[i])
        return jnp.where(valid, 0.0, -1e30)

    def project_heads(c):
        def one(j, carry):
            u = 3 * c + j
            value = mm(h1[...], weight(16 + u), 1, 0) + vec[pl.ds(QKV_ROW + u, 1)]
            put_pair(qkv, u, value.astype(BF16))
            return carry

        lax.fori_loop(0, 3, one, 0)

    def attend(i, c, p):
        rows = pl.ds(pl.multiple_of(i * 2 * R, 16), 2 * R)
        q = qkv[c * 6 + p, rows].astype(F32) * HD**-0.5
        k = qkv[c * 6 + 2 + p, rows].astype(F32)
        v = qkv[c * 6 + 4 + p, rows]
        bias = key_bias(i)
        heads = []
        for e in range(2):
            inhead = head_lanes(e, lane)
            first_extra = lane == extra(e)
            qm = jnp.where(inhead, q, jnp.where(first_extra, 1.0, 0.0)).astype(BF16)
            km = jnp.where(inhead, k, jnp.where(first_extra, bias, 0.0)).astype(BF16)
            heads.append((qm, km))
        for m in range(2):
            outs, sums = [], []
            for e in range(2):
                qm, km = heads[e]
                scores = mm(qm[m * R : (m + 1) * R], km, 1, 1)
                peak = jnp.max(scores, -1, keepdims=True)
                exps = jnp.exp(scores - peak)
                total = jnp.sum(exps, -1, keepdims=True)
                outs.append(mm(exps.astype(BF16), v, 1, 0) * (1.0 / total))
                sums.append(peak + jnp.log(total))
            tile = pl.ds(pl.multiple_of(i * 2 * R + m * R, 16), R)
            ctx[2 * c + p, tile] = jnp.where(low_lanes, outs[0], outs[1]).astype(BF16)
            column = lane[:R]
            head = (2 * c + p) * 2
            lse[tile] = jnp.where(
                column == head, sums[0], jnp.where(column == head + 1, sums[1], lse[tile])
            )

    for c in range(2):
        project_heads(c)

        def attend_step(n, carry):
            if linked:
                pl.when(n < 3)(lambda: gather_tick(3 + 4 * LAG + 3 * c + n))
            attend(lax.div(n, 2), c, lax.rem(n, 2))
            return carry

        lax.fori_loop(0, images * 2, attend_step, 0)

    project(0, 0, [(ctx, n) for n in range(4)], [22, 23])
    gather_ticks(9 + 4 * LAG, 11 + 4 * LAG)
    partial_wait(0, 0)
    for i in range(images):

        def norm_two(rows, full, c, last):
            middle = tok[rows].astype(F32) + summed(0, rows) + out_bias
            mid[rows] = middle
            normed, _ = stats(middle)
            h2[full] = (normed * gain2 + shift2).astype(BF16)

        token_loop(i, norm_two)
        token_exchange(2, h2, i).start()
        if i == 0:
            gather_tick(11 + 4 * LAG)
    gather_tick(12 + 4 * LAG)
    cot_copy.wait()
    take_tokens(cot_in, cot, lambda i: i * 2 * R, 0, chunks)
    for i in range(images):
        token_exchange(1, cot, i).start()
    for i in range(images):
        token_exchange(2, h2, i).wait()

    def hidden(u, carry):
        if linked:
            pl.when(lax.rem(u, 2) == 0)(lambda: gather_tick(13 + 4 * LAG + lax.div(u, 2)))
        pre = mm(h2[...], weight(8 + u), 1, 0) + vec[pl.ds(FC1_ROW + u, 1)]
        sig = 0.5 * jnp.tanh(0.851 * pre) + 0.5
        active = pre * sig
        slope = sig + 1.702 * active * (1.0 - sig)
        put_pair(act, u, active.astype(BF16))
        put_pair(gp, u, slope.astype(BF16))
        return carry

    lax.fori_loop(0, 8, hidden, 0)
    for i in range(images):
        token_exchange(1, cot, i).wait()

    def hidden_back(u, carry):
        put_grad(u, mm(cot[...], pair(act, u), 0, 0))
        gather_tick(17 + 4 * LAG + u)
        pre_grad = mm(cot[...], weight(u), 1, 0) * pair(gp, u).astype(F32)
        gvec[pl.ds(28 + u, 1)] = jnp.sum(pre_grad, 0, keepdims=True)
        put_pair(gp, u, pre_grad.astype(BF16))
        if linked:
            pl.when(u >= 3)(lambda: scatter_tick(u - 3))
        return carry

    lax.fori_loop(0, 8, hidden_back, 0)

    def odd_tick(base):
        if not linked:
            return None

        def tick(j):
            pl.when(lax.rem(j, 2) == 1)(lambda: scatter_tick(base + lax.div(j, 2)))

        return tick

    project(1, 1, [(act, n) for n in range(16)], list(range(8)), odd_tick(5))

    def first_grad(u, carry):
        put_grad(8 + u, mm(h2[...], pair(gp, u), 0, 0))
        return carry

    lax.fori_loop(0, 4, first_grad, 0)
    scatter_tick(7)
    partial_wait(1, 1)
    for i in range(images):

        def finish(rows, full, c, last):
            total = mid[rows] + summed(1, rows) + fc2_bias
            put_tokens(result, c, i, total.astype(BF16), last)

        token_loop(i, finish)
    scatter_tick(8)
    project(2, 0, [(gp, n) for n in range(16)], list(range(8, 16)), odd_tick(9))
    lax.fori_loop(4, 6, first_grad, 0)
    partial_wait(2, 0)

    def add_rows(n, value):
        acc[n] += value[:8] + value[8:]

    for i in range(images):

        def norm_two_back(rows, full, c, last):
            grad = summed(0, rows)
            normed, inverse = stats(mid[rows])
            cots = cot[full].astype(F32)
            middle_grad = cots + stats_back(grad * gain2, normed, inverse)
            add_rows(2, middle_grad)
            add_rows(3, grad * normed)
            add_rows(4, grad)
            add_rows(5, cots)
            mid[rows] = middle_grad
            cot[full] = middle_grad.astype(BF16)

        token_loop(i, norm_two_back)
        token_exchange(3, cot, i).start()
        if i == 0:
            scatter_tick(11)
    scatter_tick(12)
    lax.fori_loop(6, 8, first_grad, 0)
    for i in range(images):
        token_exchange(3, cot, i).wait()

    def out_back(u, carry):
        put_grad(16 + u, mm(cot[...], pair(ctx, u), 0, 0))
        return carry

    lax.fori_loop(0, 2, out_back, 0)
    scatter_tick(13)

    def context_back(u, carry):
        value = mm(cot[...], weight(22 + u), 1, 0)
        put_pair(act, 6 + u, value.astype(BF16))
        return carry

    lax.fori_loop(0, 2, context_back, 0)

    def attend_back(i, c, p):
        rows = pl.ds(pl.multiple_of(i * 2 * R, 16), 2 * R)
        q = qkv[c * 6 + p, rows].astype(F32) * HD**-0.5
        k = qkv[c * 6 + 2 + p, rows]
        v = qkv[c * 6 + 4 + p, rows]
        up = act[12 + 2 * c + p, rows]
        inner_all = up.astype(F32) * ctx[2 * c + p, rows].astype(F32)
        sums_all = lse[rows]
        bias = key_bias(i)
        q_low = q.astype(BF16)
        q_grads, k_grads, v_grads = [], [], []
        for e in range(2):
            inhead = head_lanes(e, lane)
            at = [lane == extra(e) + n for n in range(4)]
            head = (2 * c + p) * 2 + e
            total = jnp.sum(jnp.where(lane == head, sums_all, 0.0), -1, keepdims=True)
            inner = jnp.sum(jnp.where(inhead, inner_all, 0.0), -1, keepdims=True)
            s1, s2, s3 = three_terms(-total)
            n1, n2, n3 = three_terms(-inner)
            ones = at[1] | at[2] | at[3]
            qa = jnp.where(
                inhead,
                q,
                jnp.where(
                    at[0],
                    1.0,
                    jnp.where(at[1], s1, jnp.where(at[2], s2, jnp.where(at[3], s3, 0.0))),
                ),
            ).astype(BF16)
            ka = jnp.where(
                inhead, k.astype(F32), jnp.where(at[0], bias, jnp.where(ones, 1.0, 0.0))
            ).astype(BF16)
            ua = jnp.where(
                inhead,
                up.astype(F32),
                jnp.where(at[1], n1, jnp.where(at[2], n2, jnp.where(at[3], n3, 0.0))),
            ).astype(BF16)
            va = jnp.where(inhead, v.astype(F32), jnp.where(ones, 1.0, 0.0)).astype(BF16)
            q_grad = None
            k_parts, v_parts = [], []
            for m in range(2):
                tile = slice(m * R, (m + 1) * R)
                probs = jnp.exp(mm(ka[tile], qa, 1, 1))
                grads = (probs * mm(va[tile], ua, 1, 1)).astype(BF16)
                v_parts.append(mm(probs.astype(BF16), up, 1, 0))
                k_parts.append(mm(grads, q_low, 1, 0))
                part = mm(grads, k[tile], 0, 0)
                q_grad = part if q_grad is None else q_grad + part
            q_grads.append(q_grad * HD**-0.5)
            k_grads.append(k_parts)
            v_grads.append(v_parts)
        low = lane < HD
        q_sum = jnp.where(low, q_grads[0], q_grads[1])
        act[c * 6 + p, rows] = q_sum.astype(BF16)
        v_bias = None
        for m in range(2):
            tile = pl.ds(pl.multiple_of(i * 2 * R + m * R, 16), R)
            k_sum = jnp.where(low_lanes, k_grads[0][m], k_grads[1][m])
            v_sum = jnp.where(low_lanes, v_grads[0][m], v_grads[1][m])
            act[c * 6 + 2 + p, tile] = k_sum.astype(BF16)
            act[c * 6 + 4 + p, tile] = v_sum.astype(BF16)
            part = jnp.sum(v_sum, 0, keepdims=True)
            v_bias = part if v_bias is None else v_bias + part
        bias_row = jnp.concatenate([jnp.sum(q_sum, 0, keepdims=True), v_bias], axis=1)
        gvec[pl.ds(24 + 2 * c + p, 1)] += bias_row

    for c in range(2):

        def attend_back_step(n, carry):
            if linked and c == 0:
                scatter_tick(14 + n)
            if linked and c == 1:
                pl.when(n < 3)(lambda: scatter_tick(18 + n))
            attend_back(lax.div(n, 2), c, lax.rem(n, 2))
            return carry

        lax.fori_loop(0, images * 2, attend_back_step, 0)

        def heads_grad(j, carry):
            u = 3 * c + j
            put_grad(18 + u, mm(h1[...], pair(act, u), 0, 0))
            return carry

        lax.fori_loop(0, 3, heads_grad, 0)
    scatter_tick(21)
    project(3, 1, [(act, n) for n in range(12)], list(range(16, 22)), odd_tick(22))
    partial_wait(3, 1)
    for i in range(images):

        def norm_one_back(rows, full, c, last):
            grad = summed(1, rows)
            normed, inverse = stats(tok[rows].astype(F32))
            add_rows(0, grad * normed)
            add_rows(1, grad)
            total = mid[rows] + stats_back(grad * gain1, normed, inverse)
            put_tokens(tok_grad, c, i, total.astype(BF16), last)

        token_loop(i, norm_one_back)
        if i == 0:
            scatter_tick(24)

    for n in range(6):
        total = jnp.sum(acc[n], 0, keepdims=True)
        for k in range(4):
            gvec[4 * n + k : 4 * n + k + 1] = total[:, k * UNIT : (k + 1) * UNIT]

    def sum_copy(k, stage, device):
        return remote(vs.at[stage], vr.at[k], vss.at[k], vsr.at[k], device)

    vs[0] = gvec[...]
    over_core = sum_copy(0, 0, core)
    over_core.start()
    scatter_tick(25)
    over_core.wait()
    shared = lax.broadcasted_iota(jnp.int32, (GVEC_ROWS, UNIT), 0) < 24
    gathered = vs[0] + jnp.where(shared, vr[0], 0.0)
    if linked:
        vs[1] = gathered
        for k, devices in enumerate((column, plane)):
            copies = [sum_copy(3 * k + n + 1, k + 1, device) for n, device in enumerate(devices)]
            start(copies)
            scatter_ticks(26 + 2 * k, 28 + 2 * k)
            wait(copies)
            parts = [vr[3 * k + n] for n in (1, 2, 3)]
            vs[k + 2] = vs[k + 1] + parts[0] + parts[1] + parts[2]
        scatter_ticks(30, STEPS)
        gvec[...] = vs[3]
        for n in range(4):
            kinds = [
                gq_units[
                    :,
                    (3 * (n // 2) + k) * UNIT + (n % 2) * SLAB : (3 * (n // 2) + k) * UNIT
                    + (n % 2 + 1) * SLAB,
                ]
                for k in range(3)
            ]
            keys = swap(kinds[1])
            tiles = (
                jnp.where(half_lane, kinds[0], keys),
                jnp.where(half_lane, kinds[2], kinds[0]),
                jnp.where(half_lane, keys, kinds[2]),
            )
            for k, tile in enumerate(tiles):
                gq[:, (3 * n + k) * SLAB : (3 * n + k + 1) * SLAB] = tile
    else:
        gvec[...] = gathered


def output_kernel(result, tok_grad, gq, go, g1, g2, gvec, *refs):
    outs, held, sems = refs[:14], refs[14:20], refs[20]
    sources = (result, tok_grad, gq, go, g1, g2)
    arrive = [
        pltpu.make_async_copy(source, target, sems.at[0, n])
        for n, (source, target) in enumerate(zip(sources, held))
    ]
    leave = [
        pltpu.make_async_copy(source, target, sems.at[1, n])
        for n, (source, target) in enumerate(zip(held, outs[:6]))
    ]
    for copy in arrive:
        copy.start()
    d_idx = lax.axis_index("dp")
    values = gvec[...]
    low = lax.broadcasted_iota(jnp.int32, (8, SLAB), 1) < HD
    rows = [
        jnp.concatenate([values[4 * n + k : 4 * n + k + 1] for k in range(4)], axis=1)
        for n in range(6)
    ]
    wide = jnp.concatenate(rows + [jnp.zeros_like(rows[0])] * 2, axis=0)
    mine = jnp.zeros((8, SLAB), F32)
    for n in range(wide.shape[1] // SLAB):
        tile = wide[:, n * SLAB : (n + 1) * SLAB]
        mine = jnp.where(lax.div(d_idx, 2) == n, tile, mine)
    mine = jnp.where(lax.rem(d_idx, 2) == 1, pltpu.roll(mine, HD, 1), mine)
    for n in range(6):
        outs[6 + n][...] = mine[n : n + 1, : outs[6 + n].shape[1]]
    head_rows = []
    for n in range(4):
        row = values[24 + n : 25 + n]
        q, v = row[:, :SLAB], row[:, SLAB:]
        head_rows.append(jnp.where(low[:1], q, pltpu.roll(v, HD, 1)))
        head_rows.append(jnp.where(low[:1], pltpu.roll(q, HD, 1), v))
    back = SLAB - d_idx * 8
    mine = pltpu.roll(jnp.concatenate(head_rows, axis=0), back, 1)
    outs[12][...] = mine[:, : outs[12].shape[1]]
    hidden_rows = []
    for n in range(8):
        row = values[28 + n : 29 + n]
        hidden_rows += [row[:, :SLAB], row[:, SLAB:]]
    mine = pltpu.roll(jnp.concatenate(hidden_rows, axis=0), back, 1)
    outs[13][...] = jnp.transpose(mine)[: outs[13].shape[0]]
    for n in range(6):
        arrive[n].wait()
        leave[n].start()
    for copy in leave:
        copy.wait()


def own_part(values, index, width):
    return lax.dynamic_slice_in_dim(values, index * width, width, axis=1)


def body(
    linked,
    tokens,
    lengths,
    ln1_gain,
    ln1_bias,
    qkv_weight,
    qv_bias,
    out_weight,
    out_bias,
    ln2_gain,
    ln2_bias,
    fc1_weight,
    fc1_bias,
    fc2_weight,
    fc2_bias,
    cotangent,
):
    images, half, D = tokens.shape
    parts = lax.axis_size("dp")
    dp = lax.axis_index("dp")
    heads = qv_bias.shape[0]
    R = -(-half // 16) * 16
    T = images * 2 * R
    share = D // parts
    tok = jnp.swapaxes(tokens, 0, 1)
    cot = jnp.swapaxes(cotangent, 0, 1)
    norms = (ln1_gain, ln1_bias, out_bias, ln2_gain, ln2_bias, fc2_bias)
    if linked:
        vec = (*[v.reshape(1, share) for v in norms], qv_bias, jnp.transpose(fc1_bias))
        wq = qkv_weight
    else:
        norms = lax.all_gather(jnp.stack(norms), "dp", axis=1, tiled=True).reshape(6, 4, UNIT)
        norms = jnp.pad(jnp.swapaxes(norms, 0, 1), ((0, 0), (0, 2), (0, 0))).reshape(32, UNIT)
        qv = lax.all_gather(qv_bias, "dp", axis=1, tiled=True).reshape(2, 2, 2, 2, HD)
        q_rows = qv[:, :, :, 0].reshape(2, 1, UNIT)
        v_rows = qv[:, :, :, 1].reshape(2, 1, UNIT)
        qkv_rows = jnp.concatenate([q_rows, jnp.zeros_like(q_rows), v_rows], axis=1)
        fc1_rows = lax.all_gather(fc1_bias, "dp", axis=1, tiled=True).reshape(8, UNIT)
        unused = jnp.zeros((VEC_ROWS - 46, UNIT), BF16)
        vec = (jnp.concatenate([norms, qkv_rows.reshape(6, UNIT), fc1_rows, unused]),)
        grouped = qkv_weight.reshape(share, heads // 4, 4, 3, HD)
        wq = jnp.swapaxes(grouped, 2, 3).reshape(share, heads * 3 * HD)
    weights = [wq, out_weight, fc1_weight, fc2_weight]
    if not linked:
        weights = [
            lax.all_gather(w, "dp", axis=0, tiled=True).reshape(
                BLOCKS + (D // 16, w.shape[1])
            )
            for w in weights
        ]
    vmem = pl.BlockSpec(memory_space=pltpu.VMEM)
    hbm = pl.BlockSpec(memory_space=pl.ANY)
    if linked:
        grads = [jax.ShapeDtypeStruct(w.shape, F32) for w in weights]
    else:
        grads = [jax.ShapeDtypeStruct(w.shape, BF16) for w in weights]
    grad_spec = vmem if linked else hbm
    dma = pltpu.SemaphoreType.DMA
    block = BLOCKS + (D // 16, UNIT)
    outs = pl.pallas_call(
        functools.partial(layer_kernel, images, half, R, linked),
        out_shape=[
            jax.ShapeDtypeStruct((half, images, D), BF16),
            jax.ShapeDtypeStruct((half, images, D), BF16),
            *grads,
            jax.ShapeDtypeStruct((GVEC_ROWS, UNIT), F32),
        ],
        in_specs=[
            pl.BlockSpec(memory_space=pltpu.SMEM),
            hbm,
            hbm,
            tuple(vmem for _ in vec),
            vmem if linked else hbm,
            hbm,
            hbm,
            hbm,
        ],
        out_specs=[vmem, vmem, grad_spec, grad_spec, grad_spec, grad_spec, vmem],
        scratch_shapes=[
            pltpu.VMEM((32,) + block, BF16),
            pltpu.VMEM((images * R, D), BF16),
            pltpu.VMEM((D // 16, 6 * UNIT), F32),
            pltpu.VMEM((40, SLAB), F32),
            pltpu.VMEM((T, D), BF16),
            pltpu.VMEM((12, T, SLAB), BF16),
            pltpu.VMEM((4, T, SLAB), BF16),
            pltpu.VMEM((T, D), BF16),
            pltpu.VMEM((16, T, SLAB), BF16),
            pltpu.VMEM((16, T, SLAB), BF16),
            pltpu.VMEM((T, D), BF16),
            pltpu.VMEM((images * R, D), F32),
            pltpu.VMEM((4, images * R, UNIT), F32),
            pltpu.VMEM((4, images * R, UNIT), BF16),
            pltpu.VMEM((2, 4, images * R, UNIT), BF16),
            pltpu.VMEM((T, SLAB), F32),
            pltpu.VMEM((VEC_ROWS, UNIT), F32),
            pltpu.VMEM((6, 8, D), F32),
            pltpu.VMEM((RING, 2, 2, 2, 2, 32, UNIT), BF16),
            pltpu.VMEM((RING, 2, 2, 2, 32, UNIT), BF16),
            pltpu.VMEM((RING, 2, 2, 32, UNIT), BF16),
            pltpu.VMEM((RING, 64, UNIT), BF16),
            pltpu.VMEM((3, VEC_ROWS, UNIT), BF16),
            pltpu.VMEM((2, 3, VEC_ROWS, UNIT), BF16),
            pltpu.VMEM((4, GVEC_ROWS, UNIT), F32),
            pltpu.VMEM((7, GVEC_ROWS, UNIT), F32),
            dma((24,)),
            dma((2,)),
            dma((RING, 4)),
            dma((RING, 4)),
            dma((RING, 4)),
            dma((RING, 4)),
            dma((4, 4)),
            dma((4, 4)),
            dma((4, images)),
            dma((4, images)),
            dma((2, 3)),
            dma((2, 3)),
            dma((7,)),
            dma((7,)),
        ],
        compiler_params=pltpu.CompilerParams(
            collective_id=0, has_side_effects=True, vmem_limit_bytes=64 * 2**20 - 2**16
        ),
        name="layer",
    )(lengths, tok, cot, vec, *weights)
    result, tok_grad, gq, go, g1, g2, gvec = outs
    if linked:
        large = (result, tok_grad, gq, go, g1, g2)
        result, tok_grad, gq, go, g1, g2, *norms_grad, qv_grad, fc1_grad = pl.pallas_call(
            output_kernel,
            out_shape=[
                *[jax.ShapeDtypeStruct(v.shape, v.dtype) for v in large],
                *[jax.ShapeDtypeStruct((1, share), F32)] * 6,
                jax.ShapeDtypeStruct((heads, 2 * HD // parts), F32),
                jax.ShapeDtypeStruct((128 // parts, fc1_bias.shape[0]), F32),
            ],
            in_specs=[hbm] * 6 + [vmem],
            out_specs=[hbm] * 6 + [vmem] * 8,
            scratch_shapes=[*[pltpu.VMEM(v.shape, v.dtype) for v in large], dma((2, 6))],
            name="outputs",
        )(*large, gvec)
        norms_grad = [v.reshape(share) for v in norms_grad]
        fc1_grad = jnp.transpose(fc1_grad)
    else:

        def owned(values):
            flat = values.reshape(D, values.shape[-1]).astype(F32)
            return lax.psum_scatter(flat, "dp", scatter_dimension=0, tiled=True)

        gq, go, g1, g2 = owned(gq), owned(go), owned(g1), owned(g2)
        gq = jnp.swapaxes(gq.reshape(share, heads // 4, 3, 4, HD), 2, 3)
        gq = gq.reshape(share, heads * 3 * HD)
        gvec = lax.psum(gvec, "dp")
        norms_grad = own_part(gvec[:24].reshape(6, D), dp, share)
        qv_grad = jnp.swapaxes(gvec[24:28].reshape(4, 2, 2, HD), 1, 2).reshape(heads, 2 * HD)
        qv_grad = own_part(qv_grad, dp, 2 * HD // parts)
        fc1_grad = own_part(gvec[28:36].reshape(-1, 128), dp, 128 // parts)
    return (
        jnp.swapaxes(result, 0, 1),
        jnp.swapaxes(tok_grad, 0, 1),
        norms_grad[0],
        norms_grad[1],
        gq,
        qv_grad,
        go,
        norms_grad[2],
        norms_grad[3],
        norms_grad[4],
        g1,
        fc1_grad,
        g2,
        norms_grad[5],
    )


def solution(mesh):
    linked = mesh.shape["dp"] == 16
    vector = P("dp")
    weight = P("dp", "tensor")
    bias = P("tensor", "dp")
    tokens = P("dp", "tensor", None)
    in_specs = (
        tokens,
        vector,
        vector,
        vector,
        weight,
        bias,
        weight,
        vector,
        vector,
        vector,
        weight,
        bias,
        weight,
        vector,
        tokens,
    )
    out_specs = (
        tokens,
        tokens,
        vector,
        vector,
        weight,
        bias,
        weight,
        vector,
        vector,
        vector,
        weight,
        bias,
        weight,
        vector,
    )
    return jax.shard_map(
        functools.partial(body, linked),
        mesh=mesh,
        in_specs=in_specs,
        out_specs=out_specs,
        check_vma=False,
    )
```
